32 devices in a mesh: rep: 16 (over z, x, core), grp: 2 (over y).
Axes of the slice: x: 2, y: 2, z: 4, core: 2. Of those that a mesh axis runs over, the one named last changes fastest.
Arguments:
- tokens: bfloat16 [16384, 1536], P(('rep', 'grp')), may hold values from -6 to 6
- cotangent: bfloat16 [16384, 1536], P(('rep', 'grp')), may hold values from -6 to 6
- routes: int32 [16384, 8], P(('rep', 'grp')), may hold values from 0 to 39, all different within a row; in each aligned block of 512 rows (0 to 511, 512 to 1023, ...) at most 143 rows name the same one
- padding: int32 [16384], P(('rep', 'grp')), may hold values 0 or 1
- parents: int32 [16, 8], P('rep'), may hold values from 0 to 6, as said below
- adapter_ids: int32 [16], P('rep'), may hold values from 0 to 3
- w_query: bfloat16 [1536, 1536], P('grp'), may hold values from -0.15625 to 0.15625
- w_keyval: bfloat16 [1536, 1024], P('grp'), may hold values from -0.15625 to 0.15625
- w_output: bfloat16 [1536, 1536], P('grp'), may hold values from -1 to 1
- w_router: bfloat16 [1536, 40], P('grp'), may hold values from -0.078125 to 0.078125
- gain_attn: bfloat16 [1536], P('grp'), may hold values from 0.5 to 1.5
- gain_ffn: bfloat16 [1536], P('grp'), may hold values from 0.5 to 1.5
- w_gateup: bfloat16 [40, 1536, 1024], P('grp'), may hold values from -0.15625 to 0.15625
- w_down: bfloat16 [40, 512, 1536], P('grp'), may hold values from -1 to 1
- a_qkv: bfloat16 [4, 1536, 48], P(None, 'grp'), may hold values from -0.15625 to 0.15625
- b_query: bfloat16 [4, 16, 1536], P(None, None, 'grp'), may hold values from -0.75 to 0.75
- b_keyval: bfloat16 [4, 2, 16, 512], P(None, None, None, 'grp'), may hold values from -0.75 to 0.75
- a_output: bfloat16 [4, 1536, 16], P(None, 'grp'), may hold values from -0.15625 to 0.15625
- b_output: bfloat16 [4, 16, 1536], P(None, None, 'grp'), may hold values from -6 to 6
- a_router: bfloat16 [4, 1536, 16], P(None, 'grp'), may hold values from -0.15625 to 0.15625
- b_router: bfloat16 [4, 16, 40], P(None, None, 'grp'), may hold values from -0.375 to 0.375
- a_gateup: bfloat16 [4, 40, 1536, 32], P(None, 'grp'), may hold values from -0.15625 to 0.15625
- b_gateup: bfloat16 [4, 40, 2, 16, 512], P(None, 'grp'), may hold values from -0.75 to 0.75
- a_down: bfloat16 [4, 40, 512, 16], P(None, 'grp'), may hold values from -0.25 to 0.25
- b_down: bfloat16 [4, 40, 16, 1536], P(None, 'grp'), may hold values from -1.5 to 1.5
Outputs:
- result: bfloat16 [16384, 1536], P(('rep', 'grp'))
- grad_tokens: bfloat16 [16384, 1536], P(('rep', 'grp'))
- grad_a_qkv: float32 [4, 1536, 48], P(None, 'grp')
- grad_b_query: float32 [4, 16, 1536], P(None, None, 'grp')
- grad_b_keyval: float32 [4, 2, 16, 512], P(None, None, None, 'grp')
- grad_a_output: float32 [4, 1536, 16], P(None, 'grp')
- grad_b_output: float32 [4, 16, 1536], P(None, None, 'grp')
- grad_a_router: float32 [4, 1536, 16], P(None, 'grp')
- grad_b_router: float32 [4, 16, 40], P(None, None, 'grp')
- grad_a_gateup: float32 [4, 40, 1536, 32], P(None, 'grp')
- grad_b_gateup: float32 [4, 40, 2, 16, 512], P(None, 'grp')
- grad_a_down: float32 [4, 40, 512, 16], P(None, 'grp')
- grad_b_down: float32 [4, 40, 16, 1536], P(None, 'grp')
The draws below stay inside these ranges and needn't reach their ends.
Inputs may be any that keep to these rules, and one draw needn't show every extreme that they name: `routes`: each row names 8 different experts. Among the 512 rows of one device no expert is named by more than 143 rows, and in some of these blocks one expert is named by exactly 143. parents[t, s] is s - 1 or s - 2 for s >= 2, and 0 for segments 0 and 1.
All inputs are finite; a program needn't handle non-finite values. No bound on the sum of `padding` on one device may be relied on, other than what follows from the above.
Results may differ from the reference program's by a relative error of at most 0.022.
Values may be sent and summed in bfloat16 or wider, within the bound.
No kernel may reach another device: no remote copies, remote signals or barrier semaphores. Data moves between devices by JAX's collectives and lax.ppermute only.
A program may use at most 512 MiB of HBM per device.

```python
import math
import jax
import jax.numpy as jnp
import numpy as np
from jax import lax

D = 1536
QUERY_HEADS = 24
KEY_VALUE_HEADS = 8
HEAD_SIZE = 64
EXPERTS = 40
FF = 512
TOPK = 8
RANK = 16
ADAPTERS = 4
SEG = 128
TREE_TOKENS = 1024
TOK_DEV = 512
TREES = 16
TOKENS = 16384
SEGS = 8
KVW = 512
CAP = 143
N_GRP = 2


def draw_parents(key, part):
    key = jax.random.fold_in(key, 7)
    jumps = jax.random.randint(key, (TREES, SEGS), 1, 3)
    labels = jnp.arange(SEGS, dtype=jnp.int32)[None, :]
    return jnp.maximum(labels - jumps, 0).astype(jnp.int32)


def set_ends(values, own_key, low, top_value):
    extent = values.shape
    spot = [jax.random.randint(jax.random.fold_in(own_key, axis), (), 0, extent[axis]) for axis in range(len(extent))]
    values = values.at[tuple(spot)].set(low)
    longest = extent.index(max(extent))
    spot[longest] = (spot[longest] + 1) % extent[longest]
    return values.at[tuple(spot)].set(top_value)


def steps_of(key, extent, split, low, largest):
    loudness = 1.0
    for position, shards_of in split:
        steps = jax.random.uniform(jax.random.fold_in(jax.random.fold_in(key, 6), position), (shards_of,), jnp.float32, low / len(split), largest / len(split))
        loudness = loudness * jnp.repeat(jnp.exp(steps), extent[position] // shards_of).reshape((-1,) + (1,) * (len(extent) - 1 - position))
    return loudness


def assign_block(stream_key, own, number, rows, number_of, top, most, skew):
    order = jax.random.permutation(stream_key, number_of)
    packed, usual = portions_of(number_of, rows * top, most, skew, True), portions_of(number_of, rows * top, most, skew, False)
    places = jnp.arange(number_of)

    def named(sizes, rotation):
        used = int((sizes > 0).sum())
        fixed = max(1, used // 4)
        moved = fixed + (places - fixed + rotation * (used - fixed)) % max(1, number_of - fixed)
        return jnp.zeros((number_of,), jnp.int32).at[order[jnp.where(places < fixed, places, moved)]].set(jnp.asarray(sizes, jnp.int32))

    sizes = jnp.where(number % 4 == 0, named(packed, number // 4), named(usual, number - number // 4 - 1))
    mixed = jax.random.permutation(jax.random.fold_in(own, 3), number_of)
    giver, sink = mixed[0:number_of // 2 * 2:2], mixed[1:number_of // 2 * 2:2]
    slack = jnp.minimum(sizes[giver] - 1, most - sizes[sink]) // 2
    slack = jnp.where((giver == order[0]) | (sink == order[0]) | (sizes[sink] == 0), 0, jnp.maximum(slack, 0))
    moved = jax.random.randint(jax.random.fold_in(own, 4), (number_of // 2,), 0, 1 << 20) % (slack + 1)
    sizes = sizes.at[giver].add(-moved).at[sink].add(moved)
    items = jnp.searchsorted(jnp.cumsum(sizes), jnp.arange(rows * top), side="right").astype(jnp.int32)
    listing = items.reshape(top, rows).T
    listing = listing[jax.random.permutation(jax.random.fold_in(own, 1), rows)]
    rotation = jax.random.randint(jax.random.fold_in(own, 2), (rows, 1), 0, top)
    return jnp.take_along_axis(listing, (jnp.arange(top)[None, :] + rotation) % top, axis=1)


def portions_of(amount, total, limit, slope, full):
    weights = [(1 << 20) // math.isqrt(rank ** slope) + 1 for rank in range(1, amount + 1)]
    largest = limit if full else min(limit, max(-(-total // amount), total * weights[0] // sum(weights)))
    least = 1 if total - largest >= amount - 1 else 0
    given, rest = [largest] + [least] * (amount - 1), total - largest - least * (amount - 1)
    while rest > 0:
        candidates = [i for i in range(1, amount) if given[i] < largest] or [i for i in range(1, amount) if given[i] < limit]
        pool, left = sum([weights[i] for i in candidates]), rest
        for i in candidates:
            extra = min(limit - given[i], max(1, left * weights[i] // pool), rest)
            given[i] = given[i] + extra
            rest = rest - extra
    return np.array(given)


def noise(key, shape, spread, reach, pieces=(), kind=jnp.bfloat16):
    factor_of = steps_of(key, shape, pieces, -0.22, 0.18) if pieces else 1.0
    values = jax.random.normal(key, shape, jnp.float32) * spread * factor_of
    return jnp.minimum(jnp.maximum(values, -reach), reach).astype(kind)


def setup_inputs(seed: int = 0) -> dict:
    key_list = jax.random.split(jax.random.key(seed), 26)
    tokens = noise(key_list[0], (TOKENS, D), 1.0, 6.0, ((0, 32),))
    cotangent = noise(key_list[1], (TOKENS, D), 1.0, 6.0, ((0, 32),))
    routes_keys = jax.random.split(jax.random.fold_in(key_list[2], 1), TOKENS // TOK_DEV)
    routes_turns = jax.random.permutation(jax.random.fold_in(key_list[2], 3), TOKENS // TOK_DEV)
    routes = jax.vmap(lambda own, number: assign_block(jax.random.fold_in(key_list[2], 2), own, number, TOK_DEV, EXPERTS, TOPK, CAP, 1))(routes_keys, routes_turns).reshape((TOKENS, TOPK))
    padding = set_ends((jax.random.randint(key_list[3], (TOKENS,), 0, 8) < 7).astype(jnp.int32), jax.random.fold_in(key_list[3], 1), 0, 1)
    parents = draw_parents(jax.random.fold_in(key_list[25], 71), 0)
    adapter_ids = set_ends(jax.random.randint(key_list[5], (TREES,), 0, ADAPTERS), jax.random.fold_in(key_list[5], 1), 0, ADAPTERS - 1).astype(jnp.int32)
    w_query = noise(key_list[6], (D, D), D ** -0.5, 0.15625, ((0, 2),))
    w_keyval = noise(key_list[7], (D, 2 * KVW), D ** -0.5, 0.15625, ((0, 2),))
    w_output = noise(key_list[8], (D, D), (HEAD_SIZE // 2) ** -0.5, 1.0, ((0, 2),))
    w_router = noise(key_list[9], (D, EXPERTS), (4 * D) ** -0.5, 0.078125, ((0, 2),))
    gain_attn = jnp.clip(1.0 + 0.1 * jax.random.normal(key_list[10], (D,), jnp.float32), 0.5, 1.5).astype(jnp.bfloat16)
    gain_ffn = jnp.clip(1.0 + 0.1 * jax.random.normal(key_list[11], (D,), jnp.float32), 0.5, 1.5).astype(jnp.bfloat16)
    w_gateup = noise(key_list[12], (EXPERTS, D, 2 * FF), D ** -0.5, 0.15625, ((0, 2),))
    w_down = noise(key_list[13], (EXPERTS, FF, D), (FF // 16) ** -0.5, 1.0, ((0, 2),))
    a_qkv = noise(key_list[14], (ADAPTERS, D, 3 * RANK), D ** -0.5, 0.15625, ((1, 2),))
    b_query = noise(key_list[15], (ADAPTERS, RANK, D), (4 * RANK) ** -0.5, 0.75, ((2, 2),))
    b_keyval = noise(key_list[16], (ADAPTERS, 2, RANK, KVW), (4 * RANK) ** -0.5, 0.75, ((3, 2),))
    a_output = noise(key_list[17], (ADAPTERS, D, RANK), D ** -0.5, 0.15625, ((1, 2),))
    b_output = noise(key_list[18], (ADAPTERS, RANK, D), 1 ** -0.5, 6.0, ((2, 2),))
    a_router = noise(key_list[19], (ADAPTERS, D, RANK), D ** -0.5, 0.15625, ((1, 2),))
    b_router = noise(key_list[20], (ADAPTERS, RANK, EXPERTS), (16 * RANK) ** -0.5, 0.375, ((2, 2),))
    a_gateup = noise(key_list[21], (ADAPTERS, EXPERTS, D, 2 * RANK), D ** -0.5, 0.15625, ((1, 2),))
    b_gateup = noise(key_list[22], (ADAPTERS, EXPERTS, 2, RANK, FF), (4 * RANK) ** -0.5, 0.75, ((1, 2),))
    a_down = noise(key_list[23], (ADAPTERS, EXPERTS, FF, RANK), FF ** -0.5, 0.25, ((1, 2),))
    b_down = noise(key_list[24], (ADAPTERS, EXPERTS, RANK, D), RANK ** -0.5, 1.5, ((1, 2),))
    return {"tokens": tokens, "cotangent": cotangent, "routes": routes, "padding": padding, "parents": parents, "adapter_ids": adapter_ids, "w_query": w_query, "w_keyval": w_keyval, "w_output": w_output, "w_router": w_router, "gain_attn": gain_attn, "gain_ffn": gain_ffn, "w_gateup": w_gateup, "w_down": w_down, "a_qkv": a_qkv, "b_query": b_query, "b_keyval": b_keyval, "a_output": a_output, "b_output": b_output, "a_router": a_router, "b_router": b_router, "a_gateup": a_gateup, "b_gateup": b_gateup, "a_down": a_down, "b_down": b_down}


@jax.custom_vjp
def low(v):
    return lax.optimization_barrier(v.astype(jnp.bfloat16)).astype(jnp.float32)

@jax.custom_vjp
def low_back(v):
    return v

def low_keep(v):
    return (low(v), None)

def low_pass(kept, grad):
    return (grad,)

def back_keep(v):
    return (v, None)

def back_low(kept, grad):
    return (low(grad),)
low.defvjp(low_keep, low_pass)
low_back.defvjp(back_keep, back_low)

def exact(left, right):
    return jnp.dot(left, right, precision=lax.Precision.HIGHEST, preferred_element_type=jnp.float32)

def rms_norm(value_rows, gain):
    return value_rows * lax.rsqrt(lax.optimization_barrier(jnp.mean(value_rows * value_rows, axis=-1, keepdims=True)) + 1e-05) * gain

def ancestry(parent_row):
    total = parent_row.shape[0]
    labels = jnp.arange(total, dtype=jnp.int32)

    def climb(count, state):
        current, table = state
        current = lax.optimization_barrier(jnp.sum(jnp.where(current[:, None] == labels[None, :], parent_row[None, :], 0), axis=1)).astype(jnp.int32)
        table = jnp.maximum(table, (current[:, None] == labels[None, :]).astype(jnp.int32))
        return (current, table)
    start_index = (labels[:, None] == labels[None, :]).astype(jnp.int32)
    return lax.fori_loop(0, total, climb, (labels, start_index))[1]

def tree_mask(parent_row, pad_row, first, count, tree_length):
    table = ancestry(parent_row)
    segs_here = count // SEG
    segs_all = tree_length // SEG
    rows = lax.dynamic_slice_in_dim(table, (first // SEG).astype(jnp.int32), segs_here, 0)
    linked = jnp.broadcast_to(rows[:, None, :, None] > 0, (segs_here, SEG, segs_all, SEG)).reshape(count, tree_length)
    query_pos = first + jnp.arange(count, dtype=jnp.int32)
    key_pos = jnp.arange(tree_length, dtype=jnp.int32)
    same = query_pos[:, None] // SEG == key_pos[None, :] // SEG
    causal = jnp.logical_or(jnp.logical_not(same), key_pos[None, :] <= query_pos[:, None])
    live = jnp.logical_or(pad_row[None, :] > 0, key_pos[None, :] == query_pos[:, None])
    return jnp.logical_and(jnp.logical_and(linked, causal), live)

def reference(tokens, cotangent, routes, padding, parents, adapter_ids, w_query, w_keyval, w_output, w_router, gain_attn, gain_ffn, w_gateup, w_down, a_qkv, b_query, b_keyval, a_output, b_output, a_router, b_router, a_gateup, b_gateup, a_down, b_down):
    query_w = w_query.astype(jnp.float32)
    keyval_w = w_keyval.astype(jnp.float32)
    output_w = w_output.astype(jnp.float32)
    router_w = w_router.astype(jnp.float32)
    attn_gain = gain_attn.astype(jnp.float32)
    ffn_gain = gain_ffn.astype(jnp.float32)
    gateup_w = w_gateup.astype(jnp.float32)
    down_w = w_down.astype(jnp.float32)
    block_span = math.gcd(512, TREE_TOKENS)
    bound = CAP * N_GRP
    scale = HEAD_SIZE ** (-0.5)
    group_index = QUERY_HEADS // KEY_VALUE_HEADS

    def forward(tokens_f, adapters):
        qkv_a, query_b, keyval_b, output_a, output_b, router_a, router_b, gateup_a, gateup_b, down_a, down_b = adapters

        def tree_layer(items):
            tree_rows, tree_routes, pad_row, parent_row, chosen = items
            normed = low(rms_norm(tree_rows, attn_gain))
            low_rank = low(exact(normed, qkv_a[chosen]))
            query_rows = exact(normed, query_w) + exact(low_rank[:, :RANK], query_b[chosen])
            keyvals = exact(normed, keyval_w)
            key_rows = keyvals[:, :KVW] + exact(low_rank[:, RANK:2 * RANK], keyval_b[chosen, 0])
            value_rows = keyvals[:, KVW:] + exact(low_rank[:, 2 * RANK:], keyval_b[chosen, 1])
            query_rows = low(low_back(query_rows))
            key_rows = low(low_back(key_rows))
            value_rows = low(low_back(value_rows))
            heads_of_key = key_rows.reshape(TREE_TOKENS, KEY_VALUE_HEADS, HEAD_SIZE)
            heads_of_value = value_rows.reshape(TREE_TOKENS, KEY_VALUE_HEADS, HEAD_SIZE)

            def attend_block(start_index):
                mask = tree_mask(parent_row, pad_row, start_index, block_span, TREE_TOKENS)
                heads_of_query = lax.dynamic_slice_in_dim(query_rows, start_index, block_span, 0).reshape(block_span, KEY_VALUE_HEADS, group_index, HEAD_SIZE)
                scores = low_back(jnp.einsum('qgrd,kgd->grqk', heads_of_query, heads_of_key, precision=lax.Precision.HIGHEST) * scale)
                scores = jnp.where(mask[None, None], scores, -1e+30)
                top = lax.optimization_barrier(jnp.max(scores, axis=-1, keepdims=True))
                weights = jnp.exp(scores - top)
                probs = low(weights / lax.optimization_barrier(jnp.sum(weights, axis=-1, keepdims=True)))
                mixed = jnp.einsum('grqk,kgd->qgrd', probs, heads_of_value, precision=lax.Precision.HIGHEST)
                return mixed.reshape(block_span, D)
            starts = jnp.arange(TREE_TOKENS // block_span, dtype=jnp.int32) * block_span
            attended = lax.map(jax.checkpoint(attend_block), starts).reshape(TREE_TOKENS, D)
            attended = low(low_back(attended))
            attn = exact(attended, output_w) + exact(low(exact(attended, output_a[chosen])), output_b[chosen])
            middle = tree_rows + low_back(attn)
            normed_ffn = low(rms_norm(middle, ffn_gain))
            router_rank = low(exact(normed_ffn, router_a[chosen]))
            logits = low_back(exact(normed_ffn, router_w) + exact(router_rank, router_b[chosen]))
            picked = jnp.take_along_axis(logits, tree_routes, axis=1)
            gates = jax.nn.softmax(picked, axis=-1)
            padded_rows = jnp.concatenate([normed_ffn, jnp.zeros((1, D), jnp.float32)], axis=0)

            def run_expert(expert):
                hits = tree_routes == expert
                weight_row = jnp.concatenate([lax.optimization_barrier(jnp.sum(jnp.where(hits, gates, 0.0), axis=1)), jnp.zeros((1,), jnp.float32)])
                slots = jnp.nonzero(jnp.any(hits, axis=1), size=bound, fill_value=TREE_TOKENS)[0].astype(jnp.int32)
                inputs = low_back(padded_rows[slots])
                gate_up = exact(inputs, gateup_w[expert])
                rank_in = low(exact(inputs, gateup_a[chosen, expert]))
                gate_pre = low_back(gate_up[:, :FF] + exact(rank_in[:, :RANK], gateup_b[chosen, expert, 0]))
                up_pre = low_back(gate_up[:, FF:] + exact(rank_in[:, RANK:], gateup_b[chosen, expert, 1]))
                hidden = low(jax.nn.silu(gate_pre) * up_pre)
                rank_down = low(exact(hidden, down_a[chosen, expert]))
                expert_out = low(low_back(exact(hidden, down_w[expert]) + exact(rank_down, down_b[chosen, expert])))
                return (expert_out * weight_row[slots][:, None], slots)
            outputs, slot_ids = lax.map(jax.checkpoint(run_expert), jnp.arange(EXPERTS, dtype=jnp.int32))
            mixture = jnp.zeros((TREE_TOKENS + 1, D), jnp.float32).at[slot_ids.reshape(-1)].add(outputs.reshape(-1, D))
            return middle + mixture[:TREE_TOKENS]
        results = lax.map(jax.checkpoint(tree_layer), (tokens_f.reshape(TREES, TREE_TOKENS, D), routes.reshape(TREES, TREE_TOKENS, TOPK), padding.reshape(TREES, TREE_TOKENS), parents, adapter_ids))
        return results.reshape(TOKENS, D)
    adapters = (a_qkv.astype(jnp.float32), b_query.astype(jnp.float32), b_keyval.astype(jnp.float32), a_output.astype(jnp.float32), b_output.astype(jnp.float32), a_router.astype(jnp.float32), b_router.astype(jnp.float32), a_gateup.astype(jnp.float32), b_gateup.astype(jnp.float32), a_down.astype(jnp.float32), b_down.astype(jnp.float32))
    outcome, pullback = jax.vjp(forward, tokens.astype(jnp.float32), adapters)
    grad_input, grad_adapters = pullback(cotangent.astype(jnp.float32))
    grad_a_qkv, grad_b_query, grad_b_keyval, grad_a_output, grad_b_output, grad_a_router, grad_b_router, grad_a_gateup, grad_b_gateup, grad_a_down, grad_b_down = grad_adapters
    return (outcome.astype(jnp.bfloat16), grad_input.astype(jnp.bfloat16), grad_a_qkv, grad_b_query, grad_b_keyval, grad_a_output, grad_b_output, grad_a_router, grad_b_router, grad_a_gateup, grad_b_gateup, grad_a_down, grad_b_down)
```

```python
import functools

import jax
import jax.numpy as jnp
from jax import lax
from jax.experimental import pallas as pl
from jax.experimental.pallas import tpu as pltpu
from jax.sharding import PartitionSpec as P

QUERY_HEADS = 24
KEY_VALUE_HEADS = 8
HEAD_SIZE = 64
FF = 512
TOPK = 8
RANK = 16
SEG = 128
FLUSH = 5
LANES = 512

EPSILON = 1e-05
BF16 = jnp.bfloat16
F32 = jnp.float32


def product(left, right):
    return jnp.dot(left, right, preferred_element_type=F32)


def product_back(left, right):
    return lax.dot_general(left, right, (((1,), (1,)), ((), ())), preferred_element_type=F32)


def product_outer(left, right):
    return lax.dot_general(left, right, (((0,), (0,)), ((), ())), preferred_element_type=F32)


def rms_norm(value_rows, gain):
    return (
        value_rows
        * lax.rsqrt(jnp.mean(value_rows * value_rows, axis=-1, keepdims=True) + EPSILON)
        * gain
    )


def rms_back(value_rows, gain, upstream):
    factor = lax.rsqrt(jnp.mean(value_rows * value_rows, axis=-1, keepdims=True) + EPSILON)
    scaled = value_rows * factor
    incoming = upstream * gain
    return factor * (incoming - scaled * jnp.mean(incoming * scaled, axis=-1, keepdims=True))


def ancestry(parent_row):
    total = parent_row.shape[0]
    labels = jnp.arange(total, dtype=jnp.int32)

    def climb(count, state):
        current, table = state
        current = jnp.sum(
            jnp.where(current[:, None] == labels[None, :], parent_row[None, :], 0), axis=1
        )
        table = jnp.maximum(table, (current[:, None] == labels[None, :]).astype(jnp.int32))
        return (current, table)

    start_index = (labels[:, None] == labels[None, :]).astype(jnp.int32)
    return lax.fori_loop(0, total, climb, (labels, start_index))[1]


def tree_mask(parent_row, pad_row, first, count, tree_length):
    table = ancestry(parent_row)
    segs_here = count // SEG
    segs_all = tree_length // SEG
    rows = lax.dynamic_slice_in_dim(table, first // SEG, segs_here, 0)
    linked = jnp.broadcast_to(rows[:, None, :, None] > 0, (segs_here, SEG, segs_all, SEG)).reshape(
        count, tree_length
    )
    query_pos = first + jnp.arange(count, dtype=jnp.int32)
    key_pos = jnp.arange(tree_length, dtype=jnp.int32)
    same = query_pos[:, None] // SEG == key_pos[None, :] // SEG
    causal = jnp.logical_or(jnp.logical_not(same), key_pos[None, :] <= query_pos[:, None])
    live = jnp.logical_or(pad_row[None, :] > 0, key_pos[None, :] == query_pos[:, None])
    return jnp.logical_and(jnp.logical_and(linked, causal), live)


def expert_kernel(
    chosen_ref,
    x_ref,
    g_ref,
    pos_ref,
    gate_ref,
    w1_ref,
    w2_ref,
    a1_ref,
    b1_ref,
    a2_ref,
    b2_ref,
    r_out,
    d_out,
    dg_out,
    grad_out,
    hot_s,
    o_s,
    dx_s,
    accr,
    accd,
    x_s,
    g_s,
    gate_s,
    b1_s,
    dgu_s,
    *,
    blocks,
    rows_block,
    cap,
    flush,
):
    e = pl.program_id(0)
    slot = lax.rem(e, flush)
    width = x_ref.shape[-1]

    @pl.when(e == 0)
    def _():
        b1_s[...] = jnp.zeros_like(b1_s)
        accr[...] = jnp.zeros_like(accr)
        accd[...] = jnp.zeros_like(accd)

    at = pl.multiple_of(slot * cap, 16)
    for b in range(blocks):
        here = pl.ds(b * rows_block, rows_block)
        there = pl.ds(b * cap, cap)
        places = lax.broadcasted_iota(jnp.int32, (cap, rows_block), 0)
        hit = places == pos_ref[0, b : b + 1, :]
        hot = hit.astype(F32).astype(BF16)
        hot_s[b, pl.ds(at, cap), :] = hot
        x_s[there, :] = product(hot, x_ref[here, :]).astype(BF16)
        g_s[there, :] = product(hot, g_ref[here, :]).astype(BF16)
        gate_s[there, :] = jnp.sum(
            jnp.where(hit, gate_ref[0, b : b + 1, :], 0.0), axis=1, keepdims=True
        )
    b1_s[0:RANK, 0:FF] = b1_ref[0, 0, 0]
    b1_s[RANK : 2 * RANK, FF : 2 * FF] = b1_ref[0, 0, 1]

    x = x_s[...]
    gate_col = gate_s[...]
    rank_in = product_back(x, a1_ref[0, 0]).astype(BF16)
    pre = product(x, w1_ref[0]) + product(rank_in, b1_s[...])
    gate_pre = pre[:, :FF]
    up_pre = pre[:, FF:]
    sig = 1.0 / (1.0 + jnp.exp(-gate_pre))
    act = gate_pre * sig
    hidden = (act * up_pre).astype(BF16)
    rank_down = product_back(hidden, a2_ref[0, 0]).astype(BF16)
    out = (product(hidden, w2_ref[0]) + product(rank_down, b2_ref[0, 0])).astype(BF16).astype(F32)
    g = g_s[...].astype(F32)
    d_gate_col = jnp.sum(g * out, axis=1, keepdims=True)
    out = (gate_col * out).astype(BF16)
    d_exp = (gate_col * g).astype(BF16)
    d_rank_down = product_back(d_exp, b2_ref[0, 0]).astype(BF16)
    d_hidden = product_back(d_exp, w2_ref[0]) + product(d_rank_down, a2_ref[0, 0])
    dgu_s[:, :FF] = (d_hidden * up_pre * sig * (1.0 + gate_pre * (1.0 - sig))).astype(BF16)
    dgu_s[:, FF:] = (d_hidden * act).astype(BF16)
    dgu = dgu_s[...]
    d_rank_in = product_back(dgu, b1_s[...]).astype(BF16)
    dx = (product_back(dgu, w1_ref[0]) + product(d_rank_in, a1_ref[0, 0])).astype(BF16)
    for b in range(blocks):
        o_s[b, pl.ds(at, cap), :] = out[b * cap : (b + 1) * cap]
        dx_s[b, pl.ds(at, cap), :] = dx[b * cap : (b + 1) * cap]
        places = lax.broadcasted_iota(jnp.int32, (cap, rows_block), 0)
        hit = places == pos_ref[0, b : b + 1, :]
        dg_out[0, b : b + 1, :] = jnp.sum(
            jnp.where(hit, d_gate_col[b * cap : (b + 1) * cap], 0.0), axis=0, keepdims=True
        )

    grad_a1 = product_outer(d_rank_in, x)
    grad_b1 = product_outer(rank_in, dgu)
    grad_a2 = product_outer(d_rank_down, hidden)
    grad_b2 = product_outer(rank_down, d_exp)
    parts = width // LANES
    base = 0
    for i in range(parts):
        grad_out[0, base : base + 2 * RANK, :] = grad_a1[:, i * LANES : (i + 1) * LANES].astype(BF16)
        base += 2 * RANK
    grad_out[0, base : base + RANK, :] = grad_b1[:RANK, :FF].astype(BF16)
    base += RANK
    grad_out[0, base : base + RANK, :] = grad_b1[RANK:, FF:].astype(BF16)
    base += RANK
    grad_out[0, base : base + RANK, :] = grad_a2.astype(BF16)
    base += RANK
    for i in range(parts):
        grad_out[0, base : base + RANK, :] = grad_b2[:, i * LANES : (i + 1) * LANES].astype(BF16)
        base += RANK

    @pl.when(slot == flush - 1)
    def _():
        for b in range(blocks):
            here = pl.ds(b * rows_block, rows_block)
            accr[here, :] += product_outer(hot_s[b], o_s[b])
            accd[here, :] += product_outer(hot_s[b], dx_s[b])

    @pl.when(e == pl.num_programs(0) - 1)
    def _():
        r_out[...] = accr[...].astype(BF16)
        d_out[...] = accd[...].astype(BF16)


def grad_rows(width):
    return (width // LANES) * 3 * RANK + 3 * RANK


def run_experts(chosen, x, g, pos, gate, w1, w2, a1, b1, a2, b2, cap):
    experts, blocks, rows_block = pos.shape
    width = x.shape[1]
    tokens = x.shape[0]
    rows = blocks * cap
    stored = grad_rows(width)
    flush = FLUSH if experts % FLUSH == 0 else 1
    whole = lambda e, c: (0, 0)
    lead = lambda e, c: (e, 0, 0)
    return pl.pallas_call(
        functools.partial(
            expert_kernel, blocks=blocks, rows_block=rows_block, cap=cap, flush=flush
        ),
        grid_spec=pltpu.PrefetchScalarGridSpec(
            num_scalar_prefetch=1,
            grid=(experts,),
            in_specs=[
                pl.BlockSpec((tokens, width), whole, pipeline_mode=pl.Buffered(1)),
                pl.BlockSpec((tokens, width), whole, pipeline_mode=pl.Buffered(1)),
                pl.BlockSpec((1, blocks, rows_block), lead),
                pl.BlockSpec((1, blocks, rows_block), lead),
                pl.BlockSpec((1, width, 2 * FF), lead),
                pl.BlockSpec((1, FF, width), lead),
                pl.BlockSpec((1, 1, 2 * RANK, width), lambda e, c: (c[0], e, 0, 0)),
                pl.BlockSpec((1, 1, 2, RANK, FF), lambda e, c: (c[0], e, 0, 0, 0)),
                pl.BlockSpec((1, 1, RANK, FF), lambda e, c: (c[0], e, 0, 0)),
                pl.BlockSpec((1, 1, RANK, width), lambda e, c: (c[0], e, 0, 0)),
            ],
            out_specs=[
                pl.BlockSpec((tokens, width), whole, pipeline_mode=pl.Buffered(1)),
                pl.BlockSpec((tokens, width), whole, pipeline_mode=pl.Buffered(1)),
                pl.BlockSpec((1, blocks, rows_block), lead),
                pl.BlockSpec((1, stored, LANES), lead),
            ],
            scratch_shapes=[
                pltpu.VMEM((blocks, flush * cap, rows_block), BF16),
                pltpu.VMEM((blocks, flush * cap, width), BF16),
                pltpu.VMEM((blocks, flush * cap, width), BF16),
                pltpu.VMEM((tokens, width), F32),
                pltpu.VMEM((tokens, width), F32),
                pltpu.VMEM((rows, width), BF16),
                pltpu.VMEM((rows, width), BF16),
                pltpu.VMEM((rows, 1), F32),
                pltpu.VMEM((2 * RANK, 2 * FF), BF16),
                pltpu.VMEM((rows, 2 * FF), BF16),
            ],
        ),
        out_shape=[
            jax.ShapeDtypeStruct((tokens, width), BF16),
            jax.ShapeDtypeStruct((tokens, width), BF16),
            jax.ShapeDtypeStruct((experts, blocks, rows_block), F32),
            jax.ShapeDtypeStruct((experts, stored, LANES), BF16),
        ],
        compiler_params=pltpu.CompilerParams(
            vmem_limit_bytes=62 * 1024 * 1024, dimension_semantics=("arbitrary",)
        ),
        cost_estimate=pl.CostEstimate(
            flops=120_000_000_000 * experts // 20,
            bytes_accessed=5_000_000 * experts,
            transcendentals=rows * FF * experts,
        ),
        name="experts",
    )(chosen, x, g, pos, gate, w1, w2, a1, b1, a2, b2)


def swap_pairs(size):
    return [(i, i ^ 1) for i in range(size)]


def gather_rows(half, groups):
    if groups != 2:
        return lax.all_gather(half, "grp", axis=0, tiled=True)
    rows = half.shape[0] // 2
    core = lax.axis_index("rep") % 2
    member = lax.axis_index("grp")
    mine = lax.dynamic_slice_in_dim(half, core * rows, rows, 0)
    got = lax.ppermute(mine, "grp", swap_pairs(2))
    other = lax.ppermute(got, "rep", swap_pairs(lax.axis_size("rep")))
    out = jnp.zeros((4 * rows,) + half.shape[1:], half.dtype)
    out = lax.dynamic_update_slice_in_dim(out, half, member * 2 * rows, 0)
    away = (1 - member) * 2 * rows
    out = lax.dynamic_update_slice_in_dim(out, got, away + core * rows, 0)
    return lax.dynamic_update_slice_in_dim(out, other, away + (1 - core) * rows, 0)


def pack(pieces, multiple):
    flat = jnp.concatenate([piece.reshape(-1) for piece in pieces])
    return jnp.pad(flat, (0, -flat.shape[0] % multiple))


def unpack(flat, shapes):
    out = []
    offset = 0
    for shape in shapes:
        size = 1
        for extent in shape:
            size *= extent
        out.append(flat[..., offset : offset + size].reshape(flat.shape[:-1] + shape))
        offset += size
    return out


def local(
    tokens,
    cotangent,
    routes,
    padding,
    parents,
    adapter_ids,
    w_query,
    w_keyval,
    w_output,
    w_router,
    gain_attn,
    gain_ffn,
    w_gateup,
    w_down,
    a_qkv,
    b_query,
    b_keyval,
    a_output,
    b_output,
    a_router,
    b_router,
    a_gateup,
    b_gateup,
    a_down,
    b_down,
):
    groups = lax.axis_size("grp")
    reps = lax.axis_size("rep")
    member = lax.axis_index("grp")
    count = tokens.shape[0]
    width = tokens.shape[1]
    part = width // groups
    tree_length = count * groups
    experts_dev = w_gateup.shape[0]
    experts = experts_dev * groups
    capacity = count * TOPK * 7 // (experts * 5)
    cap = -(-capacity // 16) * 16
    kv_width = KEY_VALUE_HEADS * HEAD_SIZE
    per_kv = QUERY_HEADS // KEY_VALUE_HEADS
    scale = HEAD_SIZE ** (-0.5)
    chosen = adapter_ids[0]
    first = member * count
    adapters = a_qkv.shape[0]

    shapes = (
        (3 * RANK, part),
        (RANK, part),
        (2, RANK, kv_width // groups),
        (RANK, part),
        (RANK, part),
        (RANK, part),
        (RANK, experts_dev),
        (experts, part),
        (part,),
        (part,),
        (count,),
    )
    small = pack(
        (
            a_qkv[chosen].T,
            b_query[chosen],
            b_keyval[chosen],
            a_output[chosen].T,
            b_output[chosen],
            a_router[chosen].T,
            b_router[chosen],
            w_router.T,
            gain_attn,
            gain_ffn,
            padding.astype(BF16),
        ),
        1024,
    )
    small_all = lax.all_gather(small, "grp", axis=0)

    def join(piece):
        return jnp.moveaxis(piece, 0, -2).reshape(piece.shape[1:-1] + (-1,))

    (
        qkv_in,
        query_out,
        keyval_out,
        output_in,
        output_out,
        router_in,
        router_out,
        router_full,
        attn_gain,
        ffn_gain,
        pad_all,
    ) = [join(piece) for piece in unpack(small_all, shapes)]
    attn_gain = attn_gain.astype(F32)
    ffn_gain = ffn_gain.astype(F32)
    keyval_full = gather_rows(w_keyval, groups)
    query_full = gather_rows(w_query, groups)
    output_full = gather_rows(w_output, groups)
    routes_all = lax.all_gather(routes, "grp", axis=0)
    upstream_all = lax.all_gather(cotangent, "grp", axis=0, tiled=True)
    ids_all = lax.all_gather(adapter_ids, "rep", axis=0, tiled=True)

    tokens_f = tokens.astype(F32)
    normed = rms_norm(tokens_f, attn_gain).astype(BF16)
    low_rank = product_back(normed, qkv_in).astype(BF16)
    query_rows = (product(normed, query_full) + product(low_rank[:, :RANK], query_out)).astype(BF16)
    keyvals = product(normed, keyval_full)
    key_rows = (keyvals[:, :kv_width] + product(low_rank[:, RANK : 2 * RANK], keyval_out[0])).astype(BF16)
    value_rows = (keyvals[:, kv_width:] + product(low_rank[:, 2 * RANK :], keyval_out[1])).astype(BF16)
    keyval_all = lax.all_gather(
        jnp.concatenate([key_rows, value_rows], axis=1), "grp", axis=0, tiled=True
    )
    every_key = keyval_all[:, :kv_width]
    every_value = keyval_all[:, kv_width:]
    mask = tree_mask(parents[0], pad_all, first, count, tree_length)
    heads_of_query = query_rows.reshape(count, KEY_VALUE_HEADS, per_kv, HEAD_SIZE).transpose(1, 0, 2, 3)
    heads_of_key = every_key.reshape(tree_length, KEY_VALUE_HEADS, HEAD_SIZE).transpose(1, 0, 2)
    heads_of_value = every_value.reshape(tree_length, KEY_VALUE_HEADS, HEAD_SIZE).transpose(1, 0, 2)

    def attend(operands):
        query_grp, key_grp, value_grp = operands
        scores = jnp.einsum("qrd,kd->rqk", query_grp, key_grp, preferred_element_type=F32) * scale
        scores = jnp.where(mask[None], scores, -1e30)
        top = jnp.max(scores, axis=-1, keepdims=True)
        weights = jnp.exp(scores - top)
        total = jnp.sum(weights, axis=-1, keepdims=True)
        probs = (weights / total).astype(BF16)
        mixed = jnp.einsum("rqk,kd->qrd", probs, value_grp, preferred_element_type=F32)
        return (mixed.astype(BF16), top[..., 0] + jnp.log(total[..., 0]))

    mixed_heads, log_totals = lax.map(attend, (heads_of_query, heads_of_key, heads_of_value))
    attended = mixed_heads.transpose(1, 0, 2, 3).reshape(count, width)
    out_rank = product_back(attended, output_in).astype(BF16)
    middle = tokens_f + product(attended, output_full) + product(out_rank, output_out)
    normed_ffn = rms_norm(middle, ffn_gain).astype(BF16)
    router_rank = product_back(normed_ffn, router_in).astype(BF16)
    logits = product_back(normed_ffn, router_full) + product(router_rank, router_out)

    labels = jnp.arange(experts, dtype=jnp.int32)
    named = jnp.any(routes[:, :, None] == labels, axis=1)
    best = jnp.max(jnp.where(named, logits, -jnp.inf), axis=1, keepdims=True)
    powers = jnp.where(named, jnp.exp(jnp.where(named, logits, best) - best), 0.0)
    gates = powers / jnp.sum(powers, axis=1, keepdims=True)

    mine = member * experts_dev + jnp.arange(experts_dev, dtype=jnp.int32)
    hits = jnp.any(routes_all[:, :, :, None] == mine, axis=2)
    before = (jnp.arange(count)[:, None] > jnp.arange(count)[None, :]).astype(BF16)
    ranks = jnp.einsum("ts,gse->get", before, hits.astype(BF16), preferred_element_type=F32)
    places = jnp.where(hits.transpose(0, 2, 1), ranks.astype(jnp.int32), -1).transpose(1, 0, 2)

    rows_all = lax.all_gather(normed_ffn, "grp", axis=0, tiled=True)
    gates_all = lax.all_gather(gates.T, "grp", axis=0)
    gates_mine = lax.dynamic_slice_in_dim(gates_all, member * experts_dev, experts_dev, 1).transpose(1, 0, 2)
    part_result, part_d, part_gates, expert_grads = run_experts(
        adapter_ids,
        rows_all,
        upstream_all,
        places,
        gates_mine,
        w_gateup,
        w_down,
        a_gateup.swapaxes(2, 3),
        b_gateup,
        a_down.swapaxes(2, 3),
        b_down,
        cap,
    )

    owner_hot = (jnp.arange(adapters, dtype=jnp.int32)[:, None] == ids_all[None, :]).astype(F32)
    stored = expert_grads.shape[1]
    share = experts_dev * stored // reps
    swapped = lax.all_to_all(
        expert_grads.reshape(reps, share, LANES), "rep", split_axis=0, concat_axis=0, tiled=True
    )
    summed = jnp.sum(owner_hot[:, :, None, None] * swapped.astype(F32)[None], axis=1).astype(BF16)
    spread = lax.all_gather(summed, "rep", axis=1).reshape(adapters, experts_dev, stored, LANES)

    def lanes_joined(rows, height):
        return rows.reshape(adapters, experts_dev, -1, height, LANES).swapaxes(2, 3).reshape(
            adapters, experts_dev, height, -1
        )

    parts = width // LANES
    edges = [0, parts * 2 * RANK, parts * 2 * RANK + 2 * RANK, parts * 2 * RANK + 3 * RANK, stored]
    grad_a_gateup = lanes_joined(spread[:, :, : edges[1]], 2 * RANK).swapaxes(2, 3).astype(F32)
    grad_b_gateup = spread[:, :, edges[1] : edges[2]].reshape(adapters, experts_dev, 2, RANK, FF).astype(F32)
    grad_a_down = spread[:, :, edges[2] : edges[3]].swapaxes(2, 3).astype(F32)
    grad_b_down = lanes_joined(spread[:, :, edges[3] :], RANK).astype(F32)

    both = lax.psum_scatter(
        jnp.concatenate([part_d, part_result], axis=1), "grp", scatter_dimension=0, tiled=True
    ).astype(F32)
    d_gates = lax.all_to_all(part_gates, "grp", split_axis=1, concat_axis=0, tiled=True)
    d_gates = d_gates.reshape(experts, count).T
    result = (middle + both[:, width:]).astype(BF16)
    upstream = cotangent.astype(F32)
    d_logits = (gates * (d_gates - jnp.sum(gates * d_gates, axis=1, keepdims=True))).astype(BF16)

    d_router_rank = product_back(d_logits, router_out).astype(BF16)
    d_normed_ffn = both[:, :width] + product(d_logits, router_full) + product(d_router_rank, router_in)
    grad_router_out = product_outer(router_rank, d_logits)
    grad_router_in = product_outer(d_router_rank, normed_ffn)
    d_middle = upstream + rms_back(middle, ffn_gain, d_normed_ffn)
    d_attn = d_middle.astype(BF16)
    d_out_rank = product_back(d_attn, output_out).astype(BF16)
    attended_gradient = (product_back(d_attn, output_full) + product(d_out_rank, output_in)).astype(BF16)
    grad_output_out = product_outer(out_rank, d_attn)
    grad_output_in = product_outer(d_out_rank, attended)
    heads_gradient = attended_gradient.reshape(count, KEY_VALUE_HEADS, per_kv, HEAD_SIZE).transpose(1, 0, 2, 3)

    def attend_back(operands):
        query_grp, key_grp, value_grp, d_grp, log_total = operands
        scores = jnp.einsum("qrd,kd->rqk", query_grp, key_grp, preferred_element_type=F32) * scale
        scores = jnp.where(mask[None], scores, -1e30)
        probs = jnp.exp(scores - log_total[..., None])
        d_value = jnp.einsum("rqk,qrd->kd", probs.astype(BF16), d_grp, preferred_element_type=F32)
        d_probs = jnp.einsum("qrd,kd->rqk", d_grp, value_grp, preferred_element_type=F32)
        d_scores = (probs * (d_probs - jnp.sum(probs * d_probs, axis=-1, keepdims=True))).astype(BF16)
        d_query = jnp.einsum("rqk,kd->qrd", d_scores, key_grp, preferred_element_type=F32) * scale
        d_key = jnp.einsum("rqk,qrd->kd", d_scores, query_grp, preferred_element_type=F32) * scale
        return (d_query, d_key, d_value)

    d_query_heads, d_key_heads, d_value_heads = lax.map(
        attend_back, (heads_of_query, heads_of_key, heads_of_value, heads_gradient, log_totals)
    )
    d_queries = d_query_heads.transpose(1, 0, 2, 3).reshape(count, width).astype(BF16)
    d_keys_part = d_key_heads.transpose(1, 0, 2).reshape(tree_length, kv_width)
    d_values_part = d_value_heads.transpose(1, 0, 2).reshape(tree_length, kv_width)
    d_keyvals = lax.psum_scatter(
        jnp.concatenate([d_keys_part, d_values_part], axis=1).astype(BF16),
        "grp",
        scatter_dimension=0,
        tiled=True,
    )
    d_keys = d_keyvals[:, :kv_width]
    d_values = d_keyvals[:, kv_width:]
    d_rank_qkv = jnp.concatenate(
        [
            product_back(d_queries, query_out),
            product_back(d_keys, keyval_out[0]),
            product_back(d_values, keyval_out[1]),
        ],
        axis=-1,
    ).astype(BF16)
    d_normed = (
        product_back(d_queries, query_full)
        + product_back(d_keyvals, keyval_full)
        + product(d_rank_qkv, qkv_in)
    )
    grad_input = (d_middle + rms_back(tokens_f, attn_gain, d_normed)).astype(BF16)
    grad_qkv_in = product_outer(d_rank_qkv, normed)
    grad_query_out = product_outer(low_rank[:, :RANK], d_queries)
    grad_keyval_out = jnp.stack(
        [
            product_outer(low_rank[:, RANK : 2 * RANK], d_keys),
            product_outer(low_rank[:, 2 * RANK :], d_values),
        ],
        axis=0,
    )

    def split(gradient):
        return jnp.moveaxis(
            gradient.astype(BF16).reshape(gradient.shape[:-1] + (groups, -1)), -2, 0
        ).reshape(groups, -1)

    dense = jnp.concatenate(
        [
            split(piece)
            for piece in (
                grad_qkv_in,
                grad_query_out,
                grad_keyval_out,
                grad_output_in,
                grad_output_out,
                grad_router_in,
                grad_router_out,
            )
        ],
        axis=1,
    )
    dense = jnp.pad(dense, ((0, 0), (0, -dense.shape[1] % (reps * 128))))
    dense = dense.reshape(groups, reps, -1).swapaxes(0, 1).reshape(reps * groups, -1)
    dense = lax.all_to_all(dense, ("rep", "grp"), split_axis=0, concat_axis=0, tiled=True)
    dense = jnp.sum(dense.reshape(reps, groups, -1).astype(F32), axis=1)
    dense = jnp.sum(owner_hot[:, :, None] * dense[None], axis=1).astype(BF16)
    dense = lax.all_gather(dense, "rep", axis=1).reshape(adapters, -1)
    owned = [piece.astype(F32) for piece in unpack(dense, shapes[:7])]
    return (
        result,
        grad_input,
        owned[0].swapaxes(1, 2),
        owned[1],
        owned[2],
        owned[3].swapaxes(1, 2),
        owned[4],
        owned[5].swapaxes(1, 2),
        owned[6],
        grad_a_gateup,
        grad_b_gateup,
        grad_a_down,
        grad_b_down,
    )


def solution(mesh):
    in_specs = (
        P(("rep", "grp"), None),
        P(("rep", "grp"), None),
        P(("rep", "grp"), None),
        P(("rep", "grp")),
        P("rep", None),
        P("rep"),
        P("grp", None),
        P("grp", None),
        P("grp", None),
        P("grp", None),
        P("grp"),
        P("grp"),
        P("grp", None, None),
        P("grp", None, None),
        P(None, "grp", None),
        P(None, None, "grp"),
        P(None, None, None, "grp"),
        P(None, "grp", None),
        P(None, None, "grp"),
        P(None, "grp", None),
        P(None, None, "grp"),
        P(None, "grp", None, None),
        P(None, "grp", None, None, None),
        P(None, "grp", None, None),
        P(None, "grp", None, None),
    )
    out_specs = (
        P(("rep", "grp"), None),
        P(("rep", "grp"), None),
        P(None, "grp", None),
        P(None, None, "grp"),
        P(None, None, None, "grp"),
        P(None, "grp", None),
        P(None, None, "grp"),
        P(None, "grp", None),
        P(None, None, "grp"),
        P(None, "grp", None, None),
        P(None, "grp", None, None, None),
        P(None, "grp", None, None),
        P(None, "grp", None, None),
    )
    return jax.shard_map(local, mesh=mesh, in_specs=in_specs, out_specs=out_specs, check_vma=False)
```

```python
import functools

import jax
import jax.numpy as jnp
from jax import lax
from jax.experimental import pallas as pl
from jax.experimental.pallas import tpu as pltpu
from jax.sharding import PartitionSpec as P

QUERY_HEADS = 24
KEY_VALUE_HEADS = 8
HEAD_SIZE = 64
FF = 512
TOPK = 8
RANK = 16
SEG = 128
FLUSH = 5

EPSILON = 1e-05
BF16 = jnp.bfloat16
F32 = jnp.float32


def product(left, right):
    return jnp.dot(left, right, preferred_element_type=F32)


def product_back(left, right):
    return lax.dot_general(left, right, (((1,), (1,)), ((), ())), preferred_element_type=F32)


def product_outer(left, right):
    return lax.dot_general(left, right, (((0,), (0,)), ((), ())), preferred_element_type=F32)


def rms_norm(value_rows, gain):
    return (
        value_rows
        * lax.rsqrt(jnp.mean(value_rows * value_rows, axis=-1, keepdims=True) + EPSILON)
        * gain
    )


def rms_back(value_rows, gain, upstream):
    factor = lax.rsqrt(jnp.mean(value_rows * value_rows, axis=-1, keepdims=True) + EPSILON)
    scaled = value_rows * factor
    incoming = upstream * gain
    return factor * (incoming - scaled * jnp.mean(incoming * scaled, axis=-1, keepdims=True))


def ancestry(parent_row):
    total = parent_row.shape[0]
    labels = jnp.arange(total, dtype=jnp.int32)

    def climb(count, state):
        current, table = state
        current = jnp.sum(
            jnp.where(current[:, None] == labels[None, :], parent_row[None, :], 0), axis=1
        )
        table = jnp.maximum(table, (current[:, None] == labels[None, :]).astype(jnp.int32))
        return (current, table)

    start_index = (labels[:, None] == labels[None, :]).astype(jnp.int32)
    return lax.fori_loop(0, total, climb, (labels, start_index))[1]


def tile_parts(ref_k, seg_a, seg_b):
    return jnp.concatenate(
        [
            ref_k[pl.ds(pl.multiple_of(seg_a * SEG, SEG), SEG), :],
            ref_k[pl.ds(pl.multiple_of(seg_b * SEG, SEG), SEG), :],
        ],
        axis=0,
    )


def fill_doubled(held, near_ref, far_ref, ones=False):
    near = near_ref.shape[0]
    for ref, at in ((near_ref, 0), (far_ref, near)):
        rows = ref[...].astype(F32)
        low = lax.broadcasted_iota(jnp.int32, rows.shape, 1) < HEAD_SIZE
        turned = pltpu.roll(rows, HEAD_SIZE, axis=1)
        there = pl.ds(at, rows.shape[0])
        held[0, there, :] = jnp.where(low, rows, 1.0 if ones else turned).astype(BF16)
        held[1, there, :] = jnp.where(low, turned, 1.0 if ones else rows).astype(BF16)


PLACES = (((0, 0), (0, 1), (1, 0)), ((1, 1), (2, 0), (2, 1)))


def stacked_heads(ref, at, which, scale=None):
    low = lax.broadcasted_iota(jnp.int32, (SEG, 2 * HEAD_SIZE), 1) < HEAD_SIZE
    out = []
    for column, half in PLACES[which]:
        piece = ref[at, column * 2 * HEAD_SIZE : (column + 1) * 2 * HEAD_SIZE].astype(F32)
        if scale is not None:
            piece = piece * scale
        out.append(jnp.where(low if half == 0 else jnp.logical_not(low), piece, 0.0))
    return jnp.concatenate(out, axis=0)


def unstack(first, second):
    low = lax.broadcasted_iota(jnp.int32, (SEG, 2 * HEAD_SIZE), 1) < HEAD_SIZE
    return [
        jnp.where(low, first[0:SEG], first[SEG : 2 * SEG]),
        jnp.where(low, first[2 * SEG :], second[0:SEG]),
        jnp.where(low, second[SEG : 2 * SEG], second[2 * SEG :]),
    ]


def first_bias(own_ref, live_ref, i, seg_b):
    other = jnp.broadcast_to(live_ref[seg_b], (SEG, SEG))
    tile = jnp.concatenate([own_ref[i], other], axis=1)
    return jnp.concatenate([tile] * 3, axis=0)


def next_bias(live_ref, seg_a, seg_b):
    return jnp.concatenate([live_ref[seg_a], live_ref[seg_b]], axis=1)


def attend_kernel(
    list_ref,
    steps_ref,
    q_ref,
    k_ref,
    v_ref,
    k_far,
    v_far,
    own_ref,
    live_ref,
    o_ref,
    l_ref,
    kf,
    vf,
    *,
    here,
    segs,
    scale,
):
    fill_doubled(kf, k_ref, k_far)
    fill_doubled(vf, v_ref, v_far, ones=True)
    lanes = lax.broadcasted_iota(jnp.int32, (SEG, 2 * HEAD_SIZE), 1)
    low = lanes < HEAD_SIZE
    slots = 2 * segs
    for i in range(here):
        at = pl.ds(i * SEG, SEG)
        queries = [stacked_heads(q_ref, at, which, scale).astype(BF16) for which in range(2)]

        def pair_of(t):
            return (
                lax.rem(list_ref[i * slots + 2 * t], segs),
                lax.rem(list_ref[i * slots + 2 * t + 1], segs),
            )

        seg_a, seg_b = pair_of(0)
        bias = first_bias(own_ref, live_ref, i, list_ref[i * slots + 1])
        state = []
        for which in range(2):
            s = product_back(queries[which], tile_parts(kf.at[which], seg_a, seg_b)) + bias
            top = jnp.max(s, axis=1, keepdims=True)
            p = jnp.exp(s - top).astype(BF16)
            state.append((top, product(p, tile_parts(vf.at[which], seg_a, seg_b))))

        def body(t, state):
            bias = next_bias(live_ref, list_ref[i * slots + 2 * t], list_ref[i * slots + 2 * t + 1])
            seg_a, seg_b = pair_of(t)
            out = []
            for which in range(2):
                top, acc = state[which]
                s = product_back(queries[which], tile_parts(kf.at[which], seg_a, seg_b)) + bias
                higher = jnp.maximum(top, jnp.max(s, axis=1, keepdims=True))
                p = jnp.exp(s - higher).astype(BF16)
                acc = acc * jnp.exp(top - higher) + product(p, tile_parts(vf.at[which], seg_a, seg_b))
                out.append((higher, acc))
            return tuple(out)

        state = lax.fori_loop(1, steps_ref[i], body, tuple(state))
        turned = [pltpu.roll(acc, HEAD_SIZE, axis=1) for _, acc in state]
        logs = jnp.zeros((SEG, 2 * HEAD_SIZE), F32)
        heads = []
        for which in range(2):
            for n, (_, half) in enumerate(PLACES[which]):
                rows = slice(n * SEG, (n + 1) * SEG)
                plain, other = state[which][1][rows], turned[which][rows]
                heads.append(plain / other if half == 0 else other / plain)
                total = jnp.where(low, other, plain)
                logs = jnp.where(lanes == which * 3 + n, state[which][0][rows] + jnp.log(total), logs)
        l_ref[0, at, :] = logs
        for column in range(3):
            o_ref[at, column * 2 * HEAD_SIZE : (column + 1) * 2 * HEAD_SIZE] = jnp.where(
                low, heads[2 * column], heads[2 * column + 1]
            ).astype(BF16)


def attend_back_kernel(
    list_ref,
    steps_ref,
    q_ref,
    k_ref,
    v_ref,
    k_far,
    v_far,
    own_ref,
    live_ref,
    o_ref,
    do_ref,
    l_ref,
    dq_ref,
    dk_ref,
    dv_ref,
    dk_far,
    dv_far,
    kf,
    vf,
    dkf,
    dvf,
    *,
    here,
    segs,
    scale,
):
    fill_doubled(kf, k_ref, k_far)
    fill_doubled(vf, v_ref, v_far)
    dkf[...] = jnp.zeros_like(dkf)
    dvf[...] = jnp.zeros_like(dvf)
    slots = 2 * segs
    for i in range(here):
        at = pl.ds(i * SEG, SEG)
        fixed = []
        for which in range(2):
            d_o = stacked_heads(do_ref, at, which)
            fixed.append(
                (
                    stacked_heads(q_ref, at, which, scale).astype(BF16),
                    d_o.astype(BF16),
                    jnp.sum(d_o * stacked_heads(o_ref, at, which), axis=1, keepdims=True),
                    jnp.concatenate(
                        [l_ref[0, at, which * 3 + n : which * 3 + n + 1] for n in range(3)], axis=0
                    ),
                )
            )

        def step(t, bias):
            seg_a = lax.rem(list_ref[i * slots + 2 * t], segs)
            seg_b = lax.rem(list_ref[i * slots + 2 * t + 1], segs)
            out = []
            for which, (q, d_o, delta, log_total) in enumerate(fixed):
                k = tile_parts(kf.at[which], seg_a, seg_b)
                v = tile_parts(vf.at[which], seg_a, seg_b)
                p = jnp.exp(product_back(q, k) + bias - log_total)
                d_p = product_back(d_o, v)
                d_s = (p * (d_p - delta)).astype(BF16)
                d_v = product_outer(p.astype(BF16), d_o)
                d_k = product_outer(d_s, q)
                for n, seg in enumerate((seg_a, seg_b)):
                    rows = pl.ds(pl.multiple_of(seg * SEG, SEG), SEG)
                    dkf[which, rows, :] += d_k[n * SEG : (n + 1) * SEG]
                    dvf[which, rows, :] += d_v[n * SEG : (n + 1) * SEG]
                out.append(product(d_s, k))
            return tuple(out)

        d_q = step(0, first_bias(own_ref, live_ref, i, list_ref[i * slots + 1]))

        def body(t, carry):
            bias = next_bias(live_ref, list_ref[i * slots + 2 * t], list_ref[i * slots + 2 * t + 1])
            return tuple(a + b for a, b in zip(carry, step(t, bias)))

        d_q = lax.fori_loop(1, steps_ref[i], body, d_q)
        for column, piece in enumerate(unstack(*d_q)):
            dq_ref[at, column * 2 * HEAD_SIZE : (column + 1) * 2 * HEAD_SIZE] = (piece * scale).astype(BF16)
    near = dk_ref.shape[0]
    for out, far_out, held in ((dk_ref, dk_far, dkf), (dv_ref, dv_far, dvf)):
        first = held[0] + pltpu.roll(held[0], HEAD_SIZE, axis=1)
        second = held[1] + pltpu.roll(held[1], HEAD_SIZE, axis=1)
        low = lax.broadcasted_iota(jnp.int32, first.shape, 1) < HEAD_SIZE
        total = jnp.where(low, first, second).astype(BF16)
        out[...] = total[:near]
        far_out[...] = total[near:]


def visits(parent_row, pad_near, pad_far, first):
    count = pad_near.shape[0]
    tree_length = count + pad_far.shape[0]
    segs = tree_length // SEG
    here = count // SEG
    own = jnp.arange(here, dtype=jnp.int32)
    labels = jnp.arange(segs, dtype=jnp.int32)
    table = lax.dynamic_slice_in_dim(ancestry(parent_row), first // SEG, here, 0)
    turn = (labels[:, None] == (labels[None, :] + segs - first // SEG) % segs).astype(F32)
    table = product_back(table.astype(F32), turn).astype(jnp.int32)
    table = jnp.where(labels[None, :] == own[:, None], 0, table)
    order = jnp.sum(jnp.where(labels[None, :] <= labels[:, None], table[:, None, :], 0), axis=2)
    spots = jnp.arange(1, 2 * segs, dtype=jnp.int32)
    found = jnp.logical_and(table[:, None, :] > 0, order[:, None, :] == spots[None, :, None])
    listing = jnp.where(jnp.any(found, axis=2), jnp.sum(found * labels, axis=2), segs)
    listing = jnp.concatenate([own[:, None], listing], axis=1).astype(jnp.int32)
    steps = (2 + order[:, -1]) // 2
    live = jnp.where(jnp.concatenate([pad_near, pad_far]) > 0, 0.0, -1e30).astype(F32).reshape(segs, SEG)
    places = jnp.arange(SEG)
    causal = places[None, :] <= places[:, None]
    same = places[None, :] == places[:, None]
    own_bias = jnp.where(same[None], 0.0, jnp.where(causal[None], live[:here, None, :], -1e30))
    live = jnp.concatenate([live, jnp.full((1, SEG), -1e30, F32)], axis=0)[:, None, :]
    return listing.reshape(-1), steps.astype(jnp.int32), own_bias, live


def attention_specs(count, far, here, segs):
    narrow = 2 * HEAD_SIZE
    shift = KEY_VALUE_HEADS // 2
    return [
        pl.BlockSpec((count, 3 * narrow), lambda h, a, b: (0, h)),
        pl.BlockSpec((count, narrow), lambda h, a, b: (0, h)),
        pl.BlockSpec((count, narrow), lambda h, a, b: (0, h + shift)),
        pl.BlockSpec((far, narrow), lambda h, a, b: (0, h)),
        pl.BlockSpec((far, narrow), lambda h, a, b: (0, h + shift)),
        pl.BlockSpec((here, SEG, SEG), lambda h, a, b: (0, 0, 0)),
        pl.BlockSpec((segs + 1, 1, SEG), lambda h, a, b: (0, 0, 0)),
    ]


def run_attention(listing, steps, queries, near, far, own_bias, live):
    count, width = queries.shape
    tree_length = count + far.shape[0]
    here, segs = count // SEG, tree_length // SEG
    pairs = KEY_VALUE_HEADS // 2
    narrow = 2 * HEAD_SIZE
    return pl.pallas_call(
        functools.partial(attend_kernel, here=here, segs=segs, scale=HEAD_SIZE ** (-0.5)),
        grid_spec=pltpu.PrefetchScalarGridSpec(
            num_scalar_prefetch=2,
            grid=(pairs,),
            in_specs=attention_specs(count, far.shape[0], here, segs),
            out_specs=[
                pl.BlockSpec((count, 3 * narrow), lambda h, a, b: (0, h)),
                pl.BlockSpec((1, count, narrow), lambda h, a, b: (h, 0, 0)),
            ],
            scratch_shapes=[pltpu.VMEM((2, tree_length, narrow), BF16)] * 2,
        ),
        out_shape=[
            jax.ShapeDtypeStruct((count, width), BF16),
            jax.ShapeDtypeStruct((pairs, count, narrow), F32),
        ],
        compiler_params=pltpu.CompilerParams(
            vmem_limit_bytes=40 * 1024 * 1024, dimension_semantics=("arbitrary",)
        ),
        cost_estimate=pl.CostEstimate(flops=40_000_000_000, bytes_accessed=8_000_000, transcendentals=10_000_000),
        name="attention",
    )(listing, steps, queries, near, near, far, far, own_bias, live)


def run_attention_back(listing, steps, queries, near, far, own_bias, live, attended, gradient, logs):
    count, width = queries.shape
    tree_length = count + far.shape[0]
    here, segs = count // SEG, tree_length // SEG
    pairs = KEY_VALUE_HEADS // 2
    narrow = 2 * HEAD_SIZE
    rows = pl.BlockSpec((count, 3 * narrow), lambda h, a, b: (0, h))
    outs = [pl.BlockSpec((count, narrow), lambda h, a, b: (0, h))] * 2
    outs += [pl.BlockSpec((far.shape[0], narrow), lambda h, a, b: (0, h))] * 2
    return pl.pallas_call(
        functools.partial(attend_back_kernel, here=here, segs=segs, scale=HEAD_SIZE ** (-0.5)),
        grid_spec=pltpu.PrefetchScalarGridSpec(
            num_scalar_prefetch=2,
            grid=(pairs,),
            in_specs=attention_specs(count, far.shape[0], here, segs)
            + [rows, rows, pl.BlockSpec((1, count, narrow), lambda h, a, b: (h, 0, 0))],
            out_specs=[rows] + outs,
            scratch_shapes=[pltpu.VMEM((2, tree_length, narrow), BF16)] * 2
            + [pltpu.VMEM((2, tree_length, narrow), F32)] * 2,
        ),
        out_shape=[jax.ShapeDtypeStruct((count, width), BF16)]
        + [jax.ShapeDtypeStruct((count, pairs * narrow), BF16)] * 2
        + [jax.ShapeDtypeStruct((far.shape[0], pairs * narrow), BF16)] * 2,
        compiler_params=pltpu.CompilerParams(
            vmem_limit_bytes=40 * 1024 * 1024, dimension_semantics=("arbitrary",)
        ),
        cost_estimate=pl.CostEstimate(flops=70_000_000_000, bytes_accessed=12_000_000, transcendentals=10_000_000),
        name="attention_back",
    )(listing, steps, queries, near, near, far, far, own_bias, live, attended, gradient, logs)


def expert_kernel(
    chosen_ref,
    x_ref,
    x_far,
    g_ref,
    g_far,
    pos_ref,
    gate_ref,
    w1_ref,
    w2_ref,
    a1_ref,
    b1_ref,
    a2_ref,
    b2_ref,
    r_out,
    r_far,
    d_out,
    d_far,
    dg_out,
    grad_out,
    hot_s,
    o_s,
    dx_s,
    accr,
    accd,
    x_s,
    g_s,
    gate_s,
    b1_s,
    dgu_s,
    *,
    blocks,
    rows_block,
    cap,
    flush,
):
    e = pl.program_id(0)
    slot = lax.rem(e, flush)
    width = x_ref.shape[-1]

    @pl.when(e == 0)
    def _():
        b1_s[...] = jnp.zeros_like(b1_s)
        accr[...] = jnp.zeros_like(accr)
        accd[...] = jnp.zeros_like(accd)

    at = pl.multiple_of(slot * cap, 16)
    for b in range(blocks):
        rows_ref, g_rows_ref = (x_ref, g_ref) if b == 0 else (x_far, g_far)
        here = pl.ds(max(b - 1, 0) * rows_block, rows_block)
        there = pl.ds(b * cap, cap)
        places = lax.broadcasted_iota(jnp.int32, (cap, rows_block), 0)
        hit = places == pos_ref[0, b : b + 1, :]
        hot = hit.astype(F32).astype(BF16)
        hot_s[b, pl.ds(at, cap), :] = hot
        x_s[there, :] = product(hot, rows_ref[here, :]).astype(BF16)
        g_s[there, :] = product(hot, g_rows_ref[here, :]).astype(BF16)
        gate_s[there, :] = jnp.sum(
            jnp.where(hit, gate_ref[0, b : b + 1, :], 0.0), axis=1, keepdims=True
        )
    b1_s[0:RANK, 0:FF] = b1_ref[0, 0, 0]
    b1_s[RANK : 2 * RANK, FF : 2 * FF] = b1_ref[0, 0, 1]

    x = x_s[...]
    gate_col = gate_s[...]
    rank_in = product_back(x, a1_ref[0, 0]).astype(BF16)
    pre = product(x, w1_ref[0]) + product(rank_in, b1_s[...])
    gate_pre = pre[:, :FF]
    up_pre = pre[:, FF:]
    sig = 1.0 / (1.0 + jnp.exp(-gate_pre))
    act = gate_pre * sig
    hidden = (act * up_pre).astype(BF16)
    rank_down = product_back(hidden, a2_ref[0, 0]).astype(BF16)
    out = (product(hidden, w2_ref[0]) + product(rank_down, b2_ref[0, 0])).astype(BF16).astype(F32)
    g = g_s[...].astype(F32)
    d_gate_col = jnp.sum(g * out, axis=1, keepdims=True)
    out = (gate_col * out).astype(BF16)
    d_exp = (gate_col * g).astype(BF16)
    d_rank_down = product_back(d_exp, b2_ref[0, 0]).astype(BF16)
    d_hidden = product_back(d_exp, w2_ref[0]) + product(d_rank_down, a2_ref[0, 0])
    dgu_s[:, :FF] = (d_hidden * up_pre * sig * (1.0 + gate_pre * (1.0 - sig))).astype(BF16)
    dgu_s[:, FF:] = (d_hidden * act).astype(BF16)
    dgu = dgu_s[...]
    d_rank_in = product_back(dgu, b1_s[...]).astype(BF16)
    dx = (product_back(dgu, w1_ref[0]) + product(d_rank_in, a1_ref[0, 0])).astype(BF16)
    for b in range(blocks):
        o_s[b, pl.ds(at, cap), :] = out[b * cap : (b + 1) * cap]
        dx_s[b, pl.ds(at, cap), :] = dx[b * cap : (b + 1) * cap]
        places = lax.broadcasted_iota(jnp.int32, (cap, rows_block), 0)
        hit = places == pos_ref[0, b : b + 1, :]
        dg_out[0, b : b + 1, :] = jnp.sum(
            jnp.where(hit, d_gate_col[b * cap : (b + 1) * cap], 0.0), axis=0, keepdims=True
        )

    grad_a1 = product_outer(d_rank_in, x)
    grad_b1 = product_outer(rank_in, dgu)
    grad_a2 = product_outer(d_rank_down, hidden)
    grad_b2 = product_outer(rank_down, d_exp)
    grad_out[0, 0 : 2 * RANK, :] = grad_a1.astype(BF16)
    grad_out[0, 2 * RANK : 3 * RANK, :] = grad_b2.astype(BF16)
    grad_out[0, 3 * RANK :, :FF] = grad_b1[:RANK, :FF].astype(BF16)
    grad_out[0, 3 * RANK :, FF : 2 * FF] = grad_b1[RANK:, FF:].astype(BF16)
    grad_out[0, 3 * RANK :, 2 * FF :] = grad_a2.astype(BF16)

    @pl.when(slot == flush - 1)
    def _():
        for b in range(blocks):
            here = pl.ds(b * rows_block, rows_block)
            accr[here, :] += product_outer(hot_s[b], o_s[b])
            accd[here, :] += product_outer(hot_s[b], dx_s[b])

    @pl.when(e == pl.num_programs(0) - 1)
    def _():
        r_out[...] = accr[0:rows_block, :].astype(BF16)
        r_far[...] = accr[rows_block:, :].astype(BF16)
        d_out[...] = accd[0:rows_block, :].astype(BF16)
        d_far[...] = accd[rows_block:, :].astype(BF16)


def run_experts(chosen, x, x_far, g, g_far, pos, gate, w1, w2, a1, b1, a2, b2, cap):
    experts, blocks, rows_block = pos.shape
    width = x.shape[1]
    tokens = blocks * rows_block
    rows = blocks * cap
    flush = FLUSH if experts % FLUSH == 0 else 1
    lead = lambda e, c: (e, 0, 0)
    near = pl.BlockSpec((rows_block, width), lambda e, c: (0, 0), pipeline_mode=pl.Buffered(1))
    away = pl.BlockSpec((tokens - rows_block, width), lambda e, c: (0, 0), pipeline_mode=pl.Buffered(1))
    near_shape = jax.ShapeDtypeStruct((rows_block, width), BF16)
    away_shape = jax.ShapeDtypeStruct((tokens - rows_block, width), BF16)
    return pl.pallas_call(
        functools.partial(
            expert_kernel, blocks=blocks, rows_block=rows_block, cap=cap, flush=flush
        ),
        grid_spec=pltpu.PrefetchScalarGridSpec(
            num_scalar_prefetch=1,
            grid=(experts,),
            in_specs=[
                near,
                away,
                near,
                away,
                pl.BlockSpec((1, blocks, rows_block), lead),
                pl.BlockSpec((1, blocks, rows_block), lead),
                pl.BlockSpec((1, width, 2 * FF), lead),
                pl.BlockSpec((1, FF, width), lead),
                pl.BlockSpec((1, 1, 2 * RANK, width), lambda e, c: (c[0], e, 0, 0)),
                pl.BlockSpec((1, 1, 2, RANK, FF), lambda e, c: (c[0], e, 0, 0, 0)),
                pl.BlockSpec((1, 1, RANK, FF), lambda e, c: (c[0], e, 0, 0)),
                pl.BlockSpec((1, 1, RANK, width), lambda e, c: (c[0], e, 0, 0)),
            ],
            out_specs=[
                near,
                away,
                near,
                away,
                pl.BlockSpec((1, blocks, rows_block), lead),
                pl.BlockSpec((1, 4 * RANK, width), lead),
            ],
            scratch_shapes=[
                pltpu.VMEM((blocks, flush * cap, rows_block), BF16),
                pltpu.VMEM((blocks, flush * cap, width), BF16),
                pltpu.VMEM((blocks, flush * cap, width), BF16),
                pltpu.VMEM((tokens, width), F32),
                pltpu.VMEM((tokens, width), F32),
                pltpu.VMEM((rows, width), BF16),
                pltpu.VMEM((rows, width), BF16),
                pltpu.VMEM((rows, 1), F32),
                pltpu.VMEM((2 * RANK, 2 * FF), BF16),
                pltpu.VMEM((rows, 2 * FF), BF16),
            ],
        ),
        out_shape=[
            near_shape,
            away_shape,
            near_shape,
            away_shape,
            jax.ShapeDtypeStruct((experts, blocks, rows_block), F32),
            jax.ShapeDtypeStruct((experts, 4 * RANK, width), BF16),
        ],
        compiler_params=pltpu.CompilerParams(
            vmem_limit_bytes=62 * 1024 * 1024, dimension_semantics=("arbitrary",)
        ),
        cost_estimate=pl.CostEstimate(
            flops=200_000_000_000 * experts // 20,
            bytes_accessed=5_000_000 * experts,
            transcendentals=rows * FF * experts,
        ),
        name="experts",
    )(chosen, x, x_far, g, g_far, pos, gate, w1, w2, a1, b1, a2, b2)


def unpack_kernel(rows_ref, a1_ref, b1_ref, a2_ref, b2_ref, *, ranks, share):
    records = ranks * share // (4 * RANK)
    for e in range(records):
        unit = []
        for n in range(4):
            at = (4 * e + n) * RANK
            unit.append(rows_ref[at // share, 0, at % share : at % share + RANK, :].astype(F32))
        a1_ref[0, e, 0:RANK, :] = unit[0]
        a1_ref[0, e, RANK:, :] = unit[1]
        b2_ref[0, e] = unit[2]
        b1_ref[0, e, 0] = unit[3][:, :FF]
        b1_ref[0, e, 1] = unit[3][:, FF : 2 * FF]
        a2_ref[0, e] = unit[3][:, 2 * FF :]


def unpack_grads(gathered, experts):
    ranks, adapters, share, width = gathered.shape
    if share % RANK:
        flat = gathered.swapaxes(0, 1).reshape(adapters, experts, 4 * RANK, width).astype(F32)
        last = flat[:, :, 3 * RANK :]
        return (
            flat[:, :, : 2 * RANK],
            jnp.stack([last[..., :FF], last[..., FF : 2 * FF]], axis=2),
            last[..., 2 * FF :],
            flat[:, :, 2 * RANK : 3 * RANK],
        )
    together = 1
    while together * share % (4 * RANK):
        together += 1
    held = together * share // (4 * RANK)
    return pl.pallas_call(
        functools.partial(unpack_kernel, ranks=together, share=share),
        grid=(adapters, ranks // together),
        in_specs=[pl.BlockSpec((together, 1, share, width), lambda a, i: (i, a, 0, 0))],
        out_specs=[
            pl.BlockSpec((1, held, 2 * RANK, width), lambda a, i: (a, i, 0, 0)),
            pl.BlockSpec((1, held, 2, RANK, FF), lambda a, i: (a, i, 0, 0, 0)),
            pl.BlockSpec((1, held, RANK, FF), lambda a, i: (a, i, 0, 0)),
            pl.BlockSpec((1, held, RANK, width), lambda a, i: (a, i, 0, 0)),
        ],
        out_shape=[
            jax.ShapeDtypeStruct((adapters, experts, 2 * RANK, width), F32),
            jax.ShapeDtypeStruct((adapters, experts, 2, RANK, FF), F32),
            jax.ShapeDtypeStruct((adapters, experts, RANK, FF), F32),
            jax.ShapeDtypeStruct((adapters, experts, RANK, width), F32),
        ],
        compiler_params=pltpu.CompilerParams(
            vmem_limit_bytes=40 * 1024 * 1024, dimension_semantics=("arbitrary", "arbitrary")
        ),
        cost_estimate=pl.CostEstimate(flops=0, bytes_accessed=50_000_000, transcendentals=0),
        name="unpack",
    )(gathered)


def swap_pairs(size):
    return [(i, i ^ 1) for i in range(size)]


def from_others(piece):
    groups = lax.axis_size("grp")
    if groups == 2:
        return lax.ppermute(piece, "grp", swap_pairs(2))
    rows = piece.shape[0]
    every = lax.all_gather(piece, "grp", axis=0, tiled=True)
    return jnp.roll(every, -lax.axis_index("grp") * rows, axis=0)[rows:]


def to_owners(near, far):
    groups = lax.axis_size("grp")
    if groups == 2:
        return near.astype(F32) + lax.ppermute(far, "grp", swap_pairs(2)).astype(F32)
    every = jnp.roll(jnp.concatenate([near, far], axis=0), lax.axis_index("grp") * near.shape[0], axis=0)
    return lax.psum_scatter(every, "grp", scatter_dimension=0, tiled=True).astype(F32)


def in_order(near, far):
    if lax.axis_size("grp") != 2:
        return jnp.roll(jnp.concatenate([near, far], axis=0), lax.axis_index("grp") * near.shape[0], axis=0)
    ahead = lax.axis_index("grp") == 0
    return jnp.where(ahead, jnp.concatenate([near, far], axis=0), jnp.concatenate([far, near], axis=0))


def gather_rows(half):
    if lax.axis_size("grp") != 2:
        return lax.all_gather(half, "grp", axis=0, tiled=True)
    rows = half.shape[0] // 2
    core = lax.axis_index("rep") % 2
    got = lax.ppermute(lax.dynamic_slice_in_dim(half, core * rows, rows, 0), "grp", swap_pairs(2))
    other = lax.ppermute(got, "rep", swap_pairs(lax.axis_size("rep")))
    ahead = core == 0
    far = jnp.where(ahead, jnp.concatenate([got, other], 0), jnp.concatenate([other, got], 0))
    return in_order(half, far)


def gather_rows_wide(half):
    reps = lax.axis_size("rep")
    if lax.axis_size("grp") != 2 or half.shape[0] % (reps * 16):
        return lax.all_gather(half, "grp", axis=0, tiled=True)
    rows = half.shape[0] // reps
    mine = lax.dynamic_slice_in_dim(half, lax.axis_index("rep") * rows, rows, 0)
    got = lax.ppermute(mine, "grp", swap_pairs(2))
    return in_order(half, lax.all_gather(got, "rep", axis=0, tiled=True))


def pack(pieces, multiple):
    flat = jnp.concatenate([piece.reshape(-1) for piece in pieces])
    return jnp.pad(flat, (0, -flat.shape[0] % multiple))


def unpack(flat, shapes):
    out = []
    offset = 0
    for shape in shapes:
        size = 1
        for extent in shape:
            size *= extent
        out.append(flat[..., offset : offset + size].reshape(flat.shape[:-1] + shape))
        offset += size
    return out


def local(
    tokens,
    cotangent,
    routes,
    padding,
    parents,
    adapter_ids,
    w_query,
    w_keyval,
    w_output,
    w_router,
    gain_attn,
    gain_ffn,
    w_gateup,
    w_down,
    a_qkv,
    b_query,
    b_keyval,
    a_output,
    b_output,
    a_router,
    b_router,
    a_gateup,
    b_gateup,
    a_down,
    b_down,
):
    groups = lax.axis_size("grp")
    reps = lax.axis_size("rep")
    member = lax.axis_index("grp")
    count = tokens.shape[0]
    width = tokens.shape[1]
    part = width // groups
    tree_length = count * groups
    experts_dev = w_gateup.shape[0]
    experts = experts_dev * groups
    capacity = count * TOPK * 7 // (experts * 5)
    cap = -(-capacity // 16) * 16
    kv_width = KEY_VALUE_HEADS * HEAD_SIZE
    chosen = adapter_ids[0]
    first = member * count
    adapters = a_qkv.shape[0]

    shapes = (
        (3 * RANK, part),
        (RANK, part),
        (2, RANK, kv_width // groups),
        (RANK, part),
        (RANK, part),
        (RANK, part),
        (RANK, experts_dev),
        (experts, part),
        (part,),
        (part,),
        (count,),
    )
    small = pack(
        (
            a_qkv[chosen].T,
            b_query[chosen],
            b_keyval[chosen],
            a_output[chosen].T,
            b_output[chosen],
            a_router[chosen].T,
            b_router[chosen],
            w_router.T,
            gain_attn,
            gain_ffn,
            padding.astype(BF16),
        ),
        1024,
    )
    small_all = in_order(small[None], from_others(small[None]))

    def join(piece):
        return jnp.moveaxis(piece, 0, -2).reshape(piece.shape[1:-1] + (-1,))

    (
        qkv_in,
        query_out,
        keyval_out,
        output_in,
        output_out,
        router_in,
        router_out,
        router_full,
        attn_gain,
        ffn_gain,
        pad_all,
    ) = [join(piece) for piece in unpack(small_all, shapes)]
    attn_gain = attn_gain.astype(F32)
    ffn_gain = ffn_gain.astype(F32)
    keyval_full = gather_rows(w_keyval)
    query_full = gather_rows_wide(w_query)
    output_full = gather_rows_wide(w_output)
    routes_far = from_others(routes)
    ids_all = lax.all_gather(adapter_ids, "rep", axis=0, tiled=True)

    tokens_f = tokens.astype(F32)
    normed = rms_norm(tokens_f, attn_gain).astype(BF16)
    low_rank = product_back(normed, qkv_in).astype(BF16)
    keyvals = product(normed, keyval_full)
    keyvals = jnp.concatenate(
        [
            keyvals[:, :kv_width] + product(low_rank[:, RANK : 2 * RANK], keyval_out[0]),
            keyvals[:, kv_width:] + product(low_rank[:, 2 * RANK :], keyval_out[1]),
        ],
        axis=1,
    ).astype(BF16)
    keyvals_far = from_others(keyvals)
    cotangent_late, keyvals_far = lax.optimization_barrier((cotangent, keyvals_far))
    upstream_far = from_others(cotangent_late)
    query_rows = (product(normed, query_full) + product(low_rank[:, :RANK], query_out)).astype(BF16)
    pad_whole = jnp.roll(pad_all, -first)
    listing, steps, own_bias, live = visits(parents[0], pad_whole[:count], pad_whole[count:], first)
    attended, logs = run_attention(listing, steps, query_rows, keyvals, keyvals_far, own_bias, live)
    out_rank = product_back(attended, output_in).astype(BF16)
    middle = tokens_f + product(attended, output_full) + product(out_rank, output_out)
    normed_ffn = rms_norm(middle, ffn_gain).astype(BF16)
    router_rank = product_back(normed_ffn, router_in).astype(BF16)
    logits = product_back(normed_ffn, router_full) + product(router_rank, router_out)

    labels = jnp.arange(experts, dtype=jnp.int32)
    named = jnp.any(routes[:, :, None] == labels, axis=1)
    best = jnp.max(jnp.where(named, logits, -jnp.inf), axis=1, keepdims=True)
    powers = jnp.where(named, jnp.exp(jnp.where(named, logits, best) - best), 0.0)
    gates = powers / jnp.sum(powers, axis=1, keepdims=True)

    mine = member * experts_dev + jnp.arange(experts_dev, dtype=jnp.int32)
    routes_all = jnp.concatenate([routes, routes_far], axis=0).reshape(groups, count, TOPK)
    hits = jnp.any(routes_all[:, :, :, None] == mine, axis=2)
    before = (jnp.arange(count)[:, None] > jnp.arange(count)[None, :]).astype(BF16)
    ranks = jnp.einsum("ts,gse->get", before, hits.astype(BF16), preferred_element_type=F32)
    places = jnp.where(hits.transpose(0, 2, 1), ranks.astype(jnp.int32), -1).transpose(1, 0, 2)

    rows_far = from_others(normed_ffn)
    gates_t = gates.T
    if groups == 2:
        gates_near = lax.dynamic_slice_in_dim(gates_t, member * experts_dev, experts_dev, 0)
        gates_far = from_others(lax.dynamic_slice_in_dim(gates_t, (1 - member) * experts_dev, experts_dev, 0))
        gates_mine = jnp.stack([gates_near, gates_far], axis=1)
    else:
        gates_mine = lax.all_gather(gates_t, "grp", axis=0)
        gates_mine = lax.dynamic_slice_in_dim(gates_mine, member * experts_dev, experts_dev, 1)
        gates_mine = jnp.roll(gates_mine, -member, axis=0).transpose(1, 0, 2)
    result_near, result_far, d_near, d_far, part_gates, expert_grads = run_experts(
        adapter_ids,
        normed_ffn,
        rows_far,
        cotangent,
        upstream_far,
        places,
        gates_mine,
        w_gateup,
        w_down,
        a_gateup.swapaxes(2, 3),
        b_gateup,
        a_down.swapaxes(2, 3),
        b_down,
        cap,
    )

    owner_hot = (jnp.arange(adapters, dtype=jnp.int32)[:, None] == ids_all[None, :]).astype(F32)
    share = experts_dev * 4 * RANK // reps
    swapped = lax.all_to_all(
        expert_grads.reshape(reps, share, width), "rep", split_axis=0, concat_axis=0, tiled=True
    )
    summed = jnp.sum(owner_hot[:, :, None, None] * swapped.astype(F32)[None], axis=1).astype(BF16)
    spread = lax.all_gather(summed, "rep", axis=0)
    grad_a_gateup, grad_b_gateup, grad_a_down, grad_b_down = unpack_grads(spread, experts_dev)

    if groups == 2:
        d_gates = in_order(part_gates[:, 0], from_others(part_gates[:, 1]))
    else:
        d_gates = jnp.roll(part_gates, member, axis=1)
        d_gates = lax.all_to_all(d_gates, "grp", split_axis=1, concat_axis=0, tiled=True)
    d_gates = d_gates.reshape(experts, count).T
    d_sum = to_owners(d_near, d_far)
    result_far, d_sum = lax.optimization_barrier((result_far, d_sum))
    result = (middle + to_owners(result_near, result_far)).astype(BF16)
    upstream = cotangent.astype(F32)
    d_logits = (gates * (d_gates - jnp.sum(gates * d_gates, axis=1, keepdims=True))).astype(BF16)

    d_router_rank = product_back(d_logits, router_out).astype(BF16)
    d_normed_ffn = d_sum + product(d_logits, router_full) + product(d_router_rank, router_in)
    grad_router_out = product_outer(router_rank, d_logits)
    grad_router_in = product_outer(d_router_rank, normed_ffn)
    d_middle = upstream + rms_back(middle, ffn_gain, d_normed_ffn)
    d_attn = d_middle.astype(BF16)
    d_out_rank = product_back(d_attn, output_out).astype(BF16)
    attended_gradient = (product_back(d_attn, output_full) + product(d_out_rank, output_in)).astype(BF16)
    grad_output_out = product_outer(out_rank, d_attn)
    grad_output_in = product_outer(d_out_rank, attended)
    d_queries, d_keys, d_values, d_keys_far, d_values_far = run_attention_back(
        listing, steps, query_rows, keyvals, keyvals_far, own_bias, live, attended, attended_gradient, logs
    )
    d_keys = to_owners(d_keys, d_keys_far).astype(BF16)
    d_values = to_owners(d_values, d_values_far).astype(BF16)
    d_keyvals = jnp.concatenate([d_keys, d_values], axis=1)
    d_rank_qkv = jnp.concatenate(
        [
            product_back(d_queries, query_out),
            product_back(d_keys, keyval_out[0]),
            product_back(d_values, keyval_out[1]),
        ],
        axis=-1,
    ).astype(BF16)
    d_normed = (
        product_back(d_queries, query_full)
        + product_back(d_keyvals, keyval_full)
        + product(d_rank_qkv, qkv_in)
    )
    grad_input = (d_middle + rms_back(tokens_f, attn_gain, d_normed)).astype(BF16)
    grad_qkv_in = product_outer(d_rank_qkv, normed)
    grad_query_out = product_outer(low_rank[:, :RANK], d_queries)
    grad_keyval_out = jnp.stack(
        [
            product_outer(low_rank[:, RANK : 2 * RANK], d_keys),
            product_outer(low_rank[:, 2 * RANK :], d_values),
        ],
        axis=0,
    )

    def split(gradient):
        return jnp.moveaxis(
            gradient.astype(BF16).reshape(gradient.shape[:-1] + (groups, -1)), -2, 0
        ).reshape(groups, -1)

    dense = jnp.concatenate(
        [
            split(piece)
            for piece in (
                grad_qkv_in,
                grad_query_out,
                grad_keyval_out,
                grad_output_in,
                grad_output_out,
                grad_router_in,
                grad_router_out,
            )
        ],
        axis=1,
    )
    dense = jnp.pad(dense, ((0, 0), (0, -dense.shape[1] % (reps * 128))))
    dense = dense.reshape(groups, reps, -1).swapaxes(0, 1).reshape(reps * groups, -1)
    dense = lax.all_to_all(dense, ("rep", "grp"), split_axis=0, concat_axis=0, tiled=True)
    dense = jnp.sum(dense.reshape(reps, groups, -1).astype(F32), axis=1)
    dense = jnp.sum(owner_hot[:, :, None] * dense[None], axis=1).astype(BF16)
    dense = lax.all_gather(dense, "rep", axis=1).reshape(adapters, -1)
    owned = [piece.astype(F32) for piece in unpack(dense, shapes[:7])]
    return (
        result,
        grad_input,
        owned[0].swapaxes(1, 2),
        owned[1],
        owned[2],
        owned[3].swapaxes(1, 2),
        owned[4],
        owned[5].swapaxes(1, 2),
        owned[6],
        grad_a_gateup.swapaxes(2, 3),
        grad_b_gateup,
        grad_a_down.swapaxes(2, 3),
        grad_b_down,
    )


def solution(mesh):
    in_specs = (
        P(("rep", "grp"), None),
        P(("rep", "grp"), None),
        P(("rep", "grp"), None),
        P(("rep", "grp")),
        P("rep", None),
        P("rep"),
        P("grp", None),
        P("grp", None),
        P("grp", None),
        P("grp", None),
        P("grp"),
        P("grp"),
        P("grp", None, None),
        P("grp", None, None),
        P(None, "grp", None),
        P(None, None, "grp"),
        P(None, None, None, "grp"),
        P(None, "grp", None),
        P(None, None, "grp"),
        P(None, "grp", None),
        P(None, None, "grp"),
        P(None, "grp", None, None),
        P(None, "grp", None, None, None),
        P(None, "grp", None, None),
        P(None, "grp", None, None),
    )
    out_specs = (
        P(("rep", "grp"), None),
        P(("rep", "grp"), None),
        P(None, "grp", None),
        P(None, None, "grp"),
        P(None, None, None, "grp"),
        P(None, "grp", None),
        P(None, None, "grp"),
        P(None, "grp", None),
        P(None, None, "grp"),
        P(None, "grp", None, None),
        P(None, "grp", None, None, None),
        P(None, "grp", None, None),
        P(None, "grp", None, None),
    )
    return jax.shard_map(local, mesh=mesh, in_specs=in_specs, out_specs=out_specs, check_vma=False)
```

```python
import functools

import jax
import jax.numpy as jnp
from jax import lax
from jax.experimental import pallas as pl
from jax.experimental.pallas import tpu as pltpu
from jax.sharding import PartitionSpec as P

QUERY_HEADS = 24
KEY_VALUE_HEADS = 8
HEAD_SIZE = 64
FF = 512
TOPK = 8
RANK = 16
SEG = 128
FLUSH = 5
UNIT = 768

EPSILON = 1e-05
BF16 = jnp.bfloat16
F32 = jnp.float32


def product(left, right):
    return jnp.dot(left, right, preferred_element_type=F32)


def product_back(left, right):
    return lax.dot_general(left, right, (((1,), (1,)), ((), ())), preferred_element_type=F32)


def product_outer(left, right):
    return lax.dot_general(left, right, (((0,), (0,)), ((), ())), preferred_element_type=F32)


def rms_norm(value_rows, gain):
    return (
        value_rows
        * lax.rsqrt(jnp.mean(value_rows * value_rows, axis=-1, keepdims=True) + EPSILON)
        * gain
    )


def rms_back(value_rows, gain, upstream):
    factor = lax.rsqrt(jnp.mean(value_rows * value_rows, axis=-1, keepdims=True) + EPSILON)
    scaled = value_rows * factor
    incoming = upstream * gain
    return factor * (incoming - scaled * jnp.mean(incoming * scaled, axis=-1, keepdims=True))


def ancestry(parent_row):
    total = parent_row.shape[0]
    labels = jnp.arange(total, dtype=jnp.int32)

    def climb(count, state):
        current, table = state
        current = jnp.sum(
            jnp.where(current[:, None] == labels[None, :], parent_row[None, :], 0), axis=1
        )
        table = jnp.maximum(table, (current[:, None] == labels[None, :]).astype(jnp.int32))
        return (current, table)

    start_index = (labels[:, None] == labels[None, :]).astype(jnp.int32)
    return lax.fori_loop(0, total, climb, (labels, start_index))[1]


def tile_parts(ref_k, seg_a, seg_b):
    return jnp.concatenate(
        [
            ref_k[pl.ds(pl.multiple_of(seg_a * SEG, SEG), SEG), :],
            ref_k[pl.ds(pl.multiple_of(seg_b * SEG, SEG), SEG), :],
        ],
        axis=0,
    )


def fill_doubled(held, near_ref, far_ref, ones=False):
    near = near_ref.shape[0]
    for ref, at in ((near_ref, 0), (far_ref, near)):
        rows = ref[...].astype(F32)
        low = lax.broadcasted_iota(jnp.int32, rows.shape, 1) < HEAD_SIZE
        turned = pltpu.roll(rows, HEAD_SIZE, axis=1)
        there = pl.ds(at, rows.shape[0])
        held[0, there, :] = jnp.where(low, rows, 1.0 if ones else turned).astype(BF16)
        held[1, there, :] = jnp.where(low, turned, 1.0 if ones else rows).astype(BF16)


PLACES = (((0, 0), (0, 1), (1, 0)), ((1, 1), (2, 0), (2, 1)))


def stacked_heads(ref, at, which, scale=None):
    low = lax.broadcasted_iota(jnp.int32, (SEG, 2 * HEAD_SIZE), 1) < HEAD_SIZE
    out = []
    for column, half in PLACES[which]:
        piece = ref[at, column * 2 * HEAD_SIZE : (column + 1) * 2 * HEAD_SIZE].astype(F32)
        if scale is not None:
            piece = piece * scale
        out.append(jnp.where(low if half == 0 else jnp.logical_not(low), piece, 0.0))
    return jnp.concatenate(out, axis=0)


def unstack(first, second):
    low = lax.broadcasted_iota(jnp.int32, (SEG, 2 * HEAD_SIZE), 1) < HEAD_SIZE
    return [
        jnp.where(low, first[0:SEG], first[SEG : 2 * SEG]),
        jnp.where(low, first[2 * SEG :], second[0:SEG]),
        jnp.where(low, second[SEG : 2 * SEG], second[2 * SEG :]),
    ]


def first_bias(own_ref, live_ref, i, seg_b):
    other = jnp.broadcast_to(live_ref[seg_b], (SEG, SEG))
    tile = jnp.concatenate([own_ref[i], other], axis=1)
    return jnp.concatenate([tile] * 3, axis=0)


def next_bias(live_ref, seg_a, seg_b):
    return jnp.concatenate([live_ref[seg_a], live_ref[seg_b]], axis=1)


def attend_kernel(
    list_ref,
    steps_ref,
    q_ref,
    k_ref,
    v_ref,
    k_far,
    v_far,
    own_ref,
    live_ref,
    o_ref,
    l_ref,
    kf,
    vf,
    *,
    here,
    segs,
    scale,
):
    fill_doubled(kf, k_ref, k_far)
    fill_doubled(vf, v_ref, v_far, ones=True)
    lanes = lax.broadcasted_iota(jnp.int32, (SEG, 2 * HEAD_SIZE), 1)
    low = lanes < HEAD_SIZE
    slots = 2 * segs
    for i in range(here):
        at = pl.ds(i * SEG, SEG)
        queries = [stacked_heads(q_ref, at, which, scale).astype(BF16) for which in range(2)]

        def pair_of(t):
            return (
                lax.rem(list_ref[i * slots + 2 * t], segs),
                lax.rem(list_ref[i * slots + 2 * t + 1], segs),
            )

        seg_a, seg_b = pair_of(0)
        bias = first_bias(own_ref, live_ref, i, list_ref[i * slots + 1])
        state = []
        for which in range(2):
            s = product_back(queries[which], tile_parts(kf.at[which], seg_a, seg_b)) + bias
            top = jnp.max(s, axis=1, keepdims=True)
            p = jnp.exp(s - top).astype(BF16)
            state.append((top, product(p, tile_parts(vf.at[which], seg_a, seg_b))))

        def body(t, state):
            bias = next_bias(live_ref, list_ref[i * slots + 2 * t], list_ref[i * slots + 2 * t + 1])
            seg_a, seg_b = pair_of(t)
            out = []
            for which in range(2):
                top, acc = state[which]
                s = product_back(queries[which], tile_parts(kf.at[which], seg_a, seg_b)) + bias
                higher = jnp.maximum(top, jnp.max(s, axis=1, keepdims=True))
                p = jnp.exp(s - higher).astype(BF16)
                acc = acc * jnp.exp(top - higher) + product(p, tile_parts(vf.at[which], seg_a, seg_b))
                out.append((higher, acc))
            return tuple(out)

        state = lax.fori_loop(1, steps_ref[i], body, tuple(state))
        turned = [pltpu.roll(acc, HEAD_SIZE, axis=1) for _, acc in state]
        logs = jnp.zeros((SEG, 2 * HEAD_SIZE), F32)
        heads = []
        for which in range(2):
            for n, (_, half) in enumerate(PLACES[which]):
                rows = slice(n * SEG, (n + 1) * SEG)
                plain, other = state[which][1][rows], turned[which][rows]
                heads.append(plain / other if half == 0 else other / plain)
                total = jnp.where(low, other, plain)
                logs = jnp.where(lanes == which * 3 + n, state[which][0][rows] + jnp.log(total), logs)
        l_ref[0, at, :] = logs
        for column in range(3):
            o_ref[at, column * 2 * HEAD_SIZE : (column + 1) * 2 * HEAD_SIZE] = jnp.where(
                low, heads[2 * column], heads[2 * column + 1]
            ).astype(BF16)


def attend_back_kernel(
    list_ref,
    steps_ref,
    q_ref,
    k_ref,
    v_ref,
    k_far,
    v_far,
    own_ref,
    live_ref,
    o_ref,
    do_ref,
    l_ref,
    *refs,
    here,
    segs,
    scale,
    after,
):
    dq_ref, dk_ref, dv_ref, dk_far, dv_far, kf, vf, dkf, dvf = refs[after:]
    fill_doubled(kf, k_ref, k_far)
    fill_doubled(vf, v_ref, v_far)
    dkf[...] = jnp.zeros_like(dkf)
    dvf[...] = jnp.zeros_like(dvf)
    slots = 2 * segs
    for i in range(here):
        at = pl.ds(i * SEG, SEG)
        fixed = []
        for which in range(2):
            d_o = stacked_heads(do_ref, at, which)
            fixed.append(
                (
                    stacked_heads(q_ref, at, which, scale).astype(BF16),
                    d_o.astype(BF16),
                    jnp.sum(d_o * stacked_heads(o_ref, at, which), axis=1, keepdims=True),
                    jnp.concatenate(
                        [l_ref[0, at, which * 3 + n : which * 3 + n + 1] for n in range(3)], axis=0
                    ),
                )
            )

        def step(t, bias):
            seg_a = lax.rem(list_ref[i * slots + 2 * t], segs)
            seg_b = lax.rem(list_ref[i * slots + 2 * t + 1], segs)
            out = []
            for which, (q, d_o, delta, log_total) in enumerate(fixed):
                k = tile_parts(kf.at[which], seg_a, seg_b)
                v = tile_parts(vf.at[which], seg_a, seg_b)
                p = jnp.exp(product_back(q, k) + bias - log_total)
                d_p = product_back(d_o, v)
                d_s = (p * (d_p - delta)).astype(BF16)
                d_v = product_outer(p.astype(BF16), d_o)
                d_k = product_outer(d_s, q)
                for n, seg in enumerate((seg_a, seg_b)):
                    rows = pl.ds(pl.multiple_of(seg * SEG, SEG), SEG)
                    dkf[which, rows, :] += d_k[n * SEG : (n + 1) * SEG]
                    dvf[which, rows, :] += d_v[n * SEG : (n + 1) * SEG]
                out.append(product(d_s, k))
            return tuple(out)

        d_q = step(0, first_bias(own_ref, live_ref, i, list_ref[i * slots + 1]))

        def body(t, carry):
            bias = next_bias(live_ref, list_ref[i * slots + 2 * t], list_ref[i * slots + 2 * t + 1])
            return tuple(a + b for a, b in zip(carry, step(t, bias)))

        d_q = lax.fori_loop(1, steps_ref[i], body, d_q)
        for column, piece in enumerate(unstack(*d_q)):
            dq_ref[at, column * 2 * HEAD_SIZE : (column + 1) * 2 * HEAD_SIZE] = (piece * scale).astype(BF16)
    near = dk_ref.shape[0]
    for out, far_out, held in ((dk_ref, dk_far, dkf), (dv_ref, dv_far, dvf)):
        first = held[0] + pltpu.roll(held[0], HEAD_SIZE, axis=1)
        second = held[1] + pltpu.roll(held[1], HEAD_SIZE, axis=1)
        low = lax.broadcasted_iota(jnp.int32, first.shape, 1) < HEAD_SIZE
        total = jnp.where(low, first, second).astype(BF16)
        out[...] = total[:near]
        far_out[...] = total[near:]


def visits(parent_row, pad_near, pad_far, first):
    count = pad_near.shape[0]
    tree_length = count + pad_far.shape[0]
    segs = tree_length // SEG
    here = count // SEG
    own = jnp.arange(here, dtype=jnp.int32)
    labels = jnp.arange(segs, dtype=jnp.int32)
    table = lax.dynamic_slice_in_dim(ancestry(parent_row), first // SEG, here, 0)
    turn = (labels[:, None] == (labels[None, :] + segs - first // SEG) % segs).astype(F32)
    table = product_back(table.astype(F32), turn).astype(jnp.int32)
    table = jnp.where(labels[None, :] == own[:, None], 0, table)
    order = jnp.sum(jnp.where(labels[None, :] <= labels[:, None], table[:, None, :], 0), axis=2)
    spots = jnp.arange(1, 2 * segs, dtype=jnp.int32)
    found = jnp.logical_and(table[:, None, :] > 0, order[:, None, :] == spots[None, :, None])
    listing = jnp.where(jnp.any(found, axis=2), jnp.sum(found * labels, axis=2), segs)
    listing = jnp.concatenate([own[:, None], listing], axis=1).astype(jnp.int32)
    steps = (2 + order[:, -1]) // 2
    live = jnp.where(jnp.concatenate([pad_near, pad_far]) > 0, 0.0, -1e30).astype(F32).reshape(segs, SEG)
    places = jnp.arange(SEG)
    causal = places[None, :] <= places[:, None]
    same = places[None, :] == places[:, None]
    own_bias = jnp.where(same[None], 0.0, jnp.where(causal[None], live[:here, None, :], -1e30))
    live = jnp.concatenate([live, jnp.full((1, SEG), -1e30, F32)], axis=0)[:, None, :]
    return listing.reshape(-1), steps.astype(jnp.int32), own_bias, live


def attention_specs(count, far, here, segs, skip=0):
    narrow = 2 * HEAD_SIZE
    shift = KEY_VALUE_HEADS // 2 + skip
    return [
        pl.BlockSpec((count, 3 * narrow), lambda h, a, b: (0, h + skip)),
        pl.BlockSpec((count, narrow), lambda h, a, b: (0, h + skip)),
        pl.BlockSpec((count, narrow), lambda h, a, b: (0, h + shift)),
        pl.BlockSpec((far, narrow), lambda h, a, b: (0, h + skip)),
        pl.BlockSpec((far, narrow), lambda h, a, b: (0, h + shift)),
        pl.BlockSpec((here, SEG, SEG), lambda h, a, b: (0, 0, 0)),
        pl.BlockSpec((segs + 1, 1, SEG), lambda h, a, b: (0, 0, 0)),
    ]


def run_attention(listing, steps, queries, near, far, own_bias, live):
    count, width = queries.shape
    tree_length = count + far.shape[0]
    here, segs = count // SEG, tree_length // SEG
    pairs = KEY_VALUE_HEADS // 2
    narrow = 2 * HEAD_SIZE
    return pl.pallas_call(
        functools.partial(attend_kernel, here=here, segs=segs, scale=HEAD_SIZE ** (-0.5)),
        grid_spec=pltpu.PrefetchScalarGridSpec(
            num_scalar_prefetch=2,
            grid=(pairs,),
            in_specs=attention_specs(count, far.shape[0], here, segs),
            out_specs=[
                pl.BlockSpec((count, 3 * narrow), lambda h, a, b: (0, h)),
                pl.BlockSpec((1, count, narrow), lambda h, a, b: (h, 0, 0)),
            ],
            scratch_shapes=[pltpu.VMEM((2, tree_length, narrow), BF16)] * 2,
        ),
        out_shape=[
            jax.ShapeDtypeStruct((count, width), BF16),
            jax.ShapeDtypeStruct((pairs, count, narrow), F32),
        ],
        compiler_params=pltpu.CompilerParams(
            vmem_limit_bytes=40 * 1024 * 1024, dimension_semantics=("arbitrary",)
        ),
        cost_estimate=pl.CostEstimate(flops=40_000_000_000, bytes_accessed=8_000_000, transcendentals=10_000_000),
        name="attention",
    )(listing, steps, queries, near, near, far, far, own_bias, live)


def run_attention_back(
    listing, steps, queries, near, far, own_bias, live, attended, gradient, logs, skip, pairs, after=()
):
    count = queries.shape[0]
    tree_length = count + far.shape[0]
    here, segs = count // SEG, tree_length // SEG
    narrow = 2 * HEAD_SIZE
    rows = pl.BlockSpec((count, 3 * narrow), lambda h, a, b: (0, h + skip))
    outs = [pl.BlockSpec((count, narrow), lambda h, a, b: (0, h))] * 2
    outs += [pl.BlockSpec((far.shape[0], narrow), lambda h, a, b: (0, h))] * 2
    return pl.pallas_call(
        functools.partial(
            attend_back_kernel, here=here, segs=segs, scale=HEAD_SIZE ** (-0.5), after=len(after)
        ),
        grid_spec=pltpu.PrefetchScalarGridSpec(
            num_scalar_prefetch=2,
            grid=(pairs,),
            in_specs=attention_specs(count, far.shape[0], here, segs, skip)
            + [rows, rows, pl.BlockSpec((1, count, narrow), lambda h, a, b: (h + skip, 0, 0))]
            + [pl.BlockSpec(memory_space=pl.ANY)] * len(after),
            out_specs=[pl.BlockSpec((count, 3 * narrow), lambda h, a, b: (0, h))] + outs,
            scratch_shapes=[pltpu.VMEM((2, tree_length, narrow), BF16)] * 2
            + [pltpu.VMEM((2, tree_length, narrow), F32)] * 2,
        ),
        out_shape=[jax.ShapeDtypeStruct((count, 3 * pairs * narrow), BF16)]
        + [jax.ShapeDtypeStruct((count, pairs * narrow), BF16)] * 2
        + [jax.ShapeDtypeStruct((far.shape[0], pairs * narrow), BF16)] * 2,
        compiler_params=pltpu.CompilerParams(
            vmem_limit_bytes=40 * 1024 * 1024, dimension_semantics=("arbitrary",)
        ),
        cost_estimate=pl.CostEstimate(
            flops=17_000_000_000 * pairs, bytes_accessed=3_000_000 * pairs, transcendentals=0
        ),
        name="attention_back",
    )(listing, steps, queries, near, near, far, far, own_bias, live, attended, gradient, logs, *after)


def expert_kernel(
    chosen_ref,
    x_ref,
    x_far,
    g_ref,
    g_far,
    pos_ref,
    gate_ref,
    w1_ref,
    w2_ref,
    a1_ref,
    b1_ref,
    a2_ref,
    b2_ref,
    *refs,
    blocks,
    rows_block,
    cap,
    flush,
    carried,
):
    held = refs[:4] if carried else ()
    (
        r_out,
        r_far,
        d_out,
        d_far,
        dg_out,
        grad_out,
        hot_s,
        o_s,
        dx_s,
        accr,
        accd,
        x_s,
        g_s,
        gate_s,
        b1_s,
        dgu_s,
    ) = refs[len(held) :]
    e = pl.program_id(0)
    slot = lax.rem(e, flush)
    width = x_ref.shape[-1]
    halves = width // UNIT

    @pl.when(e == 0)
    def _():
        b1_s[...] = jnp.zeros_like(b1_s)
        if carried:
            for n, acc in enumerate((accr, accd)):
                acc[0:rows_block, :] = held[2 * n][...].astype(F32)
                acc[rows_block:, :] = held[2 * n + 1][...].astype(F32)
        else:
            accr[...] = jnp.zeros_like(accr)
            accd[...] = jnp.zeros_like(accd)

    at = pl.multiple_of(slot * cap, 16)
    for b in range(blocks):
        rows_ref, g_rows_ref = (x_ref, g_ref) if b == 0 else (x_far, g_far)
        here = pl.ds(max(b - 1, 0) * rows_block, rows_block)
        there = pl.ds(b * cap, cap)
        places = lax.broadcasted_iota(jnp.int32, (cap, rows_block), 0)
        hit = places == pos_ref[0, b : b + 1, :]
        hot = hit.astype(F32).astype(BF16)
        hot_s[b, pl.ds(at, cap), :] = hot
        x_s[there, :] = product(hot, rows_ref[here, :]).astype(BF16)
        g_s[there, :] = product(hot, g_rows_ref[here, :]).astype(BF16)
        gate_s[there, :] = jnp.sum(
            jnp.where(hit, gate_ref[0, b : b + 1, :], 0.0), axis=1, keepdims=True
        )
    b1_s[0:RANK, 0:FF] = b1_ref[0, 0, 0]
    b1_s[RANK : 2 * RANK, FF : 2 * FF] = b1_ref[0, 0, 1]

    x = x_s[...]
    gate_col = gate_s[...]
    rank_in = product_back(a1_ref[0, 0], x).astype(BF16)
    pre = product(x, w1_ref[0])
    gate_pre = pre[:, :FF]
    up_pre = pre[:, FF:]
    sig = 1.0 / (1.0 + jnp.exp(-gate_pre))
    act = gate_pre * sig
    hidden = (act * up_pre).astype(BF16)
    rank_down = product_back(a2_ref[0, 0], hidden).astype(BF16)
    out = product(hidden, w2_ref[0]).astype(BF16).astype(F32)
    g = g_s[...].astype(F32)
    d_gate_col = jnp.sum(g * out, axis=1, keepdims=True)
    out = (gate_col * out).astype(BF16)
    d_exp = (gate_col * g).astype(BF16)
    d_rank_down = product_back(b2_ref[0, 0], d_exp).astype(BF16)
    d_hidden = product_back(d_exp, w2_ref[0])
    dgu_s[:, :FF] = (d_hidden * up_pre * sig * (1.0 + gate_pre * (1.0 - sig))).astype(BF16)
    dgu_s[:, FF:] = (d_hidden * act).astype(BF16)
    dgu = dgu_s[...]
    d_rank_in = product_back(b1_s[...], dgu).astype(BF16)
    dx = product_back(dgu, w1_ref[0]).astype(BF16)
    for b in range(blocks):
        o_s[b, pl.ds(at, cap), :] = out[b * cap : (b + 1) * cap]
        dx_s[b, pl.ds(at, cap), :] = dx[b * cap : (b + 1) * cap]
        places = lax.broadcasted_iota(jnp.int32, (cap, rows_block), 0)
        hit = places == pos_ref[0, b : b + 1, :]
        dg_out[0, b : b + 1, :] = jnp.sum(
            jnp.where(hit, d_gate_col[b * cap : (b + 1) * cap], 0.0), axis=0, keepdims=True
        )

    grad_a1 = product(d_rank_in, x)
    grad_b1 = product(rank_in, dgu)
    grad_a2 = product(d_rank_down, hidden)
    grad_b2 = product(rank_down, d_exp)
    last = jnp.concatenate([grad_b1[:RANK, :FF], grad_b1[RANK:, FF:], grad_a2], axis=1)
    for n, piece in enumerate((grad_a1[:RANK], grad_a1[RANK:], grad_b2, last)):
        for half in range(halves):
            rows = slice((n * halves + half) * RANK, (n * halves + half + 1) * RANK)
            grad_out[0, rows, :] = piece[:, half * UNIT : (half + 1) * UNIT].astype(BF16)

    @pl.when(slot == flush - 1)
    def _():
        for b in range(blocks):
            here = pl.ds(b * rows_block, rows_block)
            accr[here, :] += product_outer(hot_s[b], o_s[b])
            accd[here, :] += product_outer(hot_s[b], dx_s[b])

    @pl.when(e == pl.num_programs(0) - 1)
    def _():
        r_out[...] = accr[0:rows_block, :].astype(BF16)
        r_far[...] = accr[rows_block:, :].astype(BF16)
        d_out[...] = accd[0:rows_block, :].astype(BF16)
        d_far[...] = accd[rows_block:, :].astype(BF16)


def run_experts(chosen, x, x_far, g, g_far, pos, gate, w1, w2, a1, b1, a2, b2, held, cap, first, count):
    _, blocks, rows_block = pos.shape
    width = x.shape[1]
    tokens = blocks * rows_block
    rows = blocks * cap
    flush = FLUSH if count % FLUSH == 0 else 1
    record = 4 * RANK * width // UNIT
    lead = lambda e, c: (e, 0, 0)
    shifted = lambda e, c: (e + first, 0, 0)
    near = pl.BlockSpec((rows_block, width), lambda e, c: (0, 0), pipeline_mode=pl.Buffered(1))
    away = pl.BlockSpec((tokens - rows_block, width), lambda e, c: (0, 0), pipeline_mode=pl.Buffered(1))
    near_shape = jax.ShapeDtypeStruct((rows_block, width), BF16)
    away_shape = jax.ShapeDtypeStruct((tokens - rows_block, width), BF16)
    return pl.pallas_call(
        functools.partial(
            expert_kernel,
            blocks=blocks,
            rows_block=rows_block,
            cap=cap,
            flush=flush,
            carried=bool(held),
        ),
        grid_spec=pltpu.PrefetchScalarGridSpec(
            num_scalar_prefetch=1,
            grid=(count,),
            in_specs=[
                near,
                away,
                near,
                away,
                pl.BlockSpec((1, blocks, rows_block), shifted),
                pl.BlockSpec((1, blocks, rows_block), shifted),
                pl.BlockSpec((1, width, 2 * FF), lead),
                pl.BlockSpec((1, FF, width), lead),
                pl.BlockSpec((1, 1, 2 * RANK, width), lambda e, c: (c[0], e + first, 0, 0)),
                pl.BlockSpec((1, 1, 2, RANK, FF), lambda e, c: (c[0], e + first, 0, 0, 0)),
                pl.BlockSpec((1, 1, RANK, FF), lambda e, c: (c[0], e + first, 0, 0)),
                pl.BlockSpec((1, 1, RANK, width), lambda e, c: (c[0], e + first, 0, 0)),
            ]
            + ([near, away, near, away] if held else []),
            out_specs=[
                near,
                away,
                near,
                away,
                pl.BlockSpec((1, blocks, rows_block), lead),
                pl.BlockSpec((1, record, UNIT), lead),
            ],
            scratch_shapes=[
                pltpu.VMEM((blocks, flush * cap, rows_block), BF16),
                pltpu.VMEM((blocks, flush * cap, width), BF16),
                pltpu.VMEM((blocks, flush * cap, width), BF16),
                pltpu.VMEM((tokens, width), F32),
                pltpu.VMEM((tokens, width), F32),
                pltpu.VMEM((rows, width), BF16),
                pltpu.VMEM((rows, width), BF16),
                pltpu.VMEM((rows, 1), F32),
                pltpu.VMEM((2 * RANK, 2 * FF), BF16),
                pltpu.VMEM((rows, 2 * FF), BF16),
            ],
        ),
        out_shape=[
            near_shape,
            away_shape,
            near_shape,
            away_shape,
            jax.ShapeDtypeStruct((count, blocks, rows_block), F32),
            jax.ShapeDtypeStruct((count, record, UNIT), BF16),
        ],
        compiler_params=pltpu.CompilerParams(
            vmem_limit_bytes=63 * 1024 * 1024, dimension_semantics=("arbitrary",)
        ),
        cost_estimate=pl.CostEstimate(
            flops=8_000_000_000 * count,
            bytes_accessed=5_000_000 * count,
            transcendentals=rows * FF * count,
        ),
        name="experts",
    )(chosen, x, x_far, g, g_far, pos, gate, w1, w2, a1, b1, a2, b2, *held)


def fold_kernel(chosen_ref, w1_ref, w2_ref, a1_ref, b1_ref, a2_ref, b2_ref, *refs):
    o1_ref, o2_ref = refs[-2:]
    for n in range(2):
        at = slice(n * FF, (n + 1) * FF)
        a1 = a1_ref[0, 0, n * RANK : (n + 1) * RANK, :]
        o1_ref[0, :, at] = (w1_ref[0, :, at].astype(F32) + product_outer(a1, b1_ref[0, 0, n])).astype(BF16)
    o2_ref[0] = (w2_ref[0].astype(F32) + product_outer(a2_ref[0, 0], b2_ref[0, 0])).astype(BF16)


def fold_adapters(chosen, w1, w2, a1, b1, a2, b2, first, count, held=(), skip=0, size=None, after=()):
    size = size or count
    placed = lambda e, c: (e + skip, 0, 0)
    _, width, _ = w1.shape
    shifted = lambda e, c: (e + first, 0, 0)
    return pl.pallas_call(
        fold_kernel,
        grid_spec=pltpu.PrefetchScalarGridSpec(
            num_scalar_prefetch=1,
            grid=(count,),
            in_specs=[
                pl.BlockSpec((1, width, 2 * FF), shifted),
                pl.BlockSpec((1, FF, width), shifted),
                pl.BlockSpec((1, 1, 2 * RANK, width), lambda e, c: (c[0], e + first, 0, 0)),
                pl.BlockSpec((1, 1, 2, RANK, FF), lambda e, c: (c[0], e + first, 0, 0, 0)),
                pl.BlockSpec((1, 1, RANK, FF), lambda e, c: (c[0], e + first, 0, 0)),
                pl.BlockSpec((1, 1, RANK, width), lambda e, c: (c[0], e + first, 0, 0)),
            ]
            + [pl.BlockSpec(memory_space=pl.ANY)] * (len(held) + len(after)),
            out_specs=[pl.BlockSpec((1, width, 2 * FF), placed), pl.BlockSpec((1, FF, width), placed)],
        ),
        out_shape=[
            jax.ShapeDtypeStruct((size, width, 2 * FF), BF16),
            jax.ShapeDtypeStruct((size, FF, width), BF16),
        ],
        input_output_aliases={7 + n: n for n in range(len(held))},
        compiler_params=pltpu.CompilerParams(
            vmem_limit_bytes=40 * 1024 * 1024, dimension_semantics=("arbitrary",)
        ),
        cost_estimate=pl.CostEstimate(
            flops=3_000_000_000 * count, bytes_accessed=12_000_000 * count, transcendentals=0
        ),
        name="fold",
    )(chosen, w1, w2, a1, b1, a2, b2, *held, *after)


def total_kernel(ids_ref, rows_ref, *refs):
    out_ref, held = refs[-2:]
    held[...] = jnp.zeros_like(held)
    for n in range(rows_ref.shape[0]):
        held[ids_ref[n]] += rows_ref[n].astype(F32)
    out_ref[...] = held[...].astype(BF16)


def totals(ids, rows, adapters, after=()):
    shape = (adapters,) + rows.shape[1:]
    if rows.shape[1] % 16:
        hot = (jnp.arange(adapters, dtype=jnp.int32)[:, None] == ids[None, :]).astype(F32)
        return jnp.sum(hot[:, :, None, None] * rows.astype(F32)[None], axis=1).astype(BF16)
    return pl.pallas_call(
        total_kernel,
        grid_spec=pltpu.PrefetchScalarGridSpec(
            num_scalar_prefetch=1,
            grid=(1,),
            in_specs=[pl.BlockSpec(rows.shape, lambda i, c: (0, 0, 0))]
            + [pl.BlockSpec(memory_space=pl.ANY)] * len(after),
            out_specs=pl.BlockSpec(shape, lambda i, c: (0, 0, 0)),
            scratch_shapes=[pltpu.VMEM(shape, F32)],
        ),
        out_shape=jax.ShapeDtypeStruct(shape, BF16),
        compiler_params=pltpu.CompilerParams(vmem_limit_bytes=32 * 1024 * 1024),
        cost_estimate=pl.CostEstimate(flops=0, bytes_accessed=5_000_000, transcendentals=0),
        name="totals",
    )(ids, rows, *after)


def add_kernel(first_ref, second_ref, third_ref, *refs):
    total = first_ref[...] + second_ref[...].astype(F32) + third_ref[...].astype(F32)
    refs[-1][...] = total.astype(BF16)


def add_up(first, second, third, after=()):
    return pl.pallas_call(
        add_kernel,
        in_specs=[pl.BlockSpec(memory_space=pltpu.VMEM)] * 3
        + [pl.BlockSpec(memory_space=pl.ANY)] * len(after),
        out_specs=pl.BlockSpec(memory_space=pltpu.VMEM),
        out_shape=jax.ShapeDtypeStruct(first.shape, BF16),
        compiler_params=pltpu.CompilerParams(vmem_limit_bytes=32 * 1024 * 1024),
        name="add_up",
    )(first, second, third, *after)


def unpack_kernel(rows_ref, *refs, share):
    a1_ref, b1_ref, a2_ref, b2_ref = refs[-4:]
    halves = a1_ref.shape[-1] // UNIT
    record = 4 * RANK * halves
    for e in range(rows_ref.shape[0] * share // record):
        unit = []
        for n in range(4 * halves):
            at = e * record + n * RANK
            unit.append(rows_ref[at // share, 0, at % share : at % share + RANK, :].astype(F32))
        for half in range(halves):
            at = slice(half * UNIT, (half + 1) * UNIT)
            a1_ref[0, e, 0:RANK, at] = unit[half]
            a1_ref[0, e, RANK:, at] = unit[halves + half]
            b2_ref[0, e, :, at] = unit[2 * halves + half]
        last = jnp.concatenate(unit[3 * halves :], axis=1)
        b1_ref[0, e, 0] = last[:, :FF]
        b1_ref[0, e, 1] = last[:, FF : 2 * FF]
        a2_ref[0, e] = last[:, 2 * FF :]


def unpack_grads(gathered, experts, first, held, width):
    ranks, adapters, share, _ = gathered.shape
    halves = width // UNIT
    record = 4 * RANK * halves
    if share % 16:
        flat = gathered.swapaxes(0, 1).reshape(adapters, experts, 4, halves, RANK, UNIT)
        flat = flat.swapaxes(3, 4).reshape(adapters, experts, 4 * RANK, width).astype(F32)
        last = flat[:, :, 3 * RANK :]
        return (
            flat[:, :, : 2 * RANK],
            jnp.stack([last[..., :FF], last[..., FF : 2 * FF]], axis=2),
            last[..., 2 * FF :],
            flat[:, :, 2 * RANK : 3 * RANK],
        )
    together = 1
    while together * share % record:
        together += 1
    each = together * share // record
    skip = first // each
    return pl.pallas_call(
        functools.partial(unpack_kernel, share=share),
        grid=(adapters, ranks // together),
        in_specs=[pl.BlockSpec((together, 1, share, UNIT), lambda a, i: (i, a, 0, 0))]
        + [pl.BlockSpec(memory_space=pl.ANY)] * len(held),
        out_specs=[
            pl.BlockSpec((1, each, 2 * RANK, width), lambda a, i: (a, i + skip, 0, 0)),
            pl.BlockSpec((1, each, 2, RANK, FF), lambda a, i: (a, i + skip, 0, 0, 0)),
            pl.BlockSpec((1, each, RANK, FF), lambda a, i: (a, i + skip, 0, 0)),
            pl.BlockSpec((1, each, RANK, width), lambda a, i: (a, i + skip, 0, 0)),
        ],
        out_shape=[
            jax.ShapeDtypeStruct((adapters, experts, 2 * RANK, width), F32),
            jax.ShapeDtypeStruct((adapters, experts, 2, RANK, FF), F32),
            jax.ShapeDtypeStruct((adapters, experts, RANK, FF), F32),
            jax.ShapeDtypeStruct((adapters, experts, RANK, width), F32),
        ],
        input_output_aliases={1 + n: n for n in range(len(held))},
        compiler_params=pltpu.CompilerParams(
            vmem_limit_bytes=40 * 1024 * 1024, dimension_semantics=("arbitrary", "arbitrary")
        ),
        cost_estimate=pl.CostEstimate(flops=0, bytes_accessed=30_000_000, transcendentals=0),
        name="unpack",
    )(gathered, *held)


def swap_pairs(size):
    return [(i, i ^ 1) for i in range(size)]


def from_others(piece):
    groups = lax.axis_size("grp")
    if groups == 2:
        return lax.ppermute(piece, "grp", swap_pairs(2))
    rows = piece.shape[0]
    every = lax.all_gather(piece, "grp", axis=0, tiled=True)
    return jnp.roll(every, -lax.axis_index("grp") * rows, axis=0)[rows:]


def owners_terms(near, far):
    if lax.axis_size("grp") == 2:
        return near, lax.ppermute(far, "grp", swap_pairs(2))
    return to_owners(near, far), jnp.zeros_like(near)


def to_owners(near, far):
    groups = lax.axis_size("grp")
    if groups == 2:
        return near.astype(F32) + lax.ppermute(far, "grp", swap_pairs(2)).astype(F32)
    every = jnp.roll(jnp.concatenate([near, far], axis=0), lax.axis_index("grp") * near.shape[0], axis=0)
    return lax.psum_scatter(every, "grp", scatter_dimension=0, tiled=True).astype(F32)


def in_order(near, far):
    if lax.axis_size("grp") != 2:
        return jnp.roll(jnp.concatenate([near, far], axis=0), lax.axis_index("grp") * near.shape[0], axis=0)
    ahead = lax.axis_index("grp") == 0
    return jnp.where(ahead, jnp.concatenate([near, far], axis=0), jnp.concatenate([far, near], axis=0))


def gather_rows(half):
    if lax.axis_size("grp") != 2:
        return lax.all_gather(half, "grp", axis=0, tiled=True)
    rows = half.shape[0] // 2
    core = lax.axis_index("rep") % 2
    got = lax.ppermute(lax.dynamic_slice_in_dim(half, core * rows, rows, 0), "grp", swap_pairs(2))
    other = lax.ppermute(got, "rep", swap_pairs(lax.axis_size("rep")))
    ahead = core == 0
    far = jnp.where(ahead, jnp.concatenate([got, other], 0), jnp.concatenate([other, got], 0))
    return in_order(half, far)


def gather_rows_wide(half):
    reps = lax.axis_size("rep")
    if lax.axis_size("grp") != 2 or half.shape[0] % (reps * 16):
        return lax.all_gather(half, "grp", axis=0, tiled=True)
    rows = half.shape[0] // reps
    mine = lax.dynamic_slice_in_dim(half, lax.axis_index("rep") * rows, rows, 0)
    got = lax.ppermute(mine, "grp", swap_pairs(2))
    return in_order(half, lax.all_gather(got, "rep", axis=0, tiled=True))


def pack(pieces, multiple):
    flat = jnp.concatenate([piece.reshape(-1) for piece in pieces])
    return jnp.pad(flat, (0, -flat.shape[0] % multiple))


def unpack(flat, shapes):
    out = []
    offset = 0
    for shape in shapes:
        size = 1
        for extent in shape:
            size *= extent
        out.append(flat[..., offset : offset + size].reshape(flat.shape[:-1] + shape))
        offset += size
    return out


def local(
    tokens,
    cotangent,
    routes,
    padding,
    parents,
    adapter_ids,
    w_query,
    w_keyval,
    w_output,
    w_router,
    gain_attn,
    gain_ffn,
    w_gateup,
    w_down,
    a_qkv,
    b_query,
    b_keyval,
    a_output,
    b_output,
    a_router,
    b_router,
    a_gateup,
    b_gateup,
    a_down,
    b_down,
):
    groups = lax.axis_size("grp")
    reps = lax.axis_size("rep")
    member = lax.axis_index("grp")
    count = tokens.shape[0]
    width = tokens.shape[1]
    part = width // groups
    tree_length = count * groups
    experts_dev = w_gateup.shape[0]
    experts = experts_dev * groups
    capacity = count * TOPK * 7 // (experts * 5)
    cap = -(-capacity // 16) * 16
    kv_width = KEY_VALUE_HEADS * HEAD_SIZE
    chosen = adapter_ids[0]
    first = member * count
    adapters = a_qkv.shape[0]

    shapes = (
        (3 * RANK, part),
        (RANK, part),
        (2, RANK, kv_width // groups),
        (RANK, part),
        (RANK, part),
        (RANK, part),
        (RANK, experts_dev),
        (experts, part),
        (part,),
        (part,),
        (count,),
    )
    small = pack(
        (
            a_qkv[chosen].T,
            b_query[chosen],
            b_keyval[chosen],
            a_output[chosen].T,
            b_output[chosen],
            a_router[chosen].T,
            b_router[chosen],
            w_router.T,
            gain_attn,
            gain_ffn,
            padding.astype(BF16),
        ),
        1024,
    )
    small_all = in_order(small[None], from_others(small[None]))

    def join(piece):
        return jnp.moveaxis(piece, 0, -2).reshape(piece.shape[1:-1] + (-1,))

    (
        qkv_in,
        query_out,
        keyval_out,
        output_in,
        output_out,
        router_in,
        router_out,
        router_full,
        attn_gain,
        ffn_gain,
        pad_all,
    ) = [join(piece) for piece in unpack(small_all, shapes)]
    attn_gain = attn_gain.astype(F32)
    ffn_gain = ffn_gain.astype(F32)
    keyval_full = gather_rows(w_keyval)
    query_full = gather_rows_wide(w_query)
    output_full = gather_rows_wide(w_output)
    routes_far = from_others(routes)
    labels_rep = (jnp.arange(128, dtype=jnp.int32) == chosen).astype(BF16)
    ids_hot = lax.all_to_all(
        jnp.broadcast_to(labels_rep, (reps, 128)), "rep", split_axis=0, concat_axis=0, tiled=True
    )
    ids_all = jnp.sum(ids_hot.astype(jnp.int32) * jnp.arange(128, dtype=jnp.int32), axis=1)
    maps = (a_gateup.swapaxes(2, 3), b_gateup, a_down.swapaxes(2, 3), b_down)
    calls = 2 if experts_dev % (2 * FLUSH) == 0 and groups == 2 else 1
    each = experts_dev // calls
    folded = [fold_adapters(adapter_ids, w_gateup, w_down, *maps, 0, each)]
    tokens, ids_all = lax.optimization_barrier((tokens, ids_all))
    upstream_far = from_others(cotangent)

    tokens_f = tokens.astype(F32)
    normed = rms_norm(tokens_f, attn_gain).astype(BF16)
    low_rank = product_back(normed, qkv_in).astype(BF16)
    keyvals = product(normed, keyval_full)
    keyvals = jnp.concatenate(
        [
            keyvals[:, :kv_width] + product(low_rank[:, RANK : 2 * RANK], keyval_out[0]),
            keyvals[:, kv_width:] + product(low_rank[:, 2 * RANK :], keyval_out[1]),
        ],
        axis=1,
    ).astype(BF16)
    if calls == 2:
        some = each // 2
        second = fold_adapters(
            adapter_ids, w_gateup, w_down, *maps, each, some, size=each, after=(keyvals,)
        )
    keyvals_far = from_others(keyvals)
    query_rows = (product(normed, query_full) + product(low_rank[:, :RANK], query_out)).astype(BF16)
    pad_whole = jnp.roll(pad_all, -first)
    listing, steps, own_bias, live = visits(parents[0], pad_whole[:count], pad_whole[count:], first)
    attended, logs = run_attention(listing, steps, query_rows, keyvals, keyvals_far, own_bias, live)
    out_rank = product_back(attended, output_in).astype(BF16)
    middle = tokens_f + product(attended, output_full) + product(out_rank, output_out)
    normed_ffn = rms_norm(middle, ffn_gain).astype(BF16)
    if calls == 2:
        folded.append(
            fold_adapters(
                adapter_ids,
                w_gateup,
                w_down,
                *maps,
                each + some,
                each - some,
                second,
                some,
                each,
                after=(normed_ffn,),
            )
        )
    router_rank = product_back(normed_ffn, router_in).astype(BF16)
    logits = product_back(normed_ffn, router_full) + product(router_rank, router_out)

    labels = jnp.arange(experts, dtype=jnp.int32)
    named = jnp.any(routes[:, :, None] == labels, axis=1)
    best = jnp.max(jnp.where(named, logits, -jnp.inf), axis=1, keepdims=True)
    powers = jnp.where(named, jnp.exp(jnp.where(named, logits, best) - best), 0.0)
    gates = powers / jnp.sum(powers, axis=1, keepdims=True)

    mine = member * experts_dev + jnp.arange(experts_dev, dtype=jnp.int32)
    routes_all = jnp.concatenate([routes, routes_far], axis=0).reshape(groups, count, TOPK)
    hits = jnp.any(routes_all[:, :, :, None] == mine, axis=2)
    before = (jnp.arange(count)[:, None] > jnp.arange(count)[None, :]).astype(BF16)
    ranks = jnp.einsum("ts,gse->get", before, hits.astype(BF16), preferred_element_type=F32)
    places = jnp.where(hits.transpose(0, 2, 1), ranks.astype(jnp.int32), -1).transpose(1, 0, 2)

    rows_far = from_others(normed_ffn)
    gates_t = gates.T
    if groups == 2:
        gates_near = lax.dynamic_slice_in_dim(gates_t, member * experts_dev, experts_dev, 0)
        gates_far = from_others(lax.dynamic_slice_in_dim(gates_t, (1 - member) * experts_dev, experts_dev, 0))
        gates_mine = jnp.stack([gates_near, gates_far], axis=1)
    else:
        gates_mine = lax.all_gather(gates_t, "grp", axis=0)
        gates_mine = lax.dynamic_slice_in_dim(gates_mine, member * experts_dev, experts_dev, 1)
        gates_mine = jnp.roll(gates_mine, -member, axis=0).transpose(1, 0, 2)
    sums = ()
    gate_terms = []
    spread = []
    for n in range(calls):
        *sums, terms, grads = run_experts(
            adapter_ids,
            normed_ffn,
            rows_far,
            cotangent,
            upstream_far,
            places,
            gates_mine,
            *folded[n],
            *maps,
            tuple(sums),
            cap,
            n * each,
            each,
        )
        gate_terms.append(terms)
        if n:
            sums[3], swapped = lax.optimization_barrier((sums[3], swapped))
            spread.append(lax.all_gather(totals(ids_all, swapped, adapters), "rep", axis=0))
        swapped = lax.all_to_all(
            grads.reshape(reps, -1, UNIT), "rep", split_axis=0, concat_axis=0, tiled=True
        )
    result_near, result_far, d_near, d_far = sums
    part_gates = jnp.concatenate(gate_terms, axis=0)
    owner_hot = (jnp.arange(adapters, dtype=jnp.int32)[:, None] == ids_all[None, :]).astype(F32)
    if groups == 2:
        d_gates = in_order(part_gates[:, 0], from_others(part_gates[:, 1]))
    else:
        d_gates = jnp.roll(part_gates, member, axis=1)
        d_gates = lax.all_to_all(d_gates, "grp", split_axis=1, concat_axis=0, tiled=True)
    d_gates = d_gates.reshape(experts, count).T
    d_sum = to_owners(d_near, d_far)
    result_far, d_sum = lax.optimization_barrier((result_far, d_sum))
    mixture = owners_terms(result_near, result_far)
    upstream = cotangent.astype(F32)
    d_logits = (gates * (d_gates - jnp.sum(gates * d_gates, axis=1, keepdims=True))).astype(BF16)

    d_router_rank = product_back(d_logits, router_out).astype(BF16)
    d_normed_ffn = d_sum + product(d_logits, router_full) + product(d_router_rank, router_in)
    grad_router_out = product_outer(router_rank, d_logits)
    grad_router_in = product_outer(d_router_rank, normed_ffn)
    d_middle = upstream + rms_back(middle, ffn_gain, d_normed_ffn)
    d_attn = d_middle.astype(BF16)
    d_out_rank = product_back(d_attn, output_out).astype(BF16)
    attended_gradient = (product_back(d_attn, output_full) + product(d_out_rank, output_in)).astype(BF16)
    grad_output_out = product_outer(out_rank, d_attn)
    grad_output_in = product_outer(d_out_rank, attended)
    parts = []
    pairs = KEY_VALUE_HEADS // 4
    for n in range(2):
        d_q, *d_kv = run_attention_back(
            listing,
            steps,
            query_rows,
            keyvals,
            keyvals_far,
            own_bias,
            live,
            attended,
            attended_gradient,
            logs,
            n * pairs,
            pairs,
        )
        d_kv = to_owners(jnp.concatenate(d_kv[:2], axis=1), jnp.concatenate(d_kv[2:], axis=1)).astype(BF16)
        parts.append((d_q, d_kv[:, : kv_width // 2], d_kv[:, kv_width // 2 :]))
    d_queries, d_keys, d_values = [jnp.concatenate(pair, axis=1) for pair in zip(*parts)]
    d_keyvals = jnp.concatenate([d_keys, d_values], axis=1)
    d_rank_qkv = jnp.concatenate(
        [
            product_back(d_queries, query_out),
            product_back(d_keys, keyval_out[0]),
            product_back(d_values, keyval_out[1]),
        ],
        axis=-1,
    ).astype(BF16)
    d_normed = (
        product_back(d_queries, query_full)
        + product_back(d_keyvals, keyval_full)
        + product(d_rank_qkv, qkv_in)
    )
    grad_input = (d_middle + rms_back(tokens_f, attn_gain, d_normed)).astype(BF16)
    grad_qkv_in = product_outer(d_rank_qkv, normed)
    grad_query_out = product_outer(low_rank[:, :RANK], d_queries)
    grad_keyval_out = jnp.stack(
        [
            product_outer(low_rank[:, RANK : 2 * RANK], d_keys),
            product_outer(low_rank[:, 2 * RANK :], d_values),
        ],
        axis=0,
    )

    last = totals(ids_all, swapped, adapters, after=(parts[0][0],))
    spread.append(lax.all_gather(last, "rep", axis=0))
    expert_grads = ()
    for n in range(calls):
        expert_grads = unpack_grads(spread[n], experts_dev, n * each, tuple(expert_grads), width)
    grad_a_gateup, grad_b_gateup, grad_a_down, grad_b_down = expert_grads

    def split(gradient):
        return jnp.moveaxis(
            gradient.astype(BF16).reshape(gradient.shape[:-1] + (groups, -1)), -2, 0
        ).reshape(groups, -1)

    dense = jnp.concatenate(
        [
            split(piece)
            for piece in (
                grad_qkv_in,
                grad_query_out,
                grad_keyval_out,
                grad_output_in,
                grad_output_out,
                grad_router_in,
                grad_router_out,
            )
        ],
        axis=1,
    )
    dense = jnp.pad(dense, ((0, 0), (0, -dense.shape[1] % (reps * 128))))
    dense = dense.reshape(groups, reps, -1).swapaxes(0, 1).reshape(reps * groups, -1)
    dense = lax.all_to_all(dense, ("rep", "grp"), split_axis=0, concat_axis=0, tiled=True)
    dense = jnp.sum(dense.reshape(reps, groups, -1).astype(F32), axis=1)
    dense = jnp.sum(owner_hot[:, :, None] * dense[None], axis=1).astype(BF16)
    result = add_up(middle, *mixture, after=(dense,))
    dense = lax.all_gather(dense, "rep", axis=1).reshape(adapters, -1)
    owned = [piece.astype(F32) for piece in unpack(dense, shapes[:7])]
    return (
        result,
        grad_input,
        owned[0].swapaxes(1, 2),
        owned[1],
        owned[2],
        owned[3].swapaxes(1, 2),
        owned[4],
        owned[5].swapaxes(1, 2),
        owned[6],
        grad_a_gateup.swapaxes(2, 3),
        grad_b_gateup,
        grad_a_down.swapaxes(2, 3),
        grad_b_down,
    )


def solution(mesh):
    in_specs = (
        P(("rep", "grp"), None),
        P(("rep", "grp"), None),
        P(("rep", "grp"), None),
        P(("rep", "grp")),
        P("rep", None),
        P("rep"),
        P("grp", None),
        P("grp", None),
        P("grp", None),
        P("grp", None),
        P("grp"),
        P("grp"),
        P("grp", None, None),
        P("grp", None, None),
        P(None, "grp", None),
        P(None, None, "grp"),
        P(None, None, None, "grp"),
        P(None, "grp", None),
        P(None, None, "grp"),
        P(None, "grp", None),
        P(None, None, "grp"),
        P(None, "grp", None, None),
        P(None, "grp", None, None, None),
        P(None, "grp", None, None),
        P(None, "grp", None, None),
    )
    out_specs = (
        P(("rep", "grp"), None),
        P(("rep", "grp"), None),
        P(None, "grp", None),
        P(None, None, "grp"),
        P(None, None, None, "grp"),
        P(None, "grp", None),
        P(None, None, "grp"),
        P(None, "grp", None),
        P(None, None, "grp"),
        P(None, "grp", None, None),
        P(None, "grp", None, None, None),
        P(None, "grp", None, None),
        P(None, "grp", None, None),
    )
    return jax.shard_map(local, mesh=mesh, in_specs=in_specs, out_specs=out_specs, check_vma=False)
```

```python
import functools

import jax
import jax.numpy as jnp
from jax import lax
from jax.experimental import pallas as pl
from jax.experimental.pallas import tpu as pltpu
from jax.sharding import PartitionSpec as P

QUERY_HEADS = 24
KEY_VALUE_HEADS = 8
HEAD_SIZE = 64
FF = 512
TOPK = 8
RANK = 16
SEG = 128
FLUSH = 5
UNIT = 768

EPSILON = 1e-05
BF16 = jnp.bfloat16
F32 = jnp.float32


def product(left, right):
    return jnp.dot(left, right, preferred_element_type=F32)


def product_back(left, right):
    return lax.dot_general(left, right, (((1,), (1,)), ((), ())), preferred_element_type=F32)


def product_outer(left, right):
    return lax.dot_general(left, right, (((0,), (0,)), ((), ())), preferred_element_type=F32)


def rms_norm(value_rows, gain):
    return (
        value_rows
        * lax.rsqrt(jnp.mean(value_rows * value_rows, axis=-1, keepdims=True) + EPSILON)
        * gain
    )


def rms_back(value_rows, gain, upstream):
    factor = lax.rsqrt(jnp.mean(value_rows * value_rows, axis=-1, keepdims=True) + EPSILON)
    scaled = value_rows * factor
    incoming = upstream * gain
    return factor * (incoming - scaled * jnp.mean(incoming * scaled, axis=-1, keepdims=True))


def ancestry(parent_row):
    total = parent_row.shape[0]
    labels = jnp.arange(total, dtype=jnp.int32)

    def climb(count, state):
        current, table = state
        current = jnp.sum(
            jnp.where(current[:, None] == labels[None, :], parent_row[None, :], 0), axis=1
        )
        table = jnp.maximum(table, (current[:, None] == labels[None, :]).astype(jnp.int32))
        return (current, table)

    start_index = (labels[:, None] == labels[None, :]).astype(jnp.int32)
    return lax.fori_loop(0, total, climb, (labels, start_index))[1]


def tile_parts(ref_k, seg_a, seg_b):
    return jnp.concatenate(
        [
            ref_k[pl.ds(pl.multiple_of(seg_a * SEG, SEG), SEG), :],
            ref_k[pl.ds(pl.multiple_of(seg_b * SEG, SEG), SEG), :],
        ],
        axis=0,
    )


def fill_doubled(held, near_ref, far_ref, ones=False):
    near = near_ref.shape[0]
    for ref, at in ((near_ref, 0), (far_ref, near)):
        rows = ref[...].astype(F32)
        low = lax.broadcasted_iota(jnp.int32, rows.shape, 1) < HEAD_SIZE
        turned = pltpu.roll(rows, HEAD_SIZE, axis=1)
        there = pl.ds(at, rows.shape[0])
        held[0, there, :] = jnp.where(low, rows, 1.0 if ones else turned).astype(BF16)
        held[1, there, :] = jnp.where(low, turned, 1.0 if ones else rows).astype(BF16)


PLACES = (((0, 0), (0, 1), (1, 0)), ((1, 1), (2, 0), (2, 1)))


def stacked_heads(ref, at, which, scale=None):
    low = lax.broadcasted_iota(jnp.int32, (SEG, 2 * HEAD_SIZE), 1) < HEAD_SIZE
    out = []
    for column, half in PLACES[which]:
        piece = ref[at, column * 2 * HEAD_SIZE : (column + 1) * 2 * HEAD_SIZE].astype(F32)
        if scale is not None:
            piece = piece * scale
        out.append(jnp.where(low if half == 0 else jnp.logical_not(low), piece, 0.0))
    return jnp.concatenate(out, axis=0)


def unstack(first, second):
    low = lax.broadcasted_iota(jnp.int32, (SEG, 2 * HEAD_SIZE), 1) < HEAD_SIZE
    return [
        jnp.where(low, first[0:SEG], first[SEG : 2 * SEG]),
        jnp.where(low, first[2 * SEG :], second[0:SEG]),
        jnp.where(low, second[SEG : 2 * SEG], second[2 * SEG :]),
    ]


def first_bias(own_ref, live_ref, i, seg_b):
    other = jnp.broadcast_to(live_ref[seg_b], (SEG, SEG))
    tile = jnp.concatenate([own_ref[i], other], axis=1)
    return jnp.concatenate([tile] * 3, axis=0)


def next_bias(live_ref, seg_a, seg_b):
    return jnp.concatenate([live_ref[seg_a], live_ref[seg_b]], axis=1)


def attend_kernel(
    list_ref,
    steps_ref,
    q_ref,
    k_ref,
    v_ref,
    k_far,
    v_far,
    own_ref,
    live_ref,
    o_ref,
    l_ref,
    kf,
    vf,
    *,
    here,
    segs,
    scale,
):
    fill_doubled(kf, k_ref, k_far)
    fill_doubled(vf, v_ref, v_far, ones=True)
    lanes = lax.broadcasted_iota(jnp.int32, (SEG, 2 * HEAD_SIZE), 1)
    low = lanes < HEAD_SIZE
    slots = 2 * segs
    for i in range(here):
        at = pl.ds(i * SEG, SEG)
        queries = [stacked_heads(q_ref, at, which, scale).astype(BF16) for which in range(2)]

        def pair_of(t):
            return (
                lax.rem(list_ref[i * slots + 2 * t], segs),
                lax.rem(list_ref[i * slots + 2 * t + 1], segs),
            )

        seg_a, seg_b = pair_of(0)
        bias = first_bias(own_ref, live_ref, i, list_ref[i * slots + 1])
        state = []
        for which in range(2):
            s = product_back(queries[which], tile_parts(kf.at[which], seg_a, seg_b)) + bias
            top = jnp.max(s, axis=1, keepdims=True)
            p = jnp.exp(s - top).astype(BF16)
            state.append((top, product(p, tile_parts(vf.at[which], seg_a, seg_b))))

        def body(t, state):
            bias = next_bias(live_ref, list_ref[i * slots + 2 * t], list_ref[i * slots + 2 * t + 1])
            seg_a, seg_b = pair_of(t)
            out = []
            for which in range(2):
                top, acc = state[which]
                s = product_back(queries[which], tile_parts(kf.at[which], seg_a, seg_b)) + bias
                higher = jnp.maximum(top, jnp.max(s, axis=1, keepdims=True))
                p = jnp.exp(s - higher).astype(BF16)
                acc = acc * jnp.exp(top - higher) + product(p, tile_parts(vf.at[which], seg_a, seg_b))
                out.append((higher, acc))
            return tuple(out)

        state = lax.fori_loop(1, steps_ref[i], body, tuple(state))
        turned = [pltpu.roll(acc, HEAD_SIZE, axis=1) for _, acc in state]
        logs = jnp.zeros((SEG, 2 * HEAD_SIZE), F32)
        heads = []
        for which in range(2):
            for n, (_, half) in enumerate(PLACES[which]):
                rows = slice(n * SEG, (n + 1) * SEG)
                plain, other = state[which][1][rows], turned[which][rows]
                heads.append(plain / other if half == 0 else other / plain)
                total = jnp.where(low, other, plain)
                logs = jnp.where(lanes == which * 3 + n, state[which][0][rows] + jnp.log(total), logs)
        l_ref[0, at, :] = logs
        for column in range(3):
            o_ref[at, column * 2 * HEAD_SIZE : (column + 1) * 2 * HEAD_SIZE] = jnp.where(
                low, heads[2 * column], heads[2 * column + 1]
            ).astype(BF16)


def attend_back_kernel(
    list_ref,
    steps_ref,
    q_ref,
    k_ref,
    v_ref,
    k_far,
    v_far,
    own_ref,
    live_ref,
    o_ref,
    do_ref,
    l_ref,
    *refs,
    here,
    segs,
    scale,
    after,
):
    dq_ref, dk_ref, dv_ref, dk_far, dv_far, kf, vf, dkf, dvf = refs[after:]
    fill_doubled(kf, k_ref, k_far)
    fill_doubled(vf, v_ref, v_far)
    dkf[...] = jnp.zeros_like(dkf)
    dvf[...] = jnp.zeros_like(dvf)
    slots = 2 * segs
    for i in range(here):
        at = pl.ds(i * SEG, SEG)
        fixed = []
        for which in range(2):
            d_o = stacked_heads(do_ref, at, which)
            fixed.append(
                (
                    stacked_heads(q_ref, at, which, scale).astype(BF16),
                    d_o.astype(BF16),
                    jnp.sum(d_o * stacked_heads(o_ref, at, which), axis=1, keepdims=True),
                    jnp.concatenate(
                        [l_ref[0, at, which * 3 + n : which * 3 + n + 1] for n in range(3)], axis=0
                    ),
                )
            )

        def step(t, bias):
            seg_a = lax.rem(list_ref[i * slots + 2 * t], segs)
            seg_b = lax.rem(list_ref[i * slots + 2 * t + 1], segs)
            out = []
            for which, (q, d_o, delta, log_total) in enumerate(fixed):
                k = tile_parts(kf.at[which], seg_a, seg_b)
                v = tile_parts(vf.at[which], seg_a, seg_b)
                p = jnp.exp(product_back(q, k) + bias - log_total)
                d_p = product_back(d_o, v)
                d_s = (p * (d_p - delta)).astype(BF16)
                d_v = product_outer(p.astype(BF16), d_o)
                d_k = product_outer(d_s, q)
                for n, seg in enumerate((seg_a, seg_b)):
                    rows = pl.ds(pl.multiple_of(seg * SEG, SEG), SEG)
                    dkf[which, rows, :] += d_k[n * SEG : (n + 1) * SEG]
                    dvf[which, rows, :] += d_v[n * SEG : (n + 1) * SEG]
                out.append(product(d_s, k))
            return tuple(out)

        d_q = step(0, first_bias(own_ref, live_ref, i, list_ref[i * slots + 1]))

        def body(t, carry):
            bias = next_bias(live_ref, list_ref[i * slots + 2 * t], list_ref[i * slots + 2 * t + 1])
            return tuple(a + b for a, b in zip(carry, step(t, bias)))

        d_q = lax.fori_loop(1, steps_ref[i], body, d_q)
        for column, piece in enumerate(unstack(*d_q)):
            dq_ref[at, column * 2 * HEAD_SIZE : (column + 1) * 2 * HEAD_SIZE] = (piece * scale).astype(BF16)
    near = dk_ref.shape[0]
    for out, far_out, held in ((dk_ref, dk_far, dkf), (dv_ref, dv_far, dvf)):
        first = held[0] + pltpu.roll(held[0], HEAD_SIZE, axis=1)
        second = held[1] + pltpu.roll(held[1], HEAD_SIZE, axis=1)
        low = lax.broadcasted_iota(jnp.int32, first.shape, 1) < HEAD_SIZE
        total = jnp.where(low, first, second).astype(BF16)
        out[...] = total[:near]
        far_out[...] = total[near:]


def visits(parent_row, pad_near, pad_far, first):
    count = pad_near.shape[0]
    tree_length = count + pad_far.shape[0]
    segs = tree_length // SEG
    here = count // SEG
    own = jnp.arange(here, dtype=jnp.int32)
    labels = jnp.arange(segs, dtype=jnp.int32)
    table = lax.dynamic_slice_in_dim(ancestry(parent_row), first // SEG, here, 0)
    turn = (labels[:, None] == (labels[None, :] + segs - first // SEG) % segs).astype(F32)
    table = product_back(table.astype(F32), turn).astype(jnp.int32)
    table = jnp.where(labels[None, :] == own[:, None], 0, table)
    order = jnp.sum(jnp.where(labels[None, :] <= labels[:, None], table[:, None, :], 0), axis=2)
    spots = jnp.arange(1, 2 * segs, dtype=jnp.int32)
    found = jnp.logical_and(table[:, None, :] > 0, order[:, None, :] == spots[None, :, None])
    listing = jnp.where(jnp.any(found, axis=2), jnp.sum(found * labels, axis=2), segs)
    listing = jnp.concatenate([own[:, None], listing], axis=1).astype(jnp.int32)
    steps = (2 + order[:, -1]) // 2
    live = jnp.where(jnp.concatenate([pad_near, pad_far]) > 0, 0.0, -1e30).astype(F32).reshape(segs, SEG)
    places = jnp.arange(SEG)
    causal = places[None, :] <= places[:, None]
    same = places[None, :] == places[:, None]
    own_bias = jnp.where(same[None], 0.0, jnp.where(causal[None], live[:here, None, :], -1e30))
    live = jnp.concatenate([live, jnp.full((1, SEG), -1e30, F32)], axis=0)[:, None, :]
    return listing.reshape(-1), steps.astype(jnp.int32), own_bias, live


def attention_specs(count, far, here, segs, skip=0):
    narrow = 2 * HEAD_SIZE
    shift = KEY_VALUE_HEADS // 2 + skip
    return [
        pl.BlockSpec((count, 3 * narrow), lambda h, a, b: (0, h + skip)),
        pl.BlockSpec((count, narrow), lambda h, a, b: (0, h + skip)),
        pl.BlockSpec((count, narrow), lambda h, a, b: (0, h + shift)),
        pl.BlockSpec((far, narrow), lambda h, a, b: (0, h + skip)),
        pl.BlockSpec((far, narrow), lambda h, a, b: (0, h + shift)),
        pl.BlockSpec((here, SEG, SEG), lambda h, a, b: (0, 0, 0)),
        pl.BlockSpec((segs + 1, 1, SEG), lambda h, a, b: (0, 0, 0)),
    ]


def run_attention(listing, steps, queries, near, far, own_bias, live):
    count, width = queries.shape
    tree_length = count + far.shape[0]
    here, segs = count // SEG, tree_length // SEG
    pairs = KEY_VALUE_HEADS // 2
    narrow = 2 * HEAD_SIZE
    return pl.pallas_call(
        functools.partial(attend_kernel, here=here, segs=segs, scale=HEAD_SIZE ** (-0.5)),
        grid_spec=pltpu.PrefetchScalarGridSpec(
            num_scalar_prefetch=2,
            grid=(pairs,),
            in_specs=attention_specs(count, far.shape[0], here, segs),
            out_specs=[
                pl.BlockSpec((count, 3 * narrow), lambda h, a, b: (0, h)),
                pl.BlockSpec((1, count, narrow), lambda h, a, b: (h, 0, 0)),
            ],
            scratch_shapes=[pltpu.VMEM((2, tree_length, narrow), BF16)] * 2,
        ),
        out_shape=[
            jax.ShapeDtypeStruct((count, width), BF16),
            jax.ShapeDtypeStruct((pairs, count, narrow), F32),
        ],
        compiler_params=pltpu.CompilerParams(
            vmem_limit_bytes=40 * 1024 * 1024, dimension_semantics=("arbitrary",)
        ),
        cost_estimate=pl.CostEstimate(flops=40_000_000_000, bytes_accessed=8_000_000, transcendentals=10_000_000),
        name="attention",
    )(listing, steps, queries, near, near, far, far, own_bias, live)


def run_attention_back(
    listing, steps, queries, near, far, own_bias, live, attended, gradient, logs, skip, pairs, after=()
):
    count = queries.shape[0]
    tree_length = count + far.shape[0]
    here, segs = count // SEG, tree_length // SEG
    narrow = 2 * HEAD_SIZE
    rows = pl.BlockSpec((count, 3 * narrow), lambda h, a, b: (0, h + skip))
    outs = [pl.BlockSpec((count, narrow), lambda h, a, b: (0, h))] * 2
    outs += [pl.BlockSpec((far.shape[0], narrow), lambda h, a, b: (0, h))] * 2
    return pl.pallas_call(
        functools.partial(
            attend_back_kernel, here=here, segs=segs, scale=HEAD_SIZE ** (-0.5), after=len(after)
        ),
        grid_spec=pltpu.PrefetchScalarGridSpec(
            num_scalar_prefetch=2,
            grid=(pairs,),
            in_specs=attention_specs(count, far.shape[0], here, segs, skip)
            + [rows, rows, pl.BlockSpec((1, count, narrow), lambda h, a, b: (h + skip, 0, 0))]
            + [pl.BlockSpec(memory_space=pl.ANY)] * len(after),
            out_specs=[pl.BlockSpec((count, 3 * narrow), lambda h, a, b: (0, h))] + outs,
            scratch_shapes=[pltpu.VMEM((2, tree_length, narrow), BF16)] * 2
            + [pltpu.VMEM((2, tree_length, narrow), F32)] * 2,
        ),
        out_shape=[jax.ShapeDtypeStruct((count, 3 * pairs * narrow), BF16)]
        + [jax.ShapeDtypeStruct((count, pairs * narrow), BF16)] * 2
        + [jax.ShapeDtypeStruct((far.shape[0], pairs * narrow), BF16)] * 2,
        compiler_params=pltpu.CompilerParams(
            vmem_limit_bytes=40 * 1024 * 1024, dimension_semantics=("arbitrary",)
        ),
        cost_estimate=pl.CostEstimate(
            flops=17_000_000_000 * pairs, bytes_accessed=3_000_000 * pairs, transcendentals=0
        ),
        name="attention_back",
    )(listing, steps, queries, near, near, far, far, own_bias, live, attended, gradient, logs, *after)


def expert_kernel(
    chosen_ref,
    x_ref,
    x_far,
    g_ref,
    g_far,
    pos_ref,
    gate_ref,
    w1_ref,
    w2_ref,
    a1_ref,
    b1_ref,
    a2_ref,
    b2_ref,
    *refs,
    blocks,
    rows_block,
    cap,
    flush,
    carried,
):
    held = refs[:4] if carried else ()
    (
        r_out,
        r_far,
        d_out,
        d_far,
        dg_out,
        grad_out,
        hot_s,
        o_s,
        dx_s,
        accr,
        accd,
        x_s,
        g_s,
        gate_s,
        b1_s,
        dgu_s,
    ) = refs[len(held) :]
    e = pl.program_id(0)
    slot = lax.rem(e, flush)
    width = x_ref.shape[-1]
    halves = width // UNIT

    @pl.when(e == 0)
    def _():
        b1_s[...] = jnp.zeros_like(b1_s)
        if carried:
            for n, acc in enumerate((accr, accd)):
                acc[0:rows_block, :] = held[2 * n][...].astype(F32)
                acc[rows_block:, :] = held[2 * n + 1][...].astype(F32)
        else:
            accr[...] = jnp.zeros_like(accr)
            accd[...] = jnp.zeros_like(accd)

    at = pl.multiple_of(slot * cap, 16)
    for b in range(blocks):
        rows_ref, g_rows_ref = (x_ref, g_ref) if b == 0 else (x_far, g_far)
        here = pl.ds(max(b - 1, 0) * rows_block, rows_block)
        there = pl.ds(b * cap, cap)
        places = lax.broadcasted_iota(jnp.int32, (cap, rows_block), 0)
        hit = places == pos_ref[0, b : b + 1, :]
        hot = hit.astype(F32).astype(BF16)
        hot_s[b, pl.ds(at, cap), :] = hot
        x_s[there, :] = product(hot, rows_ref[here, :]).astype(BF16)
        g_s[there, :] = product(hot, g_rows_ref[here, :]).astype(BF16)
        gate_s[there, :] = jnp.sum(
            jnp.where(hit, gate_ref[0, b : b + 1, :], 0.0), axis=1, keepdims=True
        )
    b1_s[0:RANK, 0:FF] = b1_ref[0, 0, 0]
    b1_s[RANK : 2 * RANK, FF : 2 * FF] = b1_ref[0, 0, 1]

    x = x_s[...]
    gate_col = gate_s[...]
    rank_in = product_back(a1_ref[0, 0], x).astype(BF16)
    pre = product(x, w1_ref[0])
    gate_pre = pre[:, :FF]
    up_pre = pre[:, FF:]
    sig = 1.0 / (1.0 + jnp.exp(-gate_pre))
    act = gate_pre * sig
    hidden = (act * up_pre).astype(BF16)
    rank_down = product_back(a2_ref[0, 0], hidden).astype(BF16)
    out = product(hidden, w2_ref[0]).astype(BF16).astype(F32)
    g = g_s[...].astype(F32)
    d_gate_col = jnp.sum(g * out, axis=1, keepdims=True)
    out = (gate_col * out).astype(BF16)
    d_exp = (gate_col * g).astype(BF16)
    d_rank_down = product_back(b2_ref[0, 0], d_exp).astype(BF16)
    d_hidden = product_back(d_exp, w2_ref[0])
    dgu_s[:, :FF] = (d_hidden * up_pre * sig * (1.0 + gate_pre * (1.0 - sig))).astype(BF16)
    dgu_s[:, FF:] = (d_hidden * act).astype(BF16)
    dgu = dgu_s[...]
    d_rank_in = product_back(b1_s[...], dgu).astype(BF16)
    dx = product_back(dgu, w1_ref[0]).astype(BF16)
    for b in range(blocks):
        o_s[b, pl.ds(at, cap), :] = out[b * cap : (b + 1) * cap]
        dx_s[b, pl.ds(at, cap), :] = dx[b * cap : (b + 1) * cap]
        places = lax.broadcasted_iota(jnp.int32, (cap, rows_block), 0)
        hit = places == pos_ref[0, b : b + 1, :]
        dg_out[0, b : b + 1, :] = jnp.sum(
            jnp.where(hit, d_gate_col[b * cap : (b + 1) * cap], 0.0), axis=0, keepdims=True
        )

    grad_a1 = product(d_rank_in, x)
    grad_b1 = product(rank_in, dgu)
    grad_a2 = product(d_rank_down, hidden)
    grad_b2 = product(rank_down, d_exp)
    last = jnp.concatenate([grad_b1[:RANK, :FF], grad_b1[RANK:, FF:], grad_a2], axis=1)
    for n, piece in enumerate((grad_a1[:RANK], grad_a1[RANK:], grad_b2, last)):
        for half in range(halves):
            rows = slice((n * halves + half) * RANK, (n * halves + half + 1) * RANK)
            grad_out[0, rows, :] = piece[:, half * UNIT : (half + 1) * UNIT].astype(BF16)

    @pl.when(slot == flush - 1)
    def _():
        for b in range(blocks):
            here = pl.ds(b * rows_block, rows_block)
            accr[here, :] += product_outer(hot_s[b], o_s[b])
            accd[here, :] += product_outer(hot_s[b], dx_s[b])

    @pl.when(e == pl.num_programs(0) - 1)
    def _():
        r_out[...] = accr[0:rows_block, :].astype(BF16)
        r_far[...] = accr[rows_block:, :].astype(BF16)
        d_out[...] = accd[0:rows_block, :].astype(BF16)
        d_far[...] = accd[rows_block:, :].astype(BF16)


def run_experts(chosen, x, x_far, g, g_far, pos, gate, w1, w2, a1, b1, a2, b2, held, cap, first, count):
    _, blocks, rows_block = pos.shape
    width = x.shape[1]
    tokens = blocks * rows_block
    rows = blocks * cap
    flush = FLUSH if count % FLUSH == 0 else 1
    record = 4 * RANK * width // UNIT
    lead = lambda e, c: (e, 0, 0)
    shifted = lambda e, c: (e + first, 0, 0)
    near = pl.BlockSpec((rows_block, width), lambda e, c: (0, 0), pipeline_mode=pl.Buffered(1))
    away = pl.BlockSpec((tokens - rows_block, width), lambda e, c: (0, 0), pipeline_mode=pl.Buffered(1))
    near_shape = jax.ShapeDtypeStruct((rows_block, width), BF16)
    away_shape = jax.ShapeDtypeStruct((tokens - rows_block, width), BF16)
    return pl.pallas_call(
        functools.partial(
            expert_kernel,
            blocks=blocks,
            rows_block=rows_block,
            cap=cap,
            flush=flush,
            carried=bool(held),
        ),
        grid_spec=pltpu.PrefetchScalarGridSpec(
            num_scalar_prefetch=1,
            grid=(count,),
            in_specs=[
                near,
                away,
                near,
                away,
                pl.BlockSpec((1, blocks, rows_block), shifted),
                pl.BlockSpec((1, blocks, rows_block), shifted),
                pl.BlockSpec((1, width, 2 * FF), lead),
                pl.BlockSpec((1, FF, width), lead),
                pl.BlockSpec((1, 1, 2 * RANK, width), lambda e, c: (c[0], e + first, 0, 0)),
                pl.BlockSpec((1, 1, 2, RANK, FF), lambda e, c: (c[0], e + first, 0, 0, 0)),
                pl.BlockSpec((1, 1, RANK, FF), lambda e, c: (c[0], e + first, 0, 0)),
                pl.BlockSpec((1, 1, RANK, width), lambda e, c: (c[0], e + first, 0, 0)),
            ]
            + ([near, away, near, away] if held else []),
            out_specs=[
                near,
                away,
                near,
                away,
                pl.BlockSpec((1, blocks, rows_block), lead),
                pl.BlockSpec((1, record, UNIT), lead),
            ],
            scratch_shapes=[
                pltpu.VMEM((blocks, flush * cap, rows_block), BF16),
                pltpu.VMEM((blocks, flush * cap, width), BF16),
                pltpu.VMEM((blocks, flush * cap, width), BF16),
                pltpu.VMEM((tokens, width), F32),
                pltpu.VMEM((tokens, width), F32),
                pltpu.VMEM((rows, width), BF16),
                pltpu.VMEM((rows, width), BF16),
                pltpu.VMEM((rows, 1), F32),
                pltpu.VMEM((2 * RANK, 2 * FF), BF16),
                pltpu.VMEM((rows, 2 * FF), BF16),
            ],
        ),
        out_shape=[
            near_shape,
            away_shape,
            near_shape,
            away_shape,
            jax.ShapeDtypeStruct((count, blocks, rows_block), F32),
            jax.ShapeDtypeStruct((count, record, UNIT), BF16),
        ],
        compiler_params=pltpu.CompilerParams(
            vmem_limit_bytes=63 * 1024 * 1024, dimension_semantics=("arbitrary",)
        ),
        cost_estimate=pl.CostEstimate(
            flops=8_000_000_000 * count,
            bytes_accessed=5_000_000 * count,
            transcendentals=rows * FF * count,
        ),
        name="experts",
    )(chosen, x, x_far, g, g_far, pos, gate, w1, w2, a1, b1, a2, b2, *held)


def fold_kernel(chosen_ref, w1_ref, w2_ref, a1_ref, b1_ref, a2_ref, b2_ref, *refs):
    o1_ref, o2_ref = refs[-2:]
    for n in range(2):
        at = slice(n * FF, (n + 1) * FF)
        a1 = a1_ref[0, 0, n * RANK : (n + 1) * RANK, :]
        o1_ref[0, :, at] = (w1_ref[0, :, at].astype(F32) + product_outer(a1, b1_ref[0, 0, n])).astype(BF16)
    o2_ref[0] = (w2_ref[0].astype(F32) + product_outer(a2_ref[0, 0], b2_ref[0, 0])).astype(BF16)


def fold_adapters(chosen, w1, w2, a1, b1, a2, b2, first, count, held=(), skip=0, size=None, after=()):
    size = size or count
    placed = lambda e, c: (e + skip, 0, 0)
    _, width, _ = w1.shape
    shifted = lambda e, c: (e + first, 0, 0)
    return pl.pallas_call(
        fold_kernel,
        grid_spec=pltpu.PrefetchScalarGridSpec(
            num_scalar_prefetch=1,
            grid=(count,),
            in_specs=[
                pl.BlockSpec((1, width, 2 * FF), shifted),
                pl.BlockSpec((1, FF, width), shifted),
                pl.BlockSpec((1, 1, 2 * RANK, width), lambda e, c: (c[0], e + first, 0, 0)),
                pl.BlockSpec((1, 1, 2, RANK, FF), lambda e, c: (c[0], e + first, 0, 0, 0)),
                pl.BlockSpec((1, 1, RANK, FF), lambda e, c: (c[0], e + first, 0, 0)),
                pl.BlockSpec((1, 1, RANK, width), lambda e, c: (c[0], e + first, 0, 0)),
            ]
            + [pl.BlockSpec(memory_space=pl.ANY)] * (len(held) + len(after)),
            out_specs=[pl.BlockSpec((1, width, 2 * FF), placed), pl.BlockSpec((1, FF, width), placed)],
        ),
        out_shape=[
            jax.ShapeDtypeStruct((size, width, 2 * FF), BF16),
            jax.ShapeDtypeStruct((size, FF, width), BF16),
        ],
        input_output_aliases={7 + n: n for n in range(len(held))},
        compiler_params=pltpu.CompilerParams(
            vmem_limit_bytes=40 * 1024 * 1024, dimension_semantics=("arbitrary",)
        ),
        cost_estimate=pl.CostEstimate(
            flops=3_000_000_000 * count, bytes_accessed=12_000_000 * count, transcendentals=0
        ),
        name="fold",
    )(chosen, w1, w2, a1, b1, a2, b2, *held, *after)


def total_kernel(ids_ref, rows_ref, *refs):
    out_ref, held = refs[-2:]
    held[...] = jnp.zeros_like(held)
    for n in range(rows_ref.shape[0]):
        held[ids_ref[n]] += rows_ref[n].astype(F32)
    out_ref[...] = held[...].astype(BF16)


def totals(ids, rows, adapters, after=()):
    shape = (adapters,) + rows.shape[1:]
    if rows.shape[1] % 16:
        hot = (jnp.arange(adapters, dtype=jnp.int32)[:, None] == ids[None, :]).astype(F32)
        return jnp.sum(hot[:, :, None, None] * rows.astype(F32)[None], axis=1).astype(BF16)
    return pl.pallas_call(
        total_kernel,
        grid_spec=pltpu.PrefetchScalarGridSpec(
            num_scalar_prefetch=1,
            grid=(1,),
            in_specs=[pl.BlockSpec(rows.shape, lambda i, c: (0, 0, 0))]
            + [pl.BlockSpec(memory_space=pl.ANY)] * len(after),
            out_specs=pl.BlockSpec(shape, lambda i, c: (0, 0, 0)),
            scratch_shapes=[pltpu.VMEM(shape, F32)],
        ),
        out_shape=jax.ShapeDtypeStruct(shape, BF16),
        compiler_params=pltpu.CompilerParams(vmem_limit_bytes=32 * 1024 * 1024),
        cost_estimate=pl.CostEstimate(flops=0, bytes_accessed=5_000_000, transcendentals=0),
        name="totals",
    )(ids, rows, *after)


def add_kernel(first_ref, second_ref, third_ref, *refs):
    total = first_ref[...] + second_ref[...].astype(F32) + third_ref[...].astype(F32)
    refs[-1][...] = total.astype(BF16)


def add_up(first, second, third, after=()):
    return pl.pallas_call(
        add_kernel,
        in_specs=[pl.BlockSpec(memory_space=pltpu.VMEM)] * 3
        + [pl.BlockSpec(memory_space=pl.ANY)] * len(after),
        out_specs=pl.BlockSpec(memory_space=pltpu.VMEM),
        out_shape=jax.ShapeDtypeStruct(first.shape, BF16),
        compiler_params=pltpu.CompilerParams(vmem_limit_bytes=32 * 1024 * 1024),
        name="add_up",
    )(first, second, third, *after)


def unpack_kernel(rows_ref, *refs, share):
    a1_ref, b1_ref, a2_ref, b2_ref = refs[-4:]
    halves = a1_ref.shape[-1] // UNIT
    record = 4 * RANK * halves
    for e in range(rows_ref.shape[0] * share // record):
        unit = []
        for n in range(4 * halves):
            at = e * record + n * RANK
            unit.append(rows_ref[at // share, 0, at % share : at % share + RANK, :].astype(F32))
        for half in range(halves):
            at = slice(half * UNIT, (half + 1) * UNIT)
            a1_ref[0, e, 0:RANK, at] = unit[half]
            a1_ref[0, e, RANK:, at] = unit[halves + half]
            b2_ref[0, e, :, at] = unit[2 * halves + half]
        last = jnp.concatenate(unit[3 * halves :], axis=1)
        b1_ref[0, e, 0] = last[:, :FF]
        b1_ref[0, e, 1] = last[:, FF : 2 * FF]
        a2_ref[0, e] = last[:, 2 * FF :]


def unpack_grads(gathered, experts, first, held, width):
    ranks, adapters, share, _ = gathered.shape
    halves = width // UNIT
    record = 4 * RANK * halves
    if share % 16:
        flat = gathered.swapaxes(0, 1).reshape(adapters, experts, 4, halves, RANK, UNIT)
        flat = flat.swapaxes(3, 4).reshape(adapters, experts, 4 * RANK, width).astype(F32)
        last = flat[:, :, 3 * RANK :]
        return (
            flat[:, :, : 2 * RANK],
            jnp.stack([last[..., :FF], last[..., FF : 2 * FF]], axis=2),
            last[..., 2 * FF :],
            flat[:, :, 2 * RANK : 3 * RANK],
        )
    together = 1
    while together * share % record:
        together += 1
    each = together * share // record
    skip = first // each
    return pl.pallas_call(
        functools.partial(unpack_kernel, share=share),
        grid=(adapters, ranks // together),
        in_specs=[pl.BlockSpec((together, 1, share, UNIT), lambda a, i: (i, a, 0, 0))]
        + [pl.BlockSpec(memory_space=pl.ANY)] * len(held),
        out_specs=[
            pl.BlockSpec((1, each, 2 * RANK, width), lambda a, i: (a, i + skip, 0, 0)),
            pl.BlockSpec((1, each, 2, RANK, FF), lambda a, i: (a, i + skip, 0, 0, 0)),
            pl.BlockSpec((1, each, RANK, FF), lambda a, i: (a, i + skip, 0, 0)),
            pl.BlockSpec((1, each, RANK, width), lambda a, i: (a, i + skip, 0, 0)),
        ],
        out_shape=[
            jax.ShapeDtypeStruct((adapters, experts, 2 * RANK, width), F32),
            jax.ShapeDtypeStruct((adapters, experts, 2, RANK, FF), F32),
            jax.ShapeDtypeStruct((adapters, experts, RANK, FF), F32),
            jax.ShapeDtypeStruct((adapters, experts, RANK, width), F32),
        ],
        input_output_aliases={1 + n: n for n in range(len(held))},
        compiler_params=pltpu.CompilerParams(
            vmem_limit_bytes=40 * 1024 * 1024, dimension_semantics=("arbitrary", "arbitrary")
        ),
        cost_estimate=pl.CostEstimate(flops=0, bytes_accessed=30_000_000, transcendentals=0),
        name="unpack",
    )(gathered, *held)


def swap_pairs(size):
    return [(i, i ^ 1) for i in range(size)]


def from_others(piece):
    groups = lax.axis_size("grp")
    if groups == 2:
        return lax.ppermute(piece, "grp", swap_pairs(2))
    rows = piece.shape[0]
    every = lax.all_gather(piece, "grp", axis=0, tiled=True)
    return jnp.roll(every, -lax.axis_index("grp") * rows, axis=0)[rows:]


def owners_terms(near, far):
    if lax.axis_size("grp") == 2:
        return near, lax.ppermute(far, "grp", swap_pairs(2))
    return to_owners(near, far), jnp.zeros_like(near)


def to_owners(near, far):
    groups = lax.axis_size("grp")
    if groups == 2:
        return near.astype(F32) + lax.ppermute(far, "grp", swap_pairs(2)).astype(F32)
    every = jnp.roll(jnp.concatenate([near, far], axis=0), lax.axis_index("grp") * near.shape[0], axis=0)
    return lax.psum_scatter(every, "grp", scatter_dimension=0, tiled=True).astype(F32)


def in_order(near, far):
    if lax.axis_size("grp") != 2:
        return jnp.roll(jnp.concatenate([near, far], axis=0), lax.axis_index("grp") * near.shape[0], axis=0)
    ahead = lax.axis_index("grp") == 0
    return jnp.where(ahead, jnp.concatenate([near, far], axis=0), jnp.concatenate([far, near], axis=0))


def gather_rows(half):
    if lax.axis_size("grp") != 2:
        return lax.all_gather(half, "grp", axis=0, tiled=True)
    rows = half.shape[0] // 2
    core = lax.axis_index("rep") % 2
    got = lax.ppermute(lax.dynamic_slice_in_dim(half, core * rows, rows, 0), "grp", swap_pairs(2))
    other = lax.ppermute(got, "rep", swap_pairs(lax.axis_size("rep")))
    ahead = core == 0
    far = jnp.where(ahead, jnp.concatenate([got, other], 0), jnp.concatenate([other, got], 0))
    return in_order(half, far)


def gather_rows_wide(half, note=None):
    reps = lax.axis_size("rep")
    if lax.axis_size("grp") != 2 or half.shape[0] % (reps * 16):
        whole = lax.all_gather(half, "grp", axis=0, tiled=True)
        return (whole, lax.all_gather(note, "rep", axis=0)) if note is not None else whole
    rows = half.shape[0] // reps
    mine = lax.dynamic_slice_in_dim(half, lax.axis_index("rep") * rows, rows, 0)
    got = lax.ppermute(mine, "grp", swap_pairs(2))
    if note is None:
        return in_order(half, lax.all_gather(got, "rep", axis=0, tiled=True))
    got = jnp.concatenate([got, jnp.broadcast_to(note[None], (8, note.shape[0]))], axis=0)
    every = lax.all_gather(got, "rep", axis=0)
    return in_order(half, every[:, :rows].reshape(half.shape)), every[:, rows]


def delayed_kernel(rows_ref, *refs):
    refs[-1][...] = rows_ref[...]


def delayed(rows, after):
    return pl.pallas_call(
        delayed_kernel,
        in_specs=[pl.BlockSpec(memory_space=pltpu.VMEM)] + [pl.BlockSpec(memory_space=pl.ANY)] * len(after),
        out_specs=pl.BlockSpec(memory_space=pltpu.VMEM),
        out_shape=jax.ShapeDtypeStruct(rows.shape, rows.dtype),
        compiler_params=pltpu.CompilerParams(vmem_limit_bytes=16 * 1024 * 1024),
        name="delayed",
    )(rows, *after)


def pack(pieces, multiple):
    flat = jnp.concatenate([piece.reshape(-1) for piece in pieces])
    return jnp.pad(flat, (0, -flat.shape[0] % multiple))


def unpack(flat, shapes):
    out = []
    offset = 0
    for shape in shapes:
        size = 1
        for extent in shape:
            size *= extent
        out.append(flat[..., offset : offset + size].reshape(flat.shape[:-1] + shape))
        offset += size
    return out


def local(
    tokens,
    cotangent,
    routes,
    padding,
    parents,
    adapter_ids,
    w_query,
    w_keyval,
    w_output,
    w_router,
    gain_attn,
    gain_ffn,
    w_gateup,
    w_down,
    a_qkv,
    b_query,
    b_keyval,
    a_output,
    b_output,
    a_router,
    b_router,
    a_gateup,
    b_gateup,
    a_down,
    b_down,
):
    groups = lax.axis_size("grp")
    reps = lax.axis_size("rep")
    member = lax.axis_index("grp")
    count = tokens.shape[0]
    width = tokens.shape[1]
    part = width // groups
    tree_length = count * groups
    experts_dev = w_gateup.shape[0]
    experts = experts_dev * groups
    capacity = count * TOPK * 7 // (experts * 5)
    cap = -(-capacity // 16) * 16
    kv_width = KEY_VALUE_HEADS * HEAD_SIZE
    chosen = adapter_ids[0]
    first = member * count
    adapters = a_qkv.shape[0]

    shapes = (
        (3 * RANK, part),
        (RANK, part),
        (2, RANK, kv_width // groups),
        (RANK, part),
        (RANK, part),
        (RANK, part),
        (RANK, experts_dev),
        (experts, part),
        (part,),
        (part,),
        (count,),
    )
    small = pack(
        (
            a_qkv[chosen].T,
            b_query[chosen],
            b_keyval[chosen],
            a_output[chosen].T,
            b_output[chosen],
            a_router[chosen].T,
            b_router[chosen],
            w_router.T,
            gain_attn,
            gain_ffn,
            padding.astype(BF16),
        ),
        1024,
    )
    small_all = in_order(small[None], from_others(small[None]))

    def join(piece):
        return jnp.moveaxis(piece, 0, -2).reshape(piece.shape[1:-1] + (-1,))

    (
        qkv_in,
        query_out,
        keyval_out,
        output_in,
        output_out,
        router_in,
        router_out,
        router_full,
        attn_gain,
        ffn_gain,
        pad_all,
    ) = [join(piece) for piece in unpack(small_all, shapes)]
    attn_gain = attn_gain.astype(F32)
    ffn_gain = ffn_gain.astype(F32)
    keyval_full = gather_rows(w_keyval)
    query_full = gather_rows_wide(w_query)
    note = (jnp.arange(width, dtype=jnp.int32) == chosen).astype(BF16)
    output_full, notes = gather_rows_wide(w_output, note)
    ids_all = jnp.sum(
        notes[:, :adapters].astype(jnp.int32) * jnp.arange(adapters, dtype=jnp.int32), axis=1
    )
    routes_far = from_others(routes)
    maps = (a_gateup.swapaxes(2, 3), b_gateup, a_down.swapaxes(2, 3), b_down)
    calls = 2 if experts_dev % (4 * FLUSH) == 0 and groups == 2 else 1
    each = experts_dev // calls
    some = -(-each // 2)

    def fold(call, late, held, after):
        at = some if late else 0
        count = each - some if late else some
        return fold_adapters(
            adapter_ids, w_gateup, w_down, *maps, call * each + at, count, held, at, each, after
        )

    first_fold = fold(0, False, (), ())

    tokens_f = tokens.astype(F32)
    normed = rms_norm(tokens_f, attn_gain).astype(BF16)
    low_rank = product_back(normed, qkv_in).astype(BF16)
    keyvals = product(normed, keyval_full)
    keyvals = jnp.concatenate(
        [
            keyvals[:, :kv_width] + product(low_rank[:, RANK : 2 * RANK], keyval_out[0]),
            keyvals[:, kv_width:] + product(low_rank[:, 2 * RANK :], keyval_out[1]),
        ],
        axis=1,
    ).astype(BF16)
    folded = [fold(0, True, first_fold, (keyvals,))]
    keyvals_far = from_others(keyvals)
    upstream_far = from_others(delayed(cotangent, (keyvals_far,)))
    query_rows = (product(normed, query_full) + product(low_rank[:, :RANK], query_out)).astype(BF16)
    pad_whole = jnp.roll(pad_all, -first)
    listing, steps, own_bias, live = visits(parents[0], pad_whole[:count], pad_whole[count:], first)
    attended, logs = run_attention(listing, steps, query_rows, keyvals, keyvals_far, own_bias, live)
    out_rank = product_back(attended, output_in).astype(BF16)
    middle = tokens_f + product(attended, output_full) + product(out_rank, output_out)
    normed_ffn = rms_norm(middle, ffn_gain).astype(BF16)
    if calls == 2:
        folded.append(fold(1, True, fold(1, False, (), (normed_ffn,)), ()))
    router_rank = product_back(normed_ffn, router_in).astype(BF16)
    logits = product_back(normed_ffn, router_full) + product(router_rank, router_out)

    labels = jnp.arange(experts, dtype=jnp.int32)
    named = jnp.any(routes[:, :, None] == labels, axis=1)
    best = jnp.max(jnp.where(named, logits, -jnp.inf), axis=1, keepdims=True)
    powers = jnp.where(named, jnp.exp(jnp.where(named, logits, best) - best), 0.0)
    gates = powers / jnp.sum(powers, axis=1, keepdims=True)

    mine = member * experts_dev + jnp.arange(experts_dev, dtype=jnp.int32)
    routes_all = jnp.concatenate([routes, routes_far], axis=0).reshape(groups, count, TOPK)
    hits = jnp.any(routes_all[:, :, :, None] == mine, axis=2)
    before = (jnp.arange(count)[:, None] > jnp.arange(count)[None, :]).astype(BF16)
    ranks = jnp.einsum("ts,gse->get", before, hits.astype(BF16), preferred_element_type=F32)
    places = jnp.where(hits.transpose(0, 2, 1), ranks.astype(jnp.int32), -1).transpose(1, 0, 2)

    rows_far = from_others(normed_ffn)
    gates_t = gates.T
    if groups == 2:
        gates_near = lax.dynamic_slice_in_dim(gates_t, member * experts_dev, experts_dev, 0)
        gates_far = from_others(lax.dynamic_slice_in_dim(gates_t, (1 - member) * experts_dev, experts_dev, 0))
        gates_mine = jnp.stack([gates_near, gates_far], axis=1)
    else:
        gates_mine = lax.all_gather(gates_t, "grp", axis=0)
        gates_mine = lax.dynamic_slice_in_dim(gates_mine, member * experts_dev, experts_dev, 1)
        gates_mine = jnp.roll(gates_mine, -member, axis=0).transpose(1, 0, 2)
    sums = ()
    gate_terms = []
    spread = []
    for n in range(calls):
        *sums, terms, grads = run_experts(
            adapter_ids,
            normed_ffn,
            rows_far,
            cotangent,
            upstream_far,
            places,
            gates_mine,
            *folded[n],
            *maps,
            tuple(sums),
            cap,
            n * each,
            each,
        )
        gate_terms.append(terms)
        if n:
            sums[3], swapped = lax.optimization_barrier((sums[3], swapped))
            spread.append(lax.all_gather(totals(ids_all, swapped, adapters), "rep", axis=0))
        swapped = lax.all_to_all(
            grads.reshape(reps, -1, UNIT), "rep", split_axis=0, concat_axis=0, tiled=True
        )
    result_near, result_far, d_near, d_far = sums
    part_gates = jnp.concatenate(gate_terms, axis=0)
    if groups == 2:
        d_gates = in_order(part_gates[:, 0], from_others(part_gates[:, 1]))
    else:
        d_gates = jnp.roll(part_gates, member, axis=1)
        d_gates = lax.all_to_all(d_gates, "grp", split_axis=1, concat_axis=0, tiled=True)
    d_gates = d_gates.reshape(experts, count).T
    d_sum = to_owners(d_near, d_far)
    result_far, d_sum = lax.optimization_barrier((result_far, d_sum))
    mixture = owners_terms(result_near, result_far)
    upstream = cotangent.astype(F32)
    d_logits = (gates * (d_gates - jnp.sum(gates * d_gates, axis=1, keepdims=True))).astype(BF16)

    d_router_rank = product_back(d_logits, router_out).astype(BF16)
    d_normed_ffn = d_sum + product(d_logits, router_full) + product(d_router_rank, router_in)
    grad_router_out = product_outer(router_rank, d_logits)
    grad_router_in = product_outer(d_router_rank, normed_ffn)
    d_middle = upstream + rms_back(middle, ffn_gain, d_normed_ffn)
    d_attn = d_middle.astype(BF16)
    d_out_rank = product_back(d_attn, output_out).astype(BF16)
    attended_gradient = (product_back(d_attn, output_full) + product(d_out_rank, output_in)).astype(BF16)
    grad_output_out = product_outer(out_rank, d_attn)
    grad_output_in = product_outer(d_out_rank, attended)
    parts = []
    pairs = KEY_VALUE_HEADS // 4
    for n in range(2):
        d_q, *d_kv = run_attention_back(
            listing,
            steps,
            query_rows,
            keyvals,
            keyvals_far,
            own_bias,
            live,
            attended,
            attended_gradient,
            logs,
            n * pairs,
            pairs,
        )
        d_kv = to_owners(jnp.concatenate(d_kv[:2], axis=1), jnp.concatenate(d_kv[2:], axis=1)).astype(BF16)
        parts.append((d_q, d_kv[:, : kv_width // 2], d_kv[:, kv_width // 2 :]))
    d_queries, d_keys, d_values = [jnp.concatenate(pair, axis=1) for pair in zip(*parts)]
    d_keyvals = jnp.concatenate([d_keys, d_values], axis=1)
    d_rank_qkv = jnp.concatenate(
        [
            product_back(d_queries, query_out),
            product_back(d_keys, keyval_out[0]),
            product_back(d_values, keyval_out[1]),
        ],
        axis=-1,
    ).astype(BF16)
    d_normed = (
        product_back(d_queries, query_full)
        + product_back(d_keyvals, keyval_full)
        + product(d_rank_qkv, qkv_in)
    )
    grad_input = (d_middle + rms_back(tokens_f, attn_gain, d_normed)).astype(BF16)
    grad_qkv_in = product_outer(d_rank_qkv, normed)
    grad_query_out = product_outer(low_rank[:, :RANK], d_queries)
    grad_keyval_out = jnp.stack(
        [
            product_outer(low_rank[:, RANK : 2 * RANK], d_keys),
            product_outer(low_rank[:, 2 * RANK :], d_values),
        ],
        axis=0,
    )

    last = totals(ids_all, swapped, adapters, after=(attended_gradient,))
    spread.append(lax.all_gather(last, "rep", axis=0))
    expert_grads = ()
    for n in range(calls):
        expert_grads = unpack_grads(spread[n], experts_dev, n * each, tuple(expert_grads), width)
    grad_a_gateup, grad_b_gateup, grad_a_down, grad_b_down = expert_grads

    tall = jnp.concatenate(
        [grad_qkv_in, grad_query_out, grad_output_in, grad_output_out, grad_router_in], axis=0
    ).astype(BF16)
    high = tall.shape[0]
    kv_part = kv_width // groups
    tall = tall.reshape(high, groups, part).swapaxes(0, 1)
    wide = [
        grad_keyval_out[0].reshape(RANK, groups, kv_part),
        grad_keyval_out[1].reshape(RANK, groups, kv_part),
        grad_router_out.reshape(RANK, groups, experts_dev),
        jnp.zeros((RANK, groups, part - 2 * kv_part - experts_dev), F32),
    ]
    wide = jnp.concatenate(wide, axis=2).astype(BF16).swapaxes(0, 1)
    dense = jnp.concatenate([tall, wide], axis=1).reshape(groups, reps, -1, part).swapaxes(0, 1)
    dense = dense.reshape(reps * groups, -1, part)
    result = add_up(middle, *mixture, after=(dense,))
    dense = lax.all_to_all(dense, ("rep", "grp"), split_axis=0, concat_axis=0, tiled=True)
    owner_hot = (jnp.arange(adapters, dtype=jnp.int32)[:, None] == jnp.repeat(ids_all, groups)[None, :])
    dense = jnp.sum(jnp.where(owner_hot[:, :, None, None], dense.astype(F32)[None], 0.0), axis=1).astype(BF16)
    dense = lax.all_gather(dense, "rep", axis=0).swapaxes(0, 1).reshape(adapters, -1, part).astype(F32)
    wide = dense[:, high:]
    owned = [
        dense[:, : 3 * RANK],
        dense[:, 3 * RANK : 4 * RANK],
        jnp.stack([wide[:, :, :kv_part], wide[:, :, kv_part : 2 * kv_part]], axis=1),
        dense[:, 4 * RANK : 5 * RANK],
        dense[:, 5 * RANK : 6 * RANK],
        dense[:, 6 * RANK : 7 * RANK],
        wide[:, :, 2 * kv_part : 2 * kv_part + experts_dev],
    ]
    return (
        result,
        grad_input,
        owned[0].swapaxes(1, 2),
        owned[1],
        owned[2],
        owned[3].swapaxes(1, 2),
        owned[4],
        owned[5].swapaxes(1, 2),
        owned[6],
        grad_a_gateup.swapaxes(2, 3),
        grad_b_gateup,
        grad_a_down.swapaxes(2, 3),
        grad_b_down,
    )


def solution(mesh):
    in_specs = (
        P(("rep", "grp"), None),
        P(("rep", "grp"), None),
        P(("rep", "grp"), None),
        P(("rep", "grp")),
        P("rep", None),
        P("rep"),
        P("grp", None),
        P("grp", None),
        P("grp", None),
        P("grp", None),
        P("grp"),
        P("grp"),
        P("grp", None, None),
        P("grp", None, None),
        P(None, "grp", None),
        P(None, None, "grp"),
        P(None, None, None, "grp"),
        P(None, "grp", None),
        P(None, None, "grp"),
        P(None, "grp", None),
        P(None, None, "grp"),
        P(None, "grp", None, None),
        P(None, "grp", None, None, None),
        P(None, "grp", None, None),
        P(None, "grp", None, None),
    )
    out_specs = (
        P(("rep", "grp"), None),
        P(("rep", "grp"), None),
        P(None, "grp", None),
        P(None, None, "grp"),
        P(None, None, None, "grp"),
        P(None, "grp", None),
        P(None, None, "grp"),
        P(None, "grp", None),
        P(None, None, "grp"),
        P(None, "grp", None, None),
        P(None, "grp", None, None, None),
        P(None, "grp", None, None),
        P(None, "grp", None, None),
    )
    return jax.shard_map(local, mesh=mesh, in_specs=in_specs, out_specs=out_specs, check_vma=False)
```

```python
import functools

import jax
import jax.numpy as jnp
from jax import lax
from jax.experimental import pallas as pl
from jax.experimental.pallas import tpu as pltpu
from jax.sharding import PartitionSpec as P

QUERY_HEADS = 24
KEY_VALUE_HEADS = 8
HEAD_SIZE = 64
FF = 512
TOPK = 8
RANK = 16
SEG = 128
FLUSH = 5
UNIT = 768

EPSILON = 1e-05
BF16 = jnp.bfloat16
F32 = jnp.float32


def product(left, right):
    return jnp.dot(left, right, preferred_element_type=F32)


def product_back(left, right):
    return lax.dot_general(left, right, (((1,), (1,)), ((), ())), preferred_element_type=F32)


def product_outer(left, right):
    return lax.dot_general(left, right, (((0,), (0,)), ((), ())), preferred_element_type=F32)


def rms_norm(value_rows, gain):
    return (
        value_rows
        * lax.rsqrt(jnp.mean(value_rows * value_rows, axis=-1, keepdims=True) + EPSILON)
        * gain
    )


def rms_back(value_rows, gain, upstream):
    factor = lax.rsqrt(jnp.mean(value_rows * value_rows, axis=-1, keepdims=True) + EPSILON)
    scaled = value_rows * factor
    incoming = upstream * gain
    return factor * (incoming - scaled * jnp.mean(incoming * scaled, axis=-1, keepdims=True))


def ancestry(parent_row):
    total = parent_row.shape[0]
    labels = jnp.arange(total, dtype=jnp.int32)
    own = labels[:, None] == labels[None, :]
    reached = jnp.logical_or(own, parent_row[:, None] == labels[None, :])
    steps = 1
    while steps < total:
        reached = jnp.any(jnp.logical_and(reached[:, :, None], reached[None, :, :]), axis=1)
        steps *= 2
    return reached.astype(jnp.int32)


def tile_parts(ref_k, seg_a, seg_b):
    return jnp.concatenate(
        [
            ref_k[pl.ds(pl.multiple_of(seg_a * SEG, SEG), SEG), :],
            ref_k[pl.ds(pl.multiple_of(seg_b * SEG, SEG), SEG), :],
        ],
        axis=0,
    )


def fill_doubled(held, near_ref, far_ref, ones=False):
    near = near_ref.shape[0]
    for ref, at in ((near_ref, 0), (far_ref, near)):
        rows = ref[...].astype(F32)
        low = lax.broadcasted_iota(jnp.int32, rows.shape, 1) < HEAD_SIZE
        turned = pltpu.roll(rows, HEAD_SIZE, axis=1)
        there = pl.ds(at, rows.shape[0])
        held[0, there, :] = jnp.where(low, rows, 1.0 if ones else turned).astype(BF16)
        held[1, there, :] = jnp.where(low, turned, 1.0 if ones else rows).astype(BF16)


PLACES = (((0, 0), (0, 1), (1, 0)), ((1, 1), (2, 0), (2, 1)))


def stacked_heads(ref, at, which, scale=None):
    low = lax.broadcasted_iota(jnp.int32, (SEG, 2 * HEAD_SIZE), 1) < HEAD_SIZE
    out = []
    for column, half in PLACES[which]:
        piece = ref[at, column * 2 * HEAD_SIZE : (column + 1) * 2 * HEAD_SIZE].astype(F32)
        if scale is not None:
            piece = piece * scale
        out.append(jnp.where(low if half == 0 else jnp.logical_not(low), piece, 0.0))
    return jnp.concatenate(out, axis=0)


def unstack(first, second):
    low = lax.broadcasted_iota(jnp.int32, (SEG, 2 * HEAD_SIZE), 1) < HEAD_SIZE
    return [
        jnp.where(low, first[0:SEG], first[SEG : 2 * SEG]),
        jnp.where(low, first[2 * SEG :], second[0:SEG]),
        jnp.where(low, second[SEG : 2 * SEG], second[2 * SEG :]),
    ]


def first_bias(own_ref, live_ref, i, seg_b):
    other = jnp.broadcast_to(live_ref[seg_b], (SEG, SEG))
    tile = jnp.concatenate([own_ref[i], other], axis=1)
    return jnp.concatenate([tile] * 3, axis=0)


def next_bias(live_ref, seg_a, seg_b):
    return jnp.concatenate([live_ref[seg_a], live_ref[seg_b]], axis=1)


def attend_kernel(
    list_ref,
    steps_ref,
    q_ref,
    k_ref,
    v_ref,
    k_far,
    v_far,
    own_ref,
    live_ref,
    o_ref,
    l_ref,
    kf,
    vf,
    *,
    here,
    segs,
    scale,
):
    fill_doubled(kf, k_ref, k_far)
    fill_doubled(vf, v_ref, v_far, ones=True)
    lanes = lax.broadcasted_iota(jnp.int32, (SEG, 2 * HEAD_SIZE), 1)
    low = lanes < HEAD_SIZE
    slots = 2 * segs
    for i in range(here):
        at = pl.ds(i * SEG, SEG)
        queries = [stacked_heads(q_ref, at, which, scale).astype(BF16) for which in range(2)]

        def pair_of(t):
            return (
                lax.rem(list_ref[i * slots + 2 * t], segs),
                lax.rem(list_ref[i * slots + 2 * t + 1], segs),
            )

        seg_a, seg_b = pair_of(0)
        bias = first_bias(own_ref, live_ref, i, list_ref[i * slots + 1])
        state = []
        for which in range(2):
            s = product_back(queries[which], tile_parts(kf.at[which], seg_a, seg_b)) + bias
            top = jnp.max(s, axis=1, keepdims=True)
            p = jnp.exp(s - top).astype(BF16)
            state.append((top, product(p, tile_parts(vf.at[which], seg_a, seg_b))))

        def body(t, state):
            bias = next_bias(live_ref, list_ref[i * slots + 2 * t], list_ref[i * slots + 2 * t + 1])
            seg_a, seg_b = pair_of(t)
            out = []
            for which in range(2):
                top, acc = state[which]
                s = product_back(queries[which], tile_parts(kf.at[which], seg_a, seg_b)) + bias
                higher = jnp.maximum(top, jnp.max(s, axis=1, keepdims=True))
                p = jnp.exp(s - higher).astype(BF16)
                acc = acc * jnp.exp(top - higher) + product(p, tile_parts(vf.at[which], seg_a, seg_b))
                out.append((higher, acc))
            return tuple(out)

        state = lax.fori_loop(1, steps_ref[i], body, tuple(state))
        turned = [pltpu.roll(acc, HEAD_SIZE, axis=1) for _, acc in state]
        logs = jnp.zeros((SEG, 2 * HEAD_SIZE), F32)
        heads = []
        for which in range(2):
            for n, (_, half) in enumerate(PLACES[which]):
                rows = slice(n * SEG, (n + 1) * SEG)
                plain, other = state[which][1][rows], turned[which][rows]
                heads.append(plain / other if half == 0 else other / plain)
                total = jnp.where(low, other, plain)
                logs = jnp.where(lanes == which * 3 + n, state[which][0][rows] + jnp.log(total), logs)
        l_ref[0, at, :] = logs
        for column in range(3):
            o_ref[at, column * 2 * HEAD_SIZE : (column + 1) * 2 * HEAD_SIZE] = jnp.where(
                low, heads[2 * column], heads[2 * column + 1]
            ).astype(BF16)


def attend_back_kernel(
    list_ref,
    steps_ref,
    q_ref,
    k_ref,
    v_ref,
    k_far,
    v_far,
    own_ref,
    live_ref,
    o_ref,
    do_ref,
    l_ref,
    *refs,
    here,
    segs,
    scale,
    after,
):
    dq_ref, dk_ref, dv_ref, dk_far, dv_far, kf, vf, dkf, dvf = refs[after:]
    fill_doubled(kf, k_ref, k_far)
    fill_doubled(vf, v_ref, v_far)
    dkf[...] = jnp.zeros_like(dkf)
    dvf[...] = jnp.zeros_like(dvf)
    slots = 2 * segs
    for i in range(here):
        at = pl.ds(i * SEG, SEG)
        fixed = []
        for which in range(2):
            d_o = stacked_heads(do_ref, at, which)
            fixed.append(
                (
                    stacked_heads(q_ref, at, which, scale).astype(BF16),
                    d_o.astype(BF16),
                    jnp.sum(d_o * stacked_heads(o_ref, at, which), axis=1, keepdims=True),
                    jnp.concatenate(
                        [l_ref[0, at, which * 3 + n : which * 3 + n + 1] for n in range(3)], axis=0
                    ),
                )
            )

        def step(t, bias):
            seg_a = lax.rem(list_ref[i * slots + 2 * t], segs)
            seg_b = lax.rem(list_ref[i * slots + 2 * t + 1], segs)
            out = []
            for which, (q, d_o, delta, log_total) in enumerate(fixed):
                k = tile_parts(kf.at[which], seg_a, seg_b)
                v = tile_parts(vf.at[which], seg_a, seg_b)
                p = jnp.exp(product_back(q, k) + bias - log_total)
                d_p = product_back(d_o, v)
                d_s = (p * (d_p - delta)).astype(BF16)
                d_v = product_outer(p.astype(BF16), d_o)
                d_k = product_outer(d_s, q)
                for n, seg in enumerate((seg_a, seg_b)):
                    rows = pl.ds(pl.multiple_of(seg * SEG, SEG), SEG)
                    dkf[which, rows, :] += d_k[n * SEG : (n + 1) * SEG]
                    dvf[which, rows, :] += d_v[n * SEG : (n + 1) * SEG]
                out.append(product(d_s, k))
            return tuple(out)

        d_q = step(0, first_bias(own_ref, live_ref, i, list_ref[i * slots + 1]))

        def body(t, carry):
            bias = next_bias(live_ref, list_ref[i * slots + 2 * t], list_ref[i * slots + 2 * t + 1])
            return tuple(a + b for a, b in zip(carry, step(t, bias)))

        d_q = lax.fori_loop(1, steps_ref[i], body, d_q)
        for column, piece in enumerate(unstack(*d_q)):
            dq_ref[at, column * 2 * HEAD_SIZE : (column + 1) * 2 * HEAD_SIZE] = (piece * scale).astype(BF16)
    near = dk_ref.shape[0]
    for out, far_out, held in ((dk_ref, dk_far, dkf), (dv_ref, dv_far, dvf)):
        first = held[0] + pltpu.roll(held[0], HEAD_SIZE, axis=1)
        second = held[1] + pltpu.roll(held[1], HEAD_SIZE, axis=1)
        low = lax.broadcasted_iota(jnp.int32, first.shape, 1) < HEAD_SIZE
        total = jnp.where(low, first, second).astype(BF16)
        out[...] = total[:near]
        far_out[...] = total[near:]


def visits(parent_row, pad_near, pad_far, first):
    count = pad_near.shape[0]
    tree_length = count + pad_far.shape[0]
    segs = tree_length // SEG
    here = count // SEG
    own = jnp.arange(here, dtype=jnp.int32)
    labels = jnp.arange(segs, dtype=jnp.int32)
    table = lax.dynamic_slice_in_dim(ancestry(parent_row), first // SEG, here, 0)
    turn = (labels[:, None] == (labels[None, :] + segs - first // SEG) % segs).astype(F32)
    table = product_back(table.astype(F32), turn).astype(jnp.int32)
    table = jnp.where(labels[None, :] == own[:, None], 0, table)
    order = jnp.sum(jnp.where(labels[None, :] <= labels[:, None], table[:, None, :], 0), axis=2)
    spots = jnp.arange(1, 2 * segs, dtype=jnp.int32)
    found = jnp.logical_and(table[:, None, :] > 0, order[:, None, :] == spots[None, :, None])
    listing = jnp.where(jnp.any(found, axis=2), jnp.sum(found * labels, axis=2), segs)
    listing = jnp.concatenate([own[:, None], listing], axis=1).astype(jnp.int32)
    steps = (2 + order[:, -1]) // 2
    live = jnp.where(jnp.concatenate([pad_near, pad_far]) > 0, 0.0, -1e30).astype(F32).reshape(segs, SEG)
    places = jnp.arange(SEG)
    causal = places[None, :] <= places[:, None]
    same = places[None, :] == places[:, None]
    own_bias = jnp.where(same[None], 0.0, jnp.where(causal[None], live[:here, None, :], -1e30))
    live = jnp.concatenate([live, jnp.full((1, SEG), -1e30, F32)], axis=0)[:, None, :]
    return listing.reshape(-1), steps.astype(jnp.int32), own_bias, live


def attention_specs(count, far, here, segs, skip=0):
    narrow = 2 * HEAD_SIZE
    shift = KEY_VALUE_HEADS // 2 + skip
    return [
        pl.BlockSpec((count, 3 * narrow), lambda h, a, b: (0, h + skip)),
        pl.BlockSpec((count, narrow), lambda h, a, b: (0, h + skip)),
        pl.BlockSpec((count, narrow), lambda h, a, b: (0, h + shift)),
        pl.BlockSpec((far, narrow), lambda h, a, b: (0, h + skip)),
        pl.BlockSpec((far, narrow), lambda h, a, b: (0, h + shift)),
        pl.BlockSpec((here, SEG, SEG), lambda h, a, b: (0, 0, 0)),
        pl.BlockSpec((segs + 1, 1, SEG), lambda h, a, b: (0, 0, 0)),
    ]


def run_attention(listing, steps, queries, near, far, own_bias, live):
    count, width = queries.shape
    tree_length = count + far.shape[0]
    here, segs = count // SEG, tree_length // SEG
    pairs = KEY_VALUE_HEADS // 2
    narrow = 2 * HEAD_SIZE
    return pl.pallas_call(
        functools.partial(attend_kernel, here=here, segs=segs, scale=HEAD_SIZE ** (-0.5)),
        grid_spec=pltpu.PrefetchScalarGridSpec(
            num_scalar_prefetch=2,
            grid=(pairs,),
            in_specs=attention_specs(count, far.shape[0], here, segs),
            out_specs=[
                pl.BlockSpec((count, 3 * narrow), lambda h, a, b: (0, h)),
                pl.BlockSpec((1, count, narrow), lambda h, a, b: (h, 0, 0)),
            ],
            scratch_shapes=[pltpu.VMEM((2, tree_length, narrow), BF16)] * 2,
        ),
        out_shape=[
            jax.ShapeDtypeStruct((count, width), BF16),
            jax.ShapeDtypeStruct((pairs, count, narrow), F32),
        ],
        compiler_params=pltpu.CompilerParams(
            vmem_limit_bytes=40 * 1024 * 1024, dimension_semantics=("arbitrary",)
        ),
        cost_estimate=pl.CostEstimate(flops=40_000_000_000, bytes_accessed=8_000_000, transcendentals=10_000_000),
        name="attention",
    )(listing, steps, queries, near, near, far, far, own_bias, live)


def run_attention_back(
    listing, steps, queries, near, far, own_bias, live, attended, gradient, logs, skip, pairs, after=()
):
    count = queries.shape[0]
    tree_length = count + far.shape[0]
    here, segs = count // SEG, tree_length // SEG
    narrow = 2 * HEAD_SIZE
    rows = pl.BlockSpec((count, 3 * narrow), lambda h, a, b: (0, h + skip))
    outs = [pl.BlockSpec((count, narrow), lambda h, a, b: (0, h))] * 2
    outs += [pl.BlockSpec((far.shape[0], narrow), lambda h, a, b: (0, h))] * 2
    return pl.pallas_call(
        functools.partial(
            attend_back_kernel, here=here, segs=segs, scale=HEAD_SIZE ** (-0.5), after=len(after)
        ),
        grid_spec=pltpu.PrefetchScalarGridSpec(
            num_scalar_prefetch=2,
            grid=(pairs,),
            in_specs=attention_specs(count, far.shape[0], here, segs, skip)
            + [rows, rows, pl.BlockSpec((1, count, narrow), lambda h, a, b: (h + skip, 0, 0))]
            + [pl.BlockSpec(memory_space=pl.ANY)] * len(after),
            out_specs=[pl.BlockSpec((count, 3 * narrow), lambda h, a, b: (0, h))] + outs,
            scratch_shapes=[pltpu.VMEM((2, tree_length, narrow), BF16)] * 2
            + [pltpu.VMEM((2, tree_length, narrow), F32)] * 2,
        ),
        out_shape=[jax.ShapeDtypeStruct((count, 3 * pairs * narrow), BF16)]
        + [jax.ShapeDtypeStruct((count, pairs * narrow), BF16)] * 2
        + [jax.ShapeDtypeStruct((far.shape[0], pairs * narrow), BF16)] * 2,
        compiler_params=pltpu.CompilerParams(
            vmem_limit_bytes=40 * 1024 * 1024, dimension_semantics=("arbitrary",)
        ),
        cost_estimate=pl.CostEstimate(
            flops=17_000_000_000 * pairs, bytes_accessed=3_000_000 * pairs, transcendentals=0
        ),
        name="attention_back",
    )(listing, steps, queries, near, near, far, far, own_bias, live, attended, gradient, logs, *after)


def expert_kernel(
    chosen_ref,
    x_ref,
    x_far,
    g_ref,
    g_far,
    pos_ref,
    gate_ref,
    w1_ref,
    w2_ref,
    a1_ref,
    b1_ref,
    a2_ref,
    b2_ref,
    *refs,
    blocks,
    rows_block,
    cap,
    flush,
    carried,
):
    held = refs[:4] if carried else ()
    (
        r_out,
        r_far,
        d_out,
        d_far,
        dg_out,
        grad_out,
        hot_s,
        o_s,
        dx_s,
        accr,
        accd,
        x_s,
        g_s,
        gate_s,
        b1_s,
        dgu_s,
    ) = refs[len(held) :]
    e = pl.program_id(0)
    slot = lax.rem(e, flush)
    width = x_ref.shape[-1]
    halves = width // UNIT

    @pl.when(e == 0)
    def _():
        b1_s[...] = jnp.zeros_like(b1_s)
        if carried:
            for n, acc in enumerate((accr, accd)):
                acc[0:rows_block, :] = held[2 * n][...].astype(F32)
                acc[rows_block:, :] = held[2 * n + 1][...].astype(F32)
        else:
            accr[...] = jnp.zeros_like(accr)
            accd[...] = jnp.zeros_like(accd)

    at = pl.multiple_of(slot * cap, 16)
    for b in range(blocks):
        rows_ref, g_rows_ref = (x_ref, g_ref) if b == 0 else (x_far, g_far)
        here = pl.ds(max(b - 1, 0) * rows_block, rows_block)
        there = pl.ds(b * cap, cap)
        places = lax.broadcasted_iota(jnp.int32, (cap, rows_block), 0)
        hit = places == pos_ref[0, b : b + 1, :]
        hot = hit.astype(F32).astype(BF16)
        hot_s[b, pl.ds(at, cap), :] = hot
        x_s[there, :] = product(hot, rows_ref[here, :]).astype(BF16)
        g_s[there, :] = product(hot, g_rows_ref[here, :]).astype(BF16)
        gate_s[there, :] = jnp.sum(
            jnp.where(hit, gate_ref[0, b : b + 1, :], 0.0), axis=1, keepdims=True
        )
    b1_s[0:RANK, 0:FF] = b1_ref[0, 0, 0]
    b1_s[RANK : 2 * RANK, FF : 2 * FF] = b1_ref[0, 0, 1]

    x = x_s[...]
    gate_col = gate_s[...]
    rank_in = product_back(a1_ref[0, 0], x).astype(BF16)
    pre = product(x, w1_ref[0])
    gate_pre = pre[:, :FF]
    up_pre = pre[:, FF:]
    sig = 1.0 / (1.0 + jnp.exp(-gate_pre))
    act = gate_pre * sig
    hidden = (act * up_pre).astype(BF16)
    rank_down = product_back(a2_ref[0, 0], hidden).astype(BF16)
    out = product(hidden, w2_ref[0]).astype(BF16).astype(F32)
    g = g_s[...].astype(F32)
    d_gate_col = jnp.sum(g * out, axis=1, keepdims=True)
    out = (gate_col * out).astype(BF16)
    d_exp = (gate_col * g).astype(BF16)
    d_rank_down = product_back(b2_ref[0, 0], d_exp).astype(BF16)
    d_hidden = product_back(d_exp, w2_ref[0])
    dgu_s[:, :FF] = (d_hidden * up_pre * sig * (1.0 + gate_pre * (1.0 - sig))).astype(BF16)
    dgu_s[:, FF:] = (d_hidden * act).astype(BF16)
    dgu = dgu_s[...]
    d_rank_in = product_back(b1_s[...], dgu).astype(BF16)
    dx = product_back(dgu, w1_ref[0]).astype(BF16)
    for b in range(blocks):
        o_s[b, pl.ds(at, cap), :] = out[b * cap : (b + 1) * cap]
        dx_s[b, pl.ds(at, cap), :] = dx[b * cap : (b + 1) * cap]
        places = lax.broadcasted_iota(jnp.int32, (cap, rows_block), 0)
        hit = places == pos_ref[0, b : b + 1, :]
        dg_out[0, b : b + 1, :] = jnp.sum(
            jnp.where(hit, d_gate_col[b * cap : (b + 1) * cap], 0.0), axis=0, keepdims=True
        )

    grad_a1 = product(d_rank_in, x)
    grad_b1 = product(rank_in, dgu)
    grad_a2 = product(d_rank_down, hidden)
    grad_b2 = product(rank_down, d_exp)
    last = jnp.concatenate([grad_b1[:RANK, :FF], grad_b1[RANK:, FF:], grad_a2], axis=1)
    for n, piece in enumerate((grad_a1[:RANK], grad_a1[RANK:], grad_b2, last)):
        for half in range(halves):
            rows = slice((n * halves + half) * RANK, (n * halves + half + 1) * RANK)
            grad_out[0, rows, :] = piece[:, half * UNIT : (half + 1) * UNIT].astype(BF16)

    @pl.when(slot == flush - 1)
    def _():
        for b in range(blocks):
            here = pl.ds(b * rows_block, rows_block)
            accr[here, :] += product_outer(hot_s[b], o_s[b])
            accd[here, :] += product_outer(hot_s[b], dx_s[b])

    @pl.when(e == pl.num_programs(0) - 1)
    def _():
        r_out[...] = accr[0:rows_block, :].astype(BF16)
        r_far[...] = accr[rows_block:, :].astype(BF16)
        d_out[...] = accd[0:rows_block, :].astype(BF16)
        d_far[...] = accd[rows_block:, :].astype(BF16)


def run_experts(chosen, x, x_far, g, g_far, pos, gate, w1, w2, a1, b1, a2, b2, held, cap, first, count):
    _, blocks, rows_block = pos.shape
    width = x.shape[1]
    tokens = blocks * rows_block
    rows = blocks * cap
    flush = FLUSH if count % FLUSH == 0 else 1
    record = 4 * RANK * width // UNIT
    lead = lambda e, c: (e, 0, 0)
    shifted = lambda e, c: (e + first, 0, 0)
    near = pl.BlockSpec((rows_block, width), lambda e, c: (0, 0), pipeline_mode=pl.Buffered(1))
    away = pl.BlockSpec((tokens - rows_block, width), lambda e, c: (0, 0), pipeline_mode=pl.Buffered(1))
    near_shape = jax.ShapeDtypeStruct((rows_block, width), BF16)
    away_shape = jax.ShapeDtypeStruct((tokens - rows_block, width), BF16)
    return pl.pallas_call(
        functools.partial(
            expert_kernel,
            blocks=blocks,
            rows_block=rows_block,
            cap=cap,
            flush=flush,
            carried=bool(held),
        ),
        grid_spec=pltpu.PrefetchScalarGridSpec(
            num_scalar_prefetch=1,
            grid=(count,),
            in_specs=[
                near,
                away,
                near,
                away,
                pl.BlockSpec((1, blocks, rows_block), shifted),
                pl.BlockSpec((1, blocks, rows_block), shifted),
                pl.BlockSpec((1, width, 2 * FF), lead),
                pl.BlockSpec((1, FF, width), lead),
                pl.BlockSpec((1, 1, 2 * RANK, width), lambda e, c: (c[0], e + first, 0, 0)),
                pl.BlockSpec((1, 1, 2, RANK, FF), lambda e, c: (c[0], e + first, 0, 0, 0)),
                pl.BlockSpec((1, 1, RANK, FF), lambda e, c: (c[0], e + first, 0, 0)),
                pl.BlockSpec((1, 1, RANK, width), lambda e, c: (c[0], e + first, 0, 0)),
            ]
            + ([near, away, near, away] if held else []),
            out_specs=[
                near,
                away,
                near,
                away,
                pl.BlockSpec((1, blocks, rows_block), lead),
                pl.BlockSpec((1, record, UNIT), lead),
            ],
            scratch_shapes=[
                pltpu.VMEM((blocks, flush * cap, rows_block), BF16),
                pltpu.VMEM((blocks, flush * cap, width), BF16),
                pltpu.VMEM((blocks, flush * cap, width), BF16),
                pltpu.VMEM((tokens, width), F32),
                pltpu.VMEM((tokens, width), F32),
                pltpu.VMEM((rows, width), BF16),
                pltpu.VMEM((rows, width), BF16),
                pltpu.VMEM((rows, 1), F32),
                pltpu.VMEM((2 * RANK, 2 * FF), BF16),
                pltpu.VMEM((rows, 2 * FF), BF16),
            ],
        ),
        out_shape=[
            near_shape,
            away_shape,
            near_shape,
            away_shape,
            jax.ShapeDtypeStruct((count, blocks, rows_block), F32),
            jax.ShapeDtypeStruct((count, record, UNIT), BF16),
        ],
        compiler_params=pltpu.CompilerParams(
            vmem_limit_bytes=63 * 1024 * 1024, dimension_semantics=("arbitrary",)
        ),
        cost_estimate=pl.CostEstimate(
            flops=8_000_000_000 * count,
            bytes_accessed=5_000_000 * count,
            transcendentals=rows * FF * count,
        ),
        name="experts",
    )(chosen, x, x_far, g, g_far, pos, gate, w1, w2, a1, b1, a2, b2, *held)


def fold_kernel(chosen_ref, w1_ref, w2_ref, a1_ref, b1_ref, a2_ref, b2_ref, *refs):
    o1_ref, o2_ref = refs[-2:]
    for n in range(2):
        at = slice(n * FF, (n + 1) * FF)
        a1 = a1_ref[0, 0, n * RANK : (n + 1) * RANK, :]
        o1_ref[0, :, at] = (w1_ref[0, :, at].astype(F32) + product_outer(a1, b1_ref[0, 0, n])).astype(BF16)
    o2_ref[0] = (w2_ref[0].astype(F32) + product_outer(a2_ref[0, 0], b2_ref[0, 0])).astype(BF16)


def fold_adapters(chosen, w1, w2, a1, b1, a2, b2, first, count, held=(), skip=0, size=None, after=()):
    size = size or count
    placed = lambda e, c: (e + skip, 0, 0)
    _, width, _ = w1.shape
    shifted = lambda e, c: (e + first, 0, 0)
    return pl.pallas_call(
        fold_kernel,
        grid_spec=pltpu.PrefetchScalarGridSpec(
            num_scalar_prefetch=1,
            grid=(count,),
            in_specs=[
                pl.BlockSpec((1, width, 2 * FF), shifted),
                pl.BlockSpec((1, FF, width), shifted),
                pl.BlockSpec((1, 1, 2 * RANK, width), lambda e, c: (c[0], e + first, 0, 0)),
                pl.BlockSpec((1, 1, 2, RANK, FF), lambda e, c: (c[0], e + first, 0, 0, 0)),
                pl.BlockSpec((1, 1, RANK, FF), lambda e, c: (c[0], e + first, 0, 0)),
                pl.BlockSpec((1, 1, RANK, width), lambda e, c: (c[0], e + first, 0, 0)),
            ]
            + [pl.BlockSpec(memory_space=pl.ANY)] * (len(held) + len(after)),
            out_specs=[pl.BlockSpec((1, width, 2 * FF), placed), pl.BlockSpec((1, FF, width), placed)],
        ),
        out_shape=[
            jax.ShapeDtypeStruct((size, width, 2 * FF), BF16),
            jax.ShapeDtypeStruct((size, FF, width), BF16),
        ],
        input_output_aliases={7 + n: n for n in range(len(held))},
        compiler_params=pltpu.CompilerParams(
            vmem_limit_bytes=40 * 1024 * 1024, dimension_semantics=("arbitrary",)
        ),
        cost_estimate=pl.CostEstimate(
            flops=3_000_000_000 * count, bytes_accessed=12_000_000 * count, transcendentals=0
        ),
        name="fold",
    )(chosen, w1, w2, a1, b1, a2, b2, *held, *after)


def total_kernel(ids_ref, rows_ref, *refs):
    out_ref, held = refs[-2:]
    held[...] = jnp.zeros_like(held)
    for n in range(rows_ref.shape[0]):
        held[ids_ref[n]] += rows_ref[n].astype(F32)
    out_ref[...] = held[...].astype(BF16)


def totals(ids, rows, adapters, after=()):
    shape = (adapters,) + rows.shape[1:]
    if rows.shape[1] % 16:
        hot = (jnp.arange(adapters, dtype=jnp.int32)[:, None] == ids[None, :]).astype(F32)
        return jnp.sum(hot[:, :, None, None] * rows.astype(F32)[None], axis=1).astype(BF16)
    return pl.pallas_call(
        total_kernel,
        grid_spec=pltpu.PrefetchScalarGridSpec(
            num_scalar_prefetch=1,
            grid=(1,),
            in_specs=[pl.BlockSpec(rows.shape, lambda i, c: (0, 0, 0))]
            + [pl.BlockSpec(memory_space=pl.ANY)] * len(after),
            out_specs=pl.BlockSpec(shape, lambda i, c: (0, 0, 0)),
            scratch_shapes=[pltpu.VMEM(shape, F32)],
        ),
        out_shape=jax.ShapeDtypeStruct(shape, BF16),
        compiler_params=pltpu.CompilerParams(vmem_limit_bytes=32 * 1024 * 1024),
        cost_estimate=pl.CostEstimate(flops=0, bytes_accessed=5_000_000, transcendentals=0),
        name="totals",
    )(ids, rows, *after)


def add_kernel(first_ref, second_ref, third_ref, *refs):
    total = first_ref[...] + second_ref[...].astype(F32) + third_ref[...].astype(F32)
    refs[-1][...] = total.astype(BF16)


def add_up(first, second, third, after=()):
    block, count = row_blocks(first)
    return pl.pallas_call(
        add_kernel,
        grid=(count,),
        in_specs=[block] * 3 + [pl.BlockSpec(memory_space=pl.ANY)] * len(after),
        out_specs=block,
        out_shape=jax.ShapeDtypeStruct(first.shape, BF16),
        compiler_params=pltpu.CompilerParams(vmem_limit_bytes=16 * 1024 * 1024),
        name="add_up",
    )(first, second, third, *after)


def unpack_kernel(rows_ref, *refs, share):
    a1_ref, b1_ref, a2_ref, b2_ref = refs[-4:]
    halves = a1_ref.shape[-1] // UNIT
    record = 4 * RANK * halves
    for e in range(rows_ref.shape[0] * share // record):
        unit = []
        for n in range(4 * halves):
            at = e * record + n * RANK
            unit.append(rows_ref[at // share, 0, at % share : at % share + RANK, :].astype(F32))
        for half in range(halves):
            at = slice(half * UNIT, (half + 1) * UNIT)
            a1_ref[0, e, 0:RANK, at] = unit[half]
            a1_ref[0, e, RANK:, at] = unit[halves + half]
            b2_ref[0, e, :, at] = unit[2 * halves + half]
        last = jnp.concatenate(unit[3 * halves :], axis=1)
        b1_ref[0, e, 0] = last[:, :FF]
        b1_ref[0, e, 1] = last[:, FF : 2 * FF]
        a2_ref[0, e] = last[:, 2 * FF :]


def unpack_grads(gathered, experts, first, held, width):
    ranks, adapters, share, _ = gathered.shape
    halves = width // UNIT
    record = 4 * RANK * halves
    if share % 16:
        flat = gathered.swapaxes(0, 1).reshape(adapters, experts, 4, halves, RANK, UNIT)
        flat = flat.swapaxes(3, 4).reshape(adapters, experts, 4 * RANK, width).astype(F32)
        last = flat[:, :, 3 * RANK :]
        return (
            flat[:, :, : 2 * RANK],
            jnp.stack([last[..., :FF], last[..., FF : 2 * FF]], axis=2),
            last[..., 2 * FF :],
            flat[:, :, 2 * RANK : 3 * RANK],
        )
    together = 1
    while together * share % record:
        together += 1
    each = together * share // record
    skip = first // each
    return pl.pallas_call(
        functools.partial(unpack_kernel, share=share),
        grid=(adapters, ranks // together),
        in_specs=[pl.BlockSpec((together, 1, share, UNIT), lambda a, i: (i, a, 0, 0))]
        + [pl.BlockSpec(memory_space=pl.ANY)] * len(held),
        out_specs=[
            pl.BlockSpec((1, each, 2 * RANK, width), lambda a, i: (a, i + skip, 0, 0)),
            pl.BlockSpec((1, each, 2, RANK, FF), lambda a, i: (a, i + skip, 0, 0, 0)),
            pl.BlockSpec((1, each, RANK, FF), lambda a, i: (a, i + skip, 0, 0)),
            pl.BlockSpec((1, each, RANK, width), lambda a, i: (a, i + skip, 0, 0)),
        ],
        out_shape=[
            jax.ShapeDtypeStruct((adapters, experts, 2 * RANK, width), F32),
            jax.ShapeDtypeStruct((adapters, experts, 2, RANK, FF), F32),
            jax.ShapeDtypeStruct((adapters, experts, RANK, FF), F32),
            jax.ShapeDtypeStruct((adapters, experts, RANK, width), F32),
        ],
        input_output_aliases={1 + n: n for n in range(len(held))},
        compiler_params=pltpu.CompilerParams(
            vmem_limit_bytes=40 * 1024 * 1024, dimension_semantics=("arbitrary", "arbitrary")
        ),
        cost_estimate=pl.CostEstimate(flops=0, bytes_accessed=30_000_000, transcendentals=0),
        name="unpack",
    )(gathered, *held)


def swap_pairs(size):
    return [(i, i ^ 1) for i in range(size)]


def from_others(piece):
    groups = lax.axis_size("grp")
    if groups == 2:
        return lax.ppermute(piece, "grp", swap_pairs(2))
    rows = piece.shape[0]
    every = lax.all_gather(piece, "grp", axis=0, tiled=True)
    return jnp.roll(every, -lax.axis_index("grp") * rows, axis=0)[rows:]


def owners_terms(near, far):
    if lax.axis_size("grp") == 2:
        return near, lax.ppermute(far, "grp", swap_pairs(2))
    return to_owners(near, far), jnp.zeros_like(near)


def to_owners(near, far):
    groups = lax.axis_size("grp")
    if groups == 2:
        return near.astype(F32) + lax.ppermute(far, "grp", swap_pairs(2)).astype(F32)
    every = jnp.roll(jnp.concatenate([near, far], axis=0), lax.axis_index("grp") * near.shape[0], axis=0)
    return lax.psum_scatter(every, "grp", scatter_dimension=0, tiled=True).astype(F32)


def in_order(near, far):
    if lax.axis_size("grp") != 2:
        return jnp.roll(jnp.concatenate([near, far], axis=0), lax.axis_index("grp") * near.shape[0], axis=0)
    ahead = lax.axis_index("grp") == 0
    return jnp.where(ahead, jnp.concatenate([near, far], axis=0), jnp.concatenate([far, near], axis=0))


def fetch_halves(half, after):
    groups = lax.axis_size("grp")
    member = lax.axis_index("grp")
    if groups != 2:
        return [(from_others(half), None)]
    rows = half.shape[0] // 2
    core = lax.axis_index("rep") % 2
    mine = delayed(lax.dynamic_slice_in_dim(half, core * rows, rows, 0), after)
    got = lax.ppermute(mine, "grp", swap_pairs(2))
    other = lax.ppermute(got, "rep", swap_pairs(lax.axis_size("rep")))
    away = (1 - member) * 2 * rows
    return [(got, away + core * rows), (other, away + (1 - core) * rows)]


def fetch_wide(half, note=None):
    reps = lax.axis_size("rep")
    if lax.axis_size("grp") != 2 or half.shape[0] % (reps * 16):
        notes = None if note is None else lax.all_gather(note, "rep", axis=0)
        far = from_others(half)
        return far, notes, half
    rows = half.shape[0] // reps
    mine = lax.dynamic_slice_in_dim(half, lax.axis_index("rep") * rows, rows, 0)
    got = lax.ppermute(mine, "grp", swap_pairs(2))
    if note is None:
        return lax.all_gather(got, "rep", axis=0, tiled=True), None, mine
    noted = jnp.concatenate([got, jnp.broadcast_to(note[None], (8, note.shape[0]))], axis=0)
    every = lax.all_gather(noted, "rep", axis=0)
    return every[:, :rows].reshape(half.shape), every[:, rows], mine


def columns(rows, start, count):
    return lax.dynamic_slice_in_dim(rows, start, count, 1)


def delayed_kernel(rows_ref, *refs):
    refs[-1][...] = rows_ref[...]


def row_blocks(rows):
    count = 4 if rows.shape[0] % 64 == 0 else 1
    shape = (rows.shape[0] // count,) + rows.shape[1:]
    return pl.BlockSpec(shape, lambda i: (i,) + (0,) * (rows.ndim - 1)), count


def delayed(rows, after):
    block, count = row_blocks(rows)
    return pl.pallas_call(
        delayed_kernel,
        grid=(count,),
        in_specs=[block] + [pl.BlockSpec(memory_space=pl.ANY)] * len(after),
        out_specs=block,
        out_shape=jax.ShapeDtypeStruct(rows.shape, rows.dtype),
        compiler_params=pltpu.CompilerParams(vmem_limit_bytes=16 * 1024 * 1024),
        name="delayed",
    )(rows, *after)


def local(
    tokens,
    cotangent,
    routes,
    padding,
    parents,
    adapter_ids,
    w_query,
    w_keyval,
    w_output,
    w_router,
    gain_attn,
    gain_ffn,
    w_gateup,
    w_down,
    a_qkv,
    b_query,
    b_keyval,
    a_output,
    b_output,
    a_router,
    b_router,
    a_gateup,
    b_gateup,
    a_down,
    b_down,
):
    groups = lax.axis_size("grp")
    reps = lax.axis_size("rep")
    member = lax.axis_index("grp")
    count = tokens.shape[0]
    width = tokens.shape[1]
    part = width // groups
    tree_length = count * groups
    experts_dev = w_gateup.shape[0]
    experts = experts_dev * groups
    capacity = count * TOPK * 7 // (experts * 5)
    cap = -(-capacity // 16) * 16
    kv_width = KEY_VALUE_HEADS * HEAD_SIZE
    chosen = adapter_ids[0]
    first = member * count
    adapters = a_qkv.shape[0]

    kv_part = kv_width // groups
    odd = jnp.concatenate([b_keyval[chosen, 0], b_keyval[chosen, 1], b_router[chosen]], axis=1)
    small = jnp.concatenate(
        [
            a_qkv.swapaxes(1, 2)[chosen],
            b_query[chosen],
            a_output.swapaxes(1, 2)[chosen],
            b_output[chosen],
            a_router.swapaxes(1, 2)[chosen],
            jnp.pad(odd, ((0, 0), (0, part - odd.shape[1]))),
            w_router.T,
            gain_attn[None],
            gain_ffn[None],
            jnp.pad(padding.astype(BF16)[None], ((0, 5), (0, part - count))),
        ],
        axis=0,
    )
    if groups == 2:
        small_far = from_others(small)
        joined = jnp.where(
            member == 0,
            jnp.concatenate([small, small_far], axis=1),
            jnp.concatenate([small_far, small], axis=1),
        )
    else:
        joined = in_order(small[None], from_others(small[None])).swapaxes(0, 1).reshape(-1, width)
    qkv_in = joined[: 3 * RANK]
    query_out = joined[3 * RANK : 4 * RANK]
    output_in = joined[4 * RANK : 5 * RANK]
    output_out = joined[5 * RANK : 6 * RANK]
    router_in = joined[6 * RANK : 7 * RANK]
    odd = joined[7 * RANK : 8 * RANK].reshape(RANK, groups, part)
    keyval_out = [odd[:, :, n * kv_part : (n + 1) * kv_part].reshape(RANK, kv_width) for n in range(2)]
    router_out = odd[:, :, 2 * kv_part : 2 * kv_part + experts_dev].reshape(RANK, experts)
    router_full = joined[8 * RANK : 8 * RANK + experts]
    last = 8 * RANK + experts
    attn_gain = joined[last]
    ffn_gain = joined[last + 1]
    pad_all = joined[last + 2].reshape(groups, part)[:, :count].reshape(-1)
    attn_gain = attn_gain.astype(F32)
    ffn_gain = ffn_gain.astype(F32)
    query_far, _, query_piece = fetch_wide(w_query)
    keyval_far = fetch_halves(w_keyval, (query_piece,))
    query_full = in_order(w_query, query_far)
    if groups == 2:
        (got, _), (other, _) = keyval_far
        ahead = lax.axis_index("rep") % 2 == 0
        keyval_full = in_order(
            w_keyval, jnp.where(ahead, jnp.concatenate([got, other], 0), jnp.concatenate([other, got], 0))
        )
    else:
        keyval_full = in_order(w_keyval, keyval_far[0][0])
    note = (jnp.arange(width, dtype=jnp.int32) == chosen).astype(BF16)
    output_far, notes, _ = fetch_wide(w_output, note)
    output_full = in_order(w_output, output_far)
    ids_all = jnp.sum(
        notes[:, :adapters].astype(jnp.int32) * jnp.arange(adapters, dtype=jnp.int32), axis=1
    )
    routes_far = from_others(routes)
    maps = (a_gateup.swapaxes(2, 3), b_gateup, a_down.swapaxes(2, 3), b_down)
    calls = 2 if experts_dev % (4 * FLUSH) == 0 and groups == 2 else 1
    each = experts_dev // calls
    some = -(-each // 2)

    def fold(call, late, held, after):
        at = some if late else 0
        count = each - some if late else some
        return fold_adapters(
            adapter_ids, w_gateup, w_down, *maps, call * each + at, count, held, at, each, after
        )

    first_fold = fold(0, False, (), ())

    tokens_f = tokens.astype(F32)
    normed = rms_norm(tokens_f, attn_gain).astype(BF16)
    low_rank = product_back(normed, qkv_in).astype(BF16)
    own_columns = columns(normed, member * part, part)
    if groups == 2:
        keyvals = product(own_columns, w_keyval)
        for piece, start in keyval_far:
            keyvals = keyvals + product(columns(normed, start, piece.shape[0]), piece)
    else:
        keyvals = product(normed, keyval_full)
    keyvals = jnp.concatenate(
        [
            keyvals[:, :kv_width] + product(low_rank[:, RANK : 2 * RANK], keyval_out[0]),
            keyvals[:, kv_width:] + product(low_rank[:, 2 * RANK :], keyval_out[1]),
        ],
        axis=1,
    ).astype(BF16)
    folded = [fold(0, True, first_fold, (keyvals,))]
    keyvals_far = from_others(keyvals)
    upstream_far = from_others(delayed(cotangent, (keyvals_far,)))
    if groups == 2:
        query_rows = product(own_columns, w_query) + product(columns(normed, (1 - member) * part, part), query_far)
    else:
        query_rows = product(normed, query_full)
    query_rows = (query_rows + product(low_rank[:, :RANK], query_out)).astype(BF16)
    pad_whole = jnp.roll(pad_all, -first)
    listing, steps, own_bias, live = visits(parents[0], pad_whole[:count], pad_whole[count:], first)
    attended, logs = run_attention(listing, steps, query_rows, keyvals, keyvals_far, own_bias, live)
    out_rank = product_back(attended, output_in).astype(BF16)
    middle = tokens_f + product(attended, output_full) + product(out_rank, output_out)
    normed_ffn = rms_norm(middle, ffn_gain).astype(BF16)
    if calls == 2:
        folded.append(fold(1, True, fold(1, False, (), (normed_ffn,)), ()))
    router_rank = product_back(normed_ffn, router_in).astype(BF16)
    logits = product_back(normed_ffn, router_full) + product(router_rank, router_out)

    labels = jnp.arange(experts, dtype=jnp.int32)
    named = jnp.any(routes[:, :, None] == labels, axis=1)
    best = jnp.max(jnp.where(named, logits, -jnp.inf), axis=1, keepdims=True)
    powers = jnp.where(named, jnp.exp(jnp.where(named, logits, best) - best), 0.0)
    gates = powers / jnp.sum(powers, axis=1, keepdims=True)

    mine = member * experts_dev + jnp.arange(experts_dev, dtype=jnp.int32)
    routes_all = jnp.concatenate([routes, routes_far], axis=0).reshape(groups, count, TOPK)
    hits = jnp.any(routes_all[:, :, :, None] == mine, axis=2)
    before = (jnp.arange(count)[:, None] > jnp.arange(count)[None, :]).astype(BF16)
    ranks = jnp.einsum("ts,gse->get", before, hits.astype(BF16), preferred_element_type=F32)
    places = jnp.where(hits.transpose(0, 2, 1), ranks.astype(jnp.int32), -1).transpose(1, 0, 2)

    rows_far = from_others(normed_ffn)
    gates_t = gates.T
    if groups == 2:
        gates_near = lax.dynamic_slice_in_dim(gates_t, member * experts_dev, experts_dev, 0)
        gates_far = from_others(lax.dynamic_slice_in_dim(gates_t, (1 - member) * experts_dev, experts_dev, 0))
        gates_mine = jnp.stack([gates_near, gates_far], axis=1)
    else:
        gates_mine = lax.all_gather(gates_t, "grp", axis=0)
        gates_mine = lax.dynamic_slice_in_dim(gates_mine, member * experts_dev, experts_dev, 1)
        gates_mine = jnp.roll(gates_mine, -member, axis=0).transpose(1, 0, 2)
    sums = ()
    gate_terms = []
    spread = []
    for n in range(calls):
        *sums, terms, grads = run_experts(
            adapter_ids,
            normed_ffn,
            rows_far,
            cotangent,
            upstream_far,
            places,
            gates_mine,
            *folded[n],
            *maps,
            tuple(sums),
            cap,
            n * each,
            each,
        )
        gate_terms.append(terms)
        if n:
            sums[3], swapped = lax.optimization_barrier((sums[3], swapped))
            spread.append(lax.all_gather(totals(ids_all, swapped, adapters), "rep", axis=0))
        swapped = lax.all_to_all(
            grads.reshape(reps, -1, UNIT), "rep", split_axis=0, concat_axis=0, tiled=True
        )
    result_near, result_far, d_near, d_far = sums
    part_gates = jnp.concatenate(gate_terms, axis=0)
    if groups == 2:
        d_gates = in_order(part_gates[:, 0], from_others(part_gates[:, 1]))
    else:
        d_gates = jnp.roll(part_gates, member, axis=1)
        d_gates = lax.all_to_all(d_gates, "grp", split_axis=1, concat_axis=0, tiled=True)
    d_gates = d_gates.reshape(experts, count).T
    d_sum = to_owners(d_near, d_far)
    upstream = cotangent.astype(F32)
    d_logits = (gates * (d_gates - jnp.sum(gates * d_gates, axis=1, keepdims=True))).astype(BF16)

    d_router_rank = product_back(d_logits, router_out).astype(BF16)
    d_normed_ffn = d_sum + product(d_logits, router_full) + product(d_router_rank, router_in)
    grad_router_out = product_outer(router_rank, d_logits)
    grad_router_in = product_outer(d_router_rank, normed_ffn)
    d_middle = upstream + rms_back(middle, ffn_gain, d_normed_ffn)
    d_attn = d_middle.astype(BF16)
    d_out_rank = product_back(d_attn, output_out).astype(BF16)
    attended_gradient = (product_back(d_attn, output_full) + product(d_out_rank, output_in)).astype(BF16)
    grad_output_out = product_outer(out_rank, d_attn)
    grad_output_in = product_outer(d_out_rank, attended)
    parts = []
    pairs = KEY_VALUE_HEADS // 4
    for n in range(2):
        d_q, *d_kv = run_attention_back(
            listing,
            steps,
            query_rows,
            keyvals,
            keyvals_far,
            own_bias,
            live,
            attended,
            attended_gradient,
            logs,
            n * pairs,
            pairs,
            (last,) if n else (),
        )
        d_kv = to_owners(jnp.concatenate(d_kv[:2], axis=1), jnp.concatenate(d_kv[2:], axis=1)).astype(BF16)
        parts.append((d_q, d_kv[:, : kv_width // 2], d_kv[:, kv_width // 2 :]))
        if n == 0:
            last = totals(ids_all, swapped, adapters, after=(d_q,))
            spread.append(lax.all_gather(last, "rep", axis=0))
    mixture = owners_terms(result_near, delayed(result_far, (parts[1][1],)))
    d_queries, d_keys, d_values = [jnp.concatenate(pair, axis=1) for pair in zip(*parts)]
    d_keyvals = jnp.concatenate([d_keys, d_values], axis=1)
    d_rank_qkv = jnp.concatenate(
        [
            product_back(d_queries, query_out),
            product_back(d_keys, keyval_out[0]),
            product_back(d_values, keyval_out[1]),
        ],
        axis=-1,
    ).astype(BF16)
    d_normed = (
        product_back(d_queries, query_full)
        + product_back(d_keyvals, keyval_full)
        + product(d_rank_qkv, qkv_in)
    )
    grad_input = (d_middle + rms_back(tokens_f, attn_gain, d_normed)).astype(BF16)
    grad_qkv_in = product_outer(d_rank_qkv, normed)
    grad_query_out = product_outer(low_rank[:, :RANK], d_queries)
    grad_keyval_out = jnp.stack(
        [
            product_outer(low_rank[:, RANK : 2 * RANK], d_keys),
            product_outer(low_rank[:, 2 * RANK :], d_values),
        ],
        axis=0,
    )

    expert_grads = ()
    for n in range(calls):
        expert_grads = unpack_grads(spread[n], experts_dev, n * each, tuple(expert_grads), width)
    grad_a_gateup, grad_b_gateup, grad_a_down, grad_b_down = expert_grads

    tall = jnp.concatenate(
        [grad_qkv_in, grad_query_out, grad_output_in, grad_output_out, grad_router_in], axis=0
    ).astype(BF16)
    high = tall.shape[0]
    tall = tall.reshape(high, groups, part).swapaxes(0, 1)
    wide = [
        grad_keyval_out[0].reshape(RANK, groups, kv_part),
        grad_keyval_out[1].reshape(RANK, groups, kv_part),
        grad_router_out.reshape(RANK, groups, experts_dev),
        jnp.zeros((RANK, groups, part - 2 * kv_part - experts_dev), F32),
    ]
    wide = jnp.concatenate(wide, axis=2).astype(BF16).swapaxes(0, 1)
    dense = jnp.concatenate([tall, wide], axis=1).reshape(groups, reps, -1, part).swapaxes(0, 1)
    dense = dense.reshape(reps * groups, -1, part)
    result = add_up(middle, *mixture, after=(dense,))
    dense = lax.all_to_all(dense, ("rep", "grp"), split_axis=0, concat_axis=0, tiled=True)
    owner_hot = (jnp.arange(adapters, dtype=jnp.int32)[:, None] == jnp.repeat(ids_all, groups)[None, :])
    dense = jnp.sum(jnp.where(owner_hot[:, :, None, None], dense.astype(F32)[None], 0.0), axis=1).astype(BF16)
    dense = lax.all_gather(dense, "rep", axis=0).swapaxes(0, 1).reshape(adapters, -1, part).astype(F32)
    wide = dense[:, high:]
    owned = [
        dense[:, : 3 * RANK],
        dense[:, 3 * RANK : 4 * RANK],
        jnp.stack([wide[:, :, :kv_part], wide[:, :, kv_part : 2 * kv_part]], axis=1),
        dense[:, 4 * RANK : 5 * RANK],
        dense[:, 5 * RANK : 6 * RANK],
        dense[:, 6 * RANK : 7 * RANK],
        wide[:, :, 2 * kv_part : 2 * kv_part + experts_dev],
    ]
    return (
        result,
        grad_input,
        owned[0].swapaxes(1, 2),
        owned[1],
        owned[2],
        owned[3].swapaxes(1, 2),
        owned[4],
        owned[5].swapaxes(1, 2),
        owned[6],
        grad_a_gateup.swapaxes(2, 3),
        grad_b_gateup,
        grad_a_down.swapaxes(2, 3),
        grad_b_down,
    )


def solution(mesh):
    in_specs = (
        P(("rep", "grp"), None),
        P(("rep", "grp"), None),
        P(("rep", "grp"), None),
        P(("rep", "grp")),
        P("rep", None),
        P("rep"),
        P("grp", None),
        P("grp", None),
        P("grp", None),
        P("grp", None),
        P("grp"),
        P("grp"),
        P("grp", None, None),
        P("grp", None, None),
        P(None, "grp", None),
        P(None, None, "grp"),
        P(None, None, None, "grp"),
        P(None, "grp", None),
        P(None, None, "grp"),
        P(None, "grp", None),
        P(None, None, "grp"),
        P(None, "grp", None, None),
        P(None, "grp", None, None, None),
        P(None, "grp", None, None),
        P(None, "grp", None, None),
    )
    out_specs = (
        P(("rep", "grp"), None),
        P(("rep", "grp"), None),
        P(None, "grp", None),
        P(None, None, "grp"),
        P(None, None, None, "grp"),
        P(None, "grp", None),
        P(None, None, "grp"),
        P(None, "grp", None),
        P(None, None, "grp"),
        P(None, "grp", None, None),
        P(None, "grp", None, None, None),
        P(None, "grp", None, None),
        P(None, "grp", None, None),
    )
    return jax.shard_map(local, mesh=mesh, in_specs=in_specs, out_specs=out_specs, check_vma=False)
```

```python
import functools

import jax
import jax.numpy as jnp
from jax import lax
from jax.experimental import pallas as pl
from jax.experimental.pallas import tpu as pltpu
from jax.sharding import PartitionSpec as P

QUERY_HEADS = 24
KEY_VALUE_HEADS = 8
HEAD_SIZE = 64
FF = 512
TOPK = 8
RANK = 16
SEG = 128
FLUSH = 5
UNIT = 768

EPSILON = 1e-05
BF16 = jnp.bfloat16
F32 = jnp.float32


def product(left, right):
    return jnp.dot(left, right, preferred_element_type=F32)


def product_back(left, right):
    return lax.dot_general(left, right, (((1,), (1,)), ((), ())), preferred_element_type=F32)


def product_outer(left, right):
    return lax.dot_general(left, right, (((0,), (0,)), ((), ())), preferred_element_type=F32)


def rms_norm(value_rows, gain):
    return (
        value_rows
        * lax.rsqrt(jnp.mean(value_rows * value_rows, axis=-1, keepdims=True) + EPSILON)
        * gain
    )


def rms_back(value_rows, gain, upstream):
    factor = lax.rsqrt(jnp.mean(value_rows * value_rows, axis=-1, keepdims=True) + EPSILON)
    scaled = value_rows * factor
    incoming = upstream * gain
    return factor * (incoming - scaled * jnp.mean(incoming * scaled, axis=-1, keepdims=True))


def ancestry(parent_row):
    total = parent_row.shape[0]
    labels = jnp.arange(total, dtype=jnp.int32)
    own = labels[:, None] == labels[None, :]
    reached = jnp.logical_or(own, parent_row[:, None] == labels[None, :])
    steps = 1
    while steps < total:
        reached = jnp.any(jnp.logical_and(reached[:, :, None], reached[None, :, :]), axis=1)
        steps *= 2
    return reached.astype(jnp.int32)


def tile_parts(ref_k, seg_a, seg_b):
    return jnp.concatenate(
        [
            ref_k[pl.ds(pl.multiple_of(seg_a * SEG, SEG), SEG), :],
            ref_k[pl.ds(pl.multiple_of(seg_b * SEG, SEG), SEG), :],
        ],
        axis=0,
    )


def fill_doubled(held, near_ref, far_ref, ones=False):
    near = near_ref.shape[0]
    for ref, at in ((near_ref, 0), (far_ref, near)):
        rows = ref[...].astype(F32)
        low = lax.broadcasted_iota(jnp.int32, rows.shape, 1) < HEAD_SIZE
        turned = pltpu.roll(rows, HEAD_SIZE, axis=1)
        there = pl.ds(at, rows.shape[0])
        held[0, there, :] = jnp.where(low, rows, 1.0 if ones else turned).astype(BF16)
        held[1, there, :] = jnp.where(low, turned, 1.0 if ones else rows).astype(BF16)


PLACES = (((0, 0), (0, 1), (1, 0)), ((1, 1), (2, 0), (2, 1)))


def stacked_heads(ref, at, which, scale=None):
    low = lax.broadcasted_iota(jnp.int32, (SEG, 2 * HEAD_SIZE), 1) < HEAD_SIZE
    out = []
    for column, half in PLACES[which]:
        piece = ref[at, column * 2 * HEAD_SIZE : (column + 1) * 2 * HEAD_SIZE].astype(F32)
        if scale is not None:
            piece = piece * scale
        out.append(jnp.where(low if half == 0 else jnp.logical_not(low), piece, 0.0))
    return jnp.concatenate(out, axis=0)


def unstack(first, second):
    low = lax.broadcasted_iota(jnp.int32, (SEG, 2 * HEAD_SIZE), 1) < HEAD_SIZE
    return [
        jnp.where(low, first[0:SEG], first[SEG : 2 * SEG]),
        jnp.where(low, first[2 * SEG :], second[0:SEG]),
        jnp.where(low, second[SEG : 2 * SEG], second[2 * SEG :]),
    ]


def first_bias(own_ref, live_ref, i, seg_b):
    other = jnp.broadcast_to(live_ref[seg_b], (SEG, SEG))
    tile = jnp.concatenate([own_ref[i], other], axis=1)
    return jnp.concatenate([tile] * 3, axis=0)


def next_bias(live_ref, seg_a, seg_b):
    return jnp.concatenate([live_ref[seg_a], live_ref[seg_b]], axis=1)


def attend_kernel(
    list_ref,
    steps_ref,
    q_ref,
    k_ref,
    v_ref,
    k_far,
    v_far,
    own_ref,
    live_ref,
    o_ref,
    l_ref,
    kf,
    vf,
    *,
    here,
    segs,
    scale,
):
    fill_doubled(kf, k_ref, k_far)
    fill_doubled(vf, v_ref, v_far, ones=True)
    lanes = lax.broadcasted_iota(jnp.int32, (SEG, 2 * HEAD_SIZE), 1)
    low = lanes < HEAD_SIZE
    slots = 2 * segs
    for i in range(here):
        at = pl.ds(i * SEG, SEG)
        queries = [stacked_heads(q_ref, at, which, scale).astype(BF16) for which in range(2)]

        def pair_of(t):
            return (
                lax.rem(list_ref[i * slots + 2 * t], segs),
                lax.rem(list_ref[i * slots + 2 * t + 1], segs),
            )

        seg_a, seg_b = pair_of(0)
        bias = first_bias(own_ref, live_ref, i, list_ref[i * slots + 1])
        state = []
        for which in range(2):
            s = product_back(queries[which], tile_parts(kf.at[which], seg_a, seg_b)) + bias
            top = jnp.max(s, axis=1, keepdims=True)
            p = jnp.exp(s - top).astype(BF16)
            state.append((top, product(p, tile_parts(vf.at[which], seg_a, seg_b))))

        def body(t, state):
            bias = next_bias(live_ref, list_ref[i * slots + 2 * t], list_ref[i * slots + 2 * t + 1])
            seg_a, seg_b = pair_of(t)
            out = []
            for which in range(2):
                top, acc = state[which]
                s = product_back(queries[which], tile_parts(kf.at[which], seg_a, seg_b)) + bias
                higher = jnp.maximum(top, jnp.max(s, axis=1, keepdims=True))
                p = jnp.exp(s - higher).astype(BF16)
                acc = acc * jnp.exp(top - higher) + product(p, tile_parts(vf.at[which], seg_a, seg_b))
                out.append((higher, acc))
            return tuple(out)

        state = lax.fori_loop(1, steps_ref[i], body, tuple(state))
        turned = [pltpu.roll(acc, HEAD_SIZE, axis=1) for _, acc in state]
        logs = jnp.zeros((SEG, 2 * HEAD_SIZE), F32)
        heads = []
        for which in range(2):
            for n, (_, half) in enumerate(PLACES[which]):
                rows = slice(n * SEG, (n + 1) * SEG)
                plain, other = state[which][1][rows], turned[which][rows]
                heads.append(plain / other if half == 0 else other / plain)
                total = jnp.where(low, other, plain)
                logs = jnp.where(lanes == which * 3 + n, state[which][0][rows] + jnp.log(total), logs)
        l_ref[0, at, :] = logs
        for column in range(3):
            o_ref[at, column * 2 * HEAD_SIZE : (column + 1) * 2 * HEAD_SIZE] = jnp.where(
                low, heads[2 * column], heads[2 * column + 1]
            ).astype(BF16)


def attend_back_kernel(
    list_ref,
    steps_ref,
    q_ref,
    k_ref,
    v_ref,
    k_far,
    v_far,
    own_ref,
    live_ref,
    o_ref,
    do_ref,
    l_ref,
    *refs,
    here,
    segs,
    scale,
    after,
):
    dq_ref, dk_ref, dv_ref, dk_far, dv_far, kf, vf, dkf, dvf = refs[after:]
    fill_doubled(kf, k_ref, k_far)
    fill_doubled(vf, v_ref, v_far)
    dkf[...] = jnp.zeros_like(dkf)
    dvf[...] = jnp.zeros_like(dvf)
    slots = 2 * segs
    for i in range(here):
        at = pl.ds(i * SEG, SEG)
        fixed = []
        for which in range(2):
            d_o = stacked_heads(do_ref, at, which)
            fixed.append(
                (
                    stacked_heads(q_ref, at, which, scale).astype(BF16),
                    d_o.astype(BF16),
                    jnp.sum(d_o * stacked_heads(o_ref, at, which), axis=1, keepdims=True),
                    jnp.concatenate(
                        [l_ref[0, at, which * 3 + n : which * 3 + n + 1] for n in range(3)], axis=0
                    ),
                )
            )

        def step(t, bias):
            seg_a = lax.rem(list_ref[i * slots + 2 * t], segs)
            seg_b = lax.rem(list_ref[i * slots + 2 * t + 1], segs)
            out = []
            for which, (q, d_o, delta, log_total) in enumerate(fixed):
                k = tile_parts(kf.at[which], seg_a, seg_b)
                v = tile_parts(vf.at[which], seg_a, seg_b)
                p = jnp.exp(product_back(q, k) + bias - log_total)
                d_p = product_back(d_o, v)
                d_s = (p * (d_p - delta)).astype(BF16)
                d_v = product_outer(p.astype(BF16), d_o)
                d_k = product_outer(d_s, q)
                for n, seg in enumerate((seg_a, seg_b)):
                    rows = pl.ds(pl.multiple_of(seg * SEG, SEG), SEG)
                    dkf[which, rows, :] += d_k[n * SEG : (n + 1) * SEG]
                    dvf[which, rows, :] += d_v[n * SEG : (n + 1) * SEG]
                out.append(product(d_s, k))
            return tuple(out)

        d_q = step(0, first_bias(own_ref, live_ref, i, list_ref[i * slots + 1]))

        def body(t, carry):
            bias = next_bias(live_ref, list_ref[i * slots + 2 * t], list_ref[i * slots + 2 * t + 1])
            return tuple(a + b for a, b in zip(carry, step(t, bias)))

        d_q = lax.fori_loop(1, steps_ref[i], body, d_q)
        for column, piece in enumerate(unstack(*d_q)):
            dq_ref[at, column * 2 * HEAD_SIZE : (column + 1) * 2 * HEAD_SIZE] = (piece * scale).astype(BF16)
    near = dk_ref.shape[0]
    for out, far_out, held in ((dk_ref, dk_far, dkf), (dv_ref, dv_far, dvf)):
        first = held[0] + pltpu.roll(held[0], HEAD_SIZE, axis=1)
        second = held[1] + pltpu.roll(held[1], HEAD_SIZE, axis=1)
        low = lax.broadcasted_iota(jnp.int32, first.shape, 1) < HEAD_SIZE
        total = jnp.where(low, first, second).astype(BF16)
        out[...] = total[:near]
        far_out[...] = total[near:]


def visits(parent_row, pad_near, pad_far, first):
    count = pad_near.shape[0]
    tree_length = count + pad_far.shape[0]
    segs = tree_length // SEG
    here = count // SEG
    own = jnp.arange(here, dtype=jnp.int32)
    labels = jnp.arange(segs, dtype=jnp.int32)
    table = lax.dynamic_slice_in_dim(ancestry(parent_row), first // SEG, here, 0)
    turn = (labels[:, None] == (labels[None, :] + segs - first // SEG) % segs).astype(F32)
    table = product_back(table.astype(F32), turn).astype(jnp.int32)
    table = jnp.where(labels[None, :] == own[:, None], 0, table)
    order = jnp.sum(jnp.where(labels[None, :] <= labels[:, None], table[:, None, :], 0), axis=2)
    spots = jnp.arange(1, 2 * segs, dtype=jnp.int32)
    found = jnp.logical_and(table[:, None, :] > 0, order[:, None, :] == spots[None, :, None])
    listing = jnp.where(jnp.any(found, axis=2), jnp.sum(found * labels, axis=2), segs)
    listing = jnp.concatenate([own[:, None], listing], axis=1).astype(jnp.int32)
    steps = (2 + order[:, -1]) // 2
    live = jnp.where(jnp.concatenate([pad_near, pad_far]) > 0, 0.0, -1e30).astype(F32).reshape(segs, SEG)
    places = jnp.arange(SEG)
    causal = places[None, :] <= places[:, None]
    same = places[None, :] == places[:, None]
    own_bias = jnp.where(same[None], 0.0, jnp.where(causal[None], live[:here, None, :], -1e30))
    live = jnp.concatenate([live, jnp.full((1, SEG), -1e30, F32)], axis=0)[:, None, :]
    return listing.reshape(-1), steps.astype(jnp.int32), own_bias, live


def attention_specs(count, far, here, segs, skip=0):
    narrow = 2 * HEAD_SIZE
    shift = KEY_VALUE_HEADS // 2 + skip
    return [
        pl.BlockSpec((count, 3 * narrow), lambda h, a, b: (0, h + skip)),
        pl.BlockSpec((count, narrow), lambda h, a, b: (0, h + skip)),
        pl.BlockSpec((count, narrow), lambda h, a, b: (0, h + shift)),
        pl.BlockSpec((far, narrow), lambda h, a, b: (0, h + skip)),
        pl.BlockSpec((far, narrow), lambda h, a, b: (0, h + shift)),
        pl.BlockSpec((here, SEG, SEG), lambda h, a, b: (0, 0, 0)),
        pl.BlockSpec((segs + 1, 1, SEG), lambda h, a, b: (0, 0, 0)),
    ]


def run_attention(listing, steps, queries, near, far, own_bias, live):
    count, width = queries.shape
    tree_length = count + far.shape[0]
    here, segs = count // SEG, tree_length // SEG
    pairs = KEY_VALUE_HEADS // 2
    narrow = 2 * HEAD_SIZE
    return pl.pallas_call(
        functools.partial(attend_kernel, here=here, segs=segs, scale=HEAD_SIZE ** (-0.5)),
        grid_spec=pltpu.PrefetchScalarGridSpec(
            num_scalar_prefetch=2,
            grid=(pairs,),
            in_specs=attention_specs(count, far.shape[0], here, segs),
            out_specs=[
                pl.BlockSpec((count, 3 * narrow), lambda h, a, b: (0, h)),
                pl.BlockSpec((1, count, narrow), lambda h, a, b: (h, 0, 0)),
            ],
            scratch_shapes=[pltpu.VMEM((2, tree_length, narrow), BF16)] * 2,
        ),
        out_shape=[
            jax.ShapeDtypeStruct((count, width), BF16),
            jax.ShapeDtypeStruct((pairs, count, narrow), F32),
        ],
        compiler_params=pltpu.CompilerParams(
            vmem_limit_bytes=60 * 1024 * 1024, dimension_semantics=("arbitrary",)
        ),
        cost_estimate=pl.CostEstimate(flops=40_000_000_000, bytes_accessed=8_000_000, transcendentals=10_000_000),
        name="attention",
    )(listing, steps, queries, near, near, far, far, own_bias, live)


def run_attention_back(
    listing, steps, queries, near, far, own_bias, live, attended, gradient, logs, skip, pairs, after=()
):
    count = queries.shape[0]
    tree_length = count + far.shape[0]
    here, segs = count // SEG, tree_length // SEG
    narrow = 2 * HEAD_SIZE
    rows = pl.BlockSpec((count, 3 * narrow), lambda h, a, b: (0, h + skip))
    outs = [pl.BlockSpec((count, narrow), lambda h, a, b: (0, h))] * 2
    outs += [pl.BlockSpec((far.shape[0], narrow), lambda h, a, b: (0, h))] * 2
    return pl.pallas_call(
        functools.partial(
            attend_back_kernel, here=here, segs=segs, scale=HEAD_SIZE ** (-0.5), after=len(after)
        ),
        grid_spec=pltpu.PrefetchScalarGridSpec(
            num_scalar_prefetch=2,
            grid=(pairs,),
            in_specs=attention_specs(count, far.shape[0], here, segs, skip)
            + [rows, rows, pl.BlockSpec((1, count, narrow), lambda h, a, b: (h + skip, 0, 0))]
            + [pl.BlockSpec(memory_space=pl.ANY)] * len(after),
            out_specs=[pl.BlockSpec((count, 3 * narrow), lambda h, a, b: (0, h))] + outs,
            scratch_shapes=[pltpu.VMEM((2, tree_length, narrow), BF16)] * 2
            + [pltpu.VMEM((2, tree_length, narrow), F32)] * 2,
        ),
        out_shape=[jax.ShapeDtypeStruct((count, 3 * pairs * narrow), BF16)]
        + [jax.ShapeDtypeStruct((count, pairs * narrow), BF16)] * 2
        + [jax.ShapeDtypeStruct((far.shape[0], pairs * narrow), BF16)] * 2,
        compiler_params=pltpu.CompilerParams(
            vmem_limit_bytes=60 * 1024 * 1024, dimension_semantics=("arbitrary",)
        ),
        cost_estimate=pl.CostEstimate(
            flops=17_000_000_000 * pairs, bytes_accessed=3_000_000 * pairs, transcendentals=0
        ),
        name="attention_back",
    )(listing, steps, queries, near, near, far, far, own_bias, live, attended, gradient, logs, *after)


def expert_kernel(
    chosen_ref,
    most_ref,
    x_ref,
    x_far,
    g_ref,
    g_far,
    pos_ref,
    gate_ref,
    w1_ref,
    w2_ref,
    a1_ref,
    b1_ref,
    a2_ref,
    b2_ref,
    *refs,
    blocks,
    rows_block,
    cap,
    flush,
    carried,
    first,
):
    held = refs[:4] if carried else ()
    (
        r_out,
        r_far,
        d_out,
        d_far,
        dg_out,
        grad_out,
        hot_s,
        o_s,
        dx_s,
        accr,
        accd,
        x_s,
        g_s,
        gate_s,
        b1_s,
        dgu_s,
    ) = refs[len(held) :]
    e = pl.program_id(0)
    slot = lax.rem(e, flush)
    width = x_ref.shape[-1]
    halves = width // UNIT

    @pl.when(e == 0)
    def _():
        b1_s[...] = jnp.zeros_like(b1_s)
        o_s[...] = jnp.zeros_like(o_s)
        dx_s[...] = jnp.zeros_like(dx_s)
        if carried:
            for n, acc in enumerate((accr, accd)):
                acc[0:rows_block, :] = held[2 * n][...].astype(F32)
                acc[rows_block:, :] = held[2 * n + 1][...].astype(F32)
        else:
            accr[...] = jnp.zeros_like(accr)
            accd[...] = jnp.zeros_like(accd)

    at = pl.multiple_of(slot * cap, 16)
    b1_s[0:RANK, 0:FF] = b1_ref[0, 0, 0]
    b1_s[RANK : 2 * RANK, FF : 2 * FF] = b1_ref[0, 0, 1]
    most = most_ref[e + first]

    def run(used):
        for b in range(blocks):
            rows_ref, g_rows_ref = (x_ref, g_ref) if b == 0 else (x_far, g_far)
            here = pl.ds(max(b - 1, 0) * rows_block, rows_block)
            there = pl.ds(b * used, used)
            places = lax.broadcasted_iota(jnp.int32, (used, rows_block), 0)
            hit = places == pos_ref[0, b : b + 1, :]
            hot = hit.astype(F32).astype(BF16)
            hot_s[b, pl.ds(at, used), :] = hot
            if used < cap:
                hot_s[b, pl.ds(at + used, cap - used), :] = jnp.zeros((cap - used, rows_block), BF16)
            x_s[there, :] = product(hot, rows_ref[here, :]).astype(BF16)
            g_s[there, :] = product(hot, g_rows_ref[here, :]).astype(BF16)
            gate_s[there, :] = jnp.sum(
                jnp.where(hit, gate_ref[0, b : b + 1, :], 0.0), axis=1, keepdims=True
            )

        rows = slice(0, blocks * used)
        x = x_s[rows]
        gate_col = gate_s[rows]
        rank_in = product_back(a1_ref[0, 0], x).astype(BF16)
        pre = product(x, w1_ref[0])
        gate_pre = pre[:, :FF]
        up_pre = pre[:, FF:]
        sig = 1.0 / (1.0 + jnp.exp(-gate_pre))
        act = gate_pre * sig
        hidden = (act * up_pre).astype(BF16)
        rank_down = product_back(a2_ref[0, 0], hidden).astype(BF16)
        out = product(hidden, w2_ref[0]).astype(BF16).astype(F32)
        g = g_s[rows].astype(F32)
        d_gate_col = jnp.sum(g * out, axis=1, keepdims=True)
        out = (gate_col * out).astype(BF16)
        d_exp = (gate_col * g).astype(BF16)
        d_rank_down = product_back(b2_ref[0, 0], d_exp).astype(BF16)
        d_hidden = product_back(d_exp, w2_ref[0])
        dgu_s[rows, :FF] = (d_hidden * up_pre * sig * (1.0 + gate_pre * (1.0 - sig))).astype(BF16)
        dgu_s[rows, FF:] = (d_hidden * act).astype(BF16)
        dgu = dgu_s[rows]
        d_rank_in = product_back(b1_s[...], dgu).astype(BF16)
        dx = product_back(dgu, w1_ref[0]).astype(BF16)
        for b in range(blocks):
            o_s[b, pl.ds(at, used), :] = out[b * used : (b + 1) * used]
            dx_s[b, pl.ds(at, used), :] = dx[b * used : (b + 1) * used]
            places = lax.broadcasted_iota(jnp.int32, (used, rows_block), 0)
            hit = places == pos_ref[0, b : b + 1, :]
            dg_out[0, b : b + 1, :] = jnp.sum(
                jnp.where(hit, d_gate_col[b * used : (b + 1) * used], 0.0), axis=0, keepdims=True
            )

        grad_a1 = product(d_rank_in, x)
        grad_b1 = product(rank_in, dgu)
        grad_a2 = product(d_rank_down, hidden)
        grad_b2 = product(rank_down, d_exp)
        last = jnp.concatenate([grad_b1[:RANK, :FF], grad_b1[RANK:, FF:], grad_a2], axis=1)
        for n, piece in enumerate((grad_a1[:RANK], grad_a1[RANK:], grad_b2, last)):
            for half in range(halves):
                rows = slice((n * halves + half) * RANK, (n * halves + half + 1) * RANK)
                grad_out[0, rows, :] = piece[:, half * UNIT : (half + 1) * UNIT].astype(BF16)


    sizes = sorted({min(cap, size) for size in (96, 112, cap)})
    for n, size in enumerate(sizes):
        fits = most <= size
        if n + 1 == len(sizes):
            fits = most > sizes[n - 1] if n else most >= 0
        elif n:
            fits = jnp.logical_and(fits, most > sizes[n - 1])
        pl.when(fits)(functools.partial(run, size))

    @pl.when(slot == flush - 1)
    def _():
        for b in range(blocks):
            here = pl.ds(b * rows_block, rows_block)
            accr[here, :] += product_outer(hot_s[b], o_s[b])
            accd[here, :] += product_outer(hot_s[b], dx_s[b])

    @pl.when(e == pl.num_programs(0) - 1)
    def _():
        r_out[...] = accr[0:rows_block, :].astype(BF16)
        r_far[...] = accr[rows_block:, :].astype(BF16)
        d_out[...] = accd[0:rows_block, :].astype(BF16)
        d_far[...] = accd[rows_block:, :].astype(BF16)


def run_experts(chosen, most, x, x_far, g, g_far, pos, gate, w1, w2, a1, b1, a2, b2, held, cap, first, count):
    _, blocks, rows_block = pos.shape
    width = x.shape[1]
    tokens = blocks * rows_block
    rows = blocks * cap
    flush = FLUSH if count % FLUSH == 0 else 1
    record = 4 * RANK * width // UNIT
    lead = lambda e, c, m: (e, 0, 0)
    shifted = lambda e, c, m: (e + first, 0, 0)
    near = pl.BlockSpec((rows_block, width), lambda e, c, m: (0, 0), pipeline_mode=pl.Buffered(1))
    away = pl.BlockSpec((tokens - rows_block, width), lambda e, c, m: (0, 0), pipeline_mode=pl.Buffered(1))
    near_shape = jax.ShapeDtypeStruct((rows_block, width), BF16)
    away_shape = jax.ShapeDtypeStruct((tokens - rows_block, width), BF16)
    return pl.pallas_call(
        functools.partial(
            expert_kernel,
            blocks=blocks,
            rows_block=rows_block,
            cap=cap,
            flush=flush,
            carried=bool(held),
            first=first,
        ),
        grid_spec=pltpu.PrefetchScalarGridSpec(
            num_scalar_prefetch=2,
            grid=(count,),
            in_specs=[
                near,
                away,
                near,
                away,
                pl.BlockSpec((1, blocks, rows_block), shifted),
                pl.BlockSpec((1, blocks, rows_block), shifted),
                pl.BlockSpec((1, width, 2 * FF), lead),
                pl.BlockSpec((1, FF, width), lead),
                pl.BlockSpec((1, 1, 2 * RANK, width), lambda e, c, m: (c[0], e + first, 0, 0)),
                pl.BlockSpec((1, 1, 2, RANK, FF), lambda e, c, m: (c[0], e + first, 0, 0, 0)),
                pl.BlockSpec((1, 1, RANK, FF), lambda e, c, m: (c[0], e + first, 0, 0)),
                pl.BlockSpec((1, 1, RANK, width), lambda e, c, m: (c[0], e + first, 0, 0)),
            ]
            + ([near, away, near, away] if held else []),
            out_specs=[
                near,
                away,
                near,
                away,
                pl.BlockSpec((1, blocks, rows_block), lead),
                pl.BlockSpec((1, record, UNIT), lead),
            ],
            scratch_shapes=[
                pltpu.VMEM((blocks, flush * cap, rows_block), BF16),
                pltpu.VMEM((blocks, flush * cap, width), BF16),
                pltpu.VMEM((blocks, flush * cap, width), BF16),
                pltpu.VMEM((tokens, width), F32),
                pltpu.VMEM((tokens, width), F32),
                pltpu.VMEM((rows, width), BF16),
                pltpu.VMEM((rows, width), BF16),
                pltpu.VMEM((rows, 1), F32),
                pltpu.VMEM((2 * RANK, 2 * FF), BF16),
                pltpu.VMEM((rows, 2 * FF), BF16),
            ],
        ),
        out_shape=[
            near_shape,
            away_shape,
            near_shape,
            away_shape,
            jax.ShapeDtypeStruct((count, blocks, rows_block), F32),
            jax.ShapeDtypeStruct((count, record, UNIT), BF16),
        ],
        compiler_params=pltpu.CompilerParams(
            vmem_limit_bytes=63 * 1024 * 1024, dimension_semantics=("arbitrary",)
        ),
        cost_estimate=pl.CostEstimate(
            flops=8_000_000_000 * count,
            bytes_accessed=5_000_000 * count,
            transcendentals=rows * FF * count,
        ),
        name="experts",
    )(chosen, most, x, x_far, g, g_far, pos, gate, w1, w2, a1, b1, a2, b2, *held)


def fold_kernel(chosen_ref, w1_ref, w2_ref, a1_ref, b1_ref, a2_ref, b2_ref, *refs):
    o1_ref, o2_ref = refs[-2:]
    for n in range(2):
        at = slice(n * FF, (n + 1) * FF)
        a1 = a1_ref[0, 0, n * RANK : (n + 1) * RANK, :]
        o1_ref[0, :, at] = (w1_ref[0, :, at].astype(F32) + product_outer(a1, b1_ref[0, 0, n])).astype(BF16)
    o2_ref[0] = (w2_ref[0].astype(F32) + product_outer(a2_ref[0, 0], b2_ref[0, 0])).astype(BF16)


def fold_adapters(chosen, w1, w2, a1, b1, a2, b2, first, count, held=(), skip=0, size=None, after=()):
    size = size or count
    placed = lambda e, c: (e + skip, 0, 0)
    _, width, _ = w1.shape
    shifted = lambda e, c: (e + first, 0, 0)
    return pl.pallas_call(
        fold_kernel,
        grid_spec=pltpu.PrefetchScalarGridSpec(
            num_scalar_prefetch=1,
            grid=(count,),
            in_specs=[
                pl.BlockSpec((1, width, 2 * FF), shifted),
                pl.BlockSpec((1, FF, width), shifted),
                pl.BlockSpec((1, 1, 2 * RANK, width), lambda e, c: (c[0], e + first, 0, 0)),
                pl.BlockSpec((1, 1, 2, RANK, FF), lambda e, c: (c[0], e + first, 0, 0, 0)),
                pl.BlockSpec((1, 1, RANK, FF), lambda e, c: (c[0], e + first, 0, 0)),
                pl.BlockSpec((1, 1, RANK, width), lambda e, c: (c[0], e + first, 0, 0)),
            ]
            + [pl.BlockSpec(memory_space=pl.ANY)] * (len(held) + len(after)),
            out_specs=[pl.BlockSpec((1, width, 2 * FF), placed), pl.BlockSpec((1, FF, width), placed)],
        ),
        out_shape=[
            jax.ShapeDtypeStruct((size, width, 2 * FF), BF16),
            jax.ShapeDtypeStruct((size, FF, width), BF16),
        ],
        input_output_aliases={7 + n: n for n in range(len(held))},
        compiler_params=pltpu.CompilerParams(
            vmem_limit_bytes=60 * 1024 * 1024, dimension_semantics=("arbitrary",)
        ),
        cost_estimate=pl.CostEstimate(
            flops=3_000_000_000 * count, bytes_accessed=12_000_000 * count, transcendentals=0
        ),
        name="fold",
    )(chosen, w1, w2, a1, b1, a2, b2, *held, *after)


def total_kernel(ids_ref, rows_ref, *refs):
    out_ref, held = refs[-2:]
    held[...] = jnp.zeros_like(held)
    for n in range(rows_ref.shape[0]):
        held[ids_ref[n]] += rows_ref[n].astype(F32)
    out_ref[...] = held[...].astype(BF16)


def totals(ids, rows, adapters, after=()):
    shape = (adapters,) + rows.shape[1:]
    if rows.shape[1] % 16:
        hot = (jnp.arange(adapters, dtype=jnp.int32)[:, None] == ids[None, :]).astype(F32)
        return jnp.sum(hot[:, :, None, None] * rows.astype(F32)[None], axis=1).astype(BF16)
    return pl.pallas_call(
        total_kernel,
        grid_spec=pltpu.PrefetchScalarGridSpec(
            num_scalar_prefetch=1,
            grid=(1,),
            in_specs=[pl.BlockSpec(rows.shape, lambda i, c: (0, 0, 0))]
            + [pl.BlockSpec(memory_space=pl.ANY)] * len(after),
            out_specs=pl.BlockSpec(shape, lambda i, c: (0, 0, 0)),
            scratch_shapes=[pltpu.VMEM(shape, F32)],
        ),
        out_shape=jax.ShapeDtypeStruct(shape, BF16),
        compiler_params=pltpu.CompilerParams(vmem_limit_bytes=60 * 1024 * 1024),
        cost_estimate=pl.CostEstimate(flops=0, bytes_accessed=5_000_000, transcendentals=0),
        name="totals",
    )(ids, rows, *after)


def add_kernel(first_ref, second_ref, third_ref, *refs):
    total = first_ref[...] + second_ref[...].astype(F32) + third_ref[...].astype(F32)
    refs[-1][...] = total.astype(BF16)


def add_up(first, second, third, after=()):
    block, count = row_blocks(first)
    return pl.pallas_call(
        add_kernel,
        grid=(count,),
        in_specs=[block] * 3 + [pl.BlockSpec(memory_space=pl.ANY)] * len(after),
        out_specs=block,
        out_shape=jax.ShapeDtypeStruct(first.shape, BF16),
        compiler_params=pltpu.CompilerParams(vmem_limit_bytes=16 * 1024 * 1024),
        name="add_up",
    )(first, second, third, *after)


def unpack_kernel(rows_ref, *refs, share):
    a1_ref, b1_ref, a2_ref, b2_ref = refs[-4:]
    halves = a1_ref.shape[-1] // UNIT
    record = 4 * RANK * halves
    for e in range(rows_ref.shape[0] * share // record):
        unit = []
        for n in range(4 * halves):
            at = e * record + n * RANK
            unit.append(rows_ref[at // share, 0, at % share : at % share + RANK, :].astype(F32))
        for half in range(halves):
            at = slice(half * UNIT, (half + 1) * UNIT)
            a1_ref[0, e, 0:RANK, at] = unit[half]
            a1_ref[0, e, RANK:, at] = unit[halves + half]
            b2_ref[0, e, :, at] = unit[2 * halves + half]
        last = jnp.concatenate(unit[3 * halves :], axis=1)
        b1_ref[0, e, 0] = last[:, :FF]
        b1_ref[0, e, 1] = last[:, FF : 2 * FF]
        a2_ref[0, e] = last[:, 2 * FF :]


def unpack_grads(gathered, experts, first, held, width):
    ranks, adapters, share, _ = gathered.shape
    halves = width // UNIT
    record = 4 * RANK * halves
    if share % 16:
        flat = gathered.swapaxes(0, 1).reshape(adapters, experts, 4, halves, RANK, UNIT)
        flat = flat.swapaxes(3, 4).reshape(adapters, experts, 4 * RANK, width).astype(F32)
        last = flat[:, :, 3 * RANK :]
        return (
            flat[:, :, : 2 * RANK],
            jnp.stack([last[..., :FF], last[..., FF : 2 * FF]], axis=2),
            last[..., 2 * FF :],
            flat[:, :, 2 * RANK : 3 * RANK],
        )
    together = 1
    while together * share % record:
        together += 1
    each = together * share // record
    skip = first // each
    return pl.pallas_call(
        functools.partial(unpack_kernel, share=share),
        grid=(adapters, ranks // together),
        in_specs=[pl.BlockSpec((together, 1, share, UNIT), lambda a, i: (i, a, 0, 0))]
        + [pl.BlockSpec(memory_space=pl.ANY)] * len(held),
        out_specs=[
            pl.BlockSpec((1, each, 2 * RANK, width), lambda a, i: (a, i + skip, 0, 0)),
            pl.BlockSpec((1, each, 2, RANK, FF), lambda a, i: (a, i + skip, 0, 0, 0)),
            pl.BlockSpec((1, each, RANK, FF), lambda a, i: (a, i + skip, 0, 0)),
            pl.BlockSpec((1, each, RANK, width), lambda a, i: (a, i + skip, 0, 0)),
        ],
        out_shape=[
            jax.ShapeDtypeStruct((adapters, experts, 2 * RANK, width), F32),
            jax.ShapeDtypeStruct((adapters, experts, 2, RANK, FF), F32),
            jax.ShapeDtypeStruct((adapters, experts, RANK, FF), F32),
            jax.ShapeDtypeStruct((adapters, experts, RANK, width), F32),
        ],
        input_output_aliases={1 + n: n for n in range(len(held))},
        compiler_params=pltpu.CompilerParams(
            vmem_limit_bytes=40 * 1024 * 1024, dimension_semantics=("arbitrary", "arbitrary")
        ),
        cost_estimate=pl.CostEstimate(flops=0, bytes_accessed=30_000_000, transcendentals=0),
        name="unpack",
    )(gathered, *held)


def swap_pairs(size):
    return [(i, i ^ 1) for i in range(size)]


def from_others(piece):
    groups = lax.axis_size("grp")
    if groups == 2:
        return lax.ppermute(piece, "grp", swap_pairs(2))
    rows = piece.shape[0]
    every = lax.all_gather(piece, "grp", axis=0, tiled=True)
    return jnp.roll(every, -lax.axis_index("grp") * rows, axis=0)[rows:]


def owners_terms(near, far):
    if lax.axis_size("grp") == 2:
        return near, lax.ppermute(far, "grp", swap_pairs(2))
    return to_owners(near, far), jnp.zeros_like(near)


def to_owners(near, far):
    groups = lax.axis_size("grp")
    if groups == 2:
        return near.astype(F32) + lax.ppermute(far, "grp", swap_pairs(2)).astype(F32)
    every = jnp.roll(jnp.concatenate([near, far], axis=0), lax.axis_index("grp") * near.shape[0], axis=0)
    return lax.psum_scatter(every, "grp", scatter_dimension=0, tiled=True).astype(F32)


def in_order(near, far):
    if lax.axis_size("grp") != 2:
        return jnp.roll(jnp.concatenate([near, far], axis=0), lax.axis_index("grp") * near.shape[0], axis=0)
    ahead = lax.axis_index("grp") == 0
    return jnp.where(ahead, jnp.concatenate([near, far], axis=0), jnp.concatenate([far, near], axis=0))


def fetch_halves(half, after):
    groups = lax.axis_size("grp")
    member = lax.axis_index("grp")
    if groups != 2:
        return [(from_others(half), None)]
    rows = half.shape[0] // 2
    core = lax.axis_index("rep") % 2
    mine = delayed(lax.dynamic_slice_in_dim(half, core * rows, rows, 0), after)
    got = lax.ppermute(mine, "grp", swap_pairs(2))
    other = lax.ppermute(got, "rep", swap_pairs(lax.axis_size("rep")))
    away = (1 - member) * 2 * rows
    return [(got, away + core * rows), (other, away + (1 - core) * rows)]


def fetch_wide(half, note=None):
    reps = lax.axis_size("rep")
    if lax.axis_size("grp") != 2 or half.shape[0] % (reps * 16):
        notes = None if note is None else lax.all_gather(note, "rep", axis=0)
        far = from_others(half)
        return far, notes, half
    rows = half.shape[0] // reps
    mine = lax.dynamic_slice_in_dim(half, lax.axis_index("rep") * rows, rows, 0)
    got = lax.ppermute(mine, "grp", swap_pairs(2))
    if note is None:
        return lax.all_gather(got, "rep", axis=0, tiled=True), None, mine
    noted = jnp.concatenate([got, jnp.broadcast_to(note[None], (8, note.shape[0]))], axis=0)
    every = lax.all_gather(noted, "rep", axis=0)
    return every[:, :rows].reshape(half.shape), every[:, rows], mine


def columns(rows, start, count):
    return lax.dynamic_slice_in_dim(rows, start, count, 1)


def delayed_kernel(rows_ref, *refs):
    refs[-1][...] = rows_ref[...]


def row_blocks(rows):
    count = 4 if rows.shape[0] % 64 == 0 else 1
    shape = (rows.shape[0] // count,) + rows.shape[1:]
    return pl.BlockSpec(shape, lambda i: (i,) + (0,) * (rows.ndim - 1)), count


def delayed(rows, after):
    block, count = row_blocks(rows)
    return pl.pallas_call(
        delayed_kernel,
        grid=(count,),
        in_specs=[block] + [pl.BlockSpec(memory_space=pl.ANY)] * len(after),
        out_specs=block,
        out_shape=jax.ShapeDtypeStruct(rows.shape, rows.dtype),
        compiler_params=pltpu.CompilerParams(vmem_limit_bytes=16 * 1024 * 1024),
        name="delayed",
    )(rows, *after)


def local(
    tokens,
    cotangent,
    routes,
    padding,
    parents,
    adapter_ids,
    w_query,
    w_keyval,
    w_output,
    w_router,
    gain_attn,
    gain_ffn,
    w_gateup,
    w_down,
    a_qkv,
    b_query,
    b_keyval,
    a_output,
    b_output,
    a_router,
    b_router,
    a_gateup,
    b_gateup,
    a_down,
    b_down,
):
    groups = lax.axis_size("grp")
    reps = lax.axis_size("rep")
    member = lax.axis_index("grp")
    count = tokens.shape[0]
    width = tokens.shape[1]
    part = width // groups
    tree_length = count * groups
    experts_dev = w_gateup.shape[0]
    experts = experts_dev * groups
    capacity = count * TOPK * 7 // (experts * 5)
    cap = -(-capacity // 16) * 16
    kv_width = KEY_VALUE_HEADS * HEAD_SIZE
    chosen = adapter_ids[0]
    first = member * count
    adapters = a_qkv.shape[0]

    kv_part = kv_width // groups
    odd = jnp.concatenate([b_keyval[chosen, 0], b_keyval[chosen, 1], b_router[chosen]], axis=1)
    small = jnp.concatenate(
        [
            a_qkv.swapaxes(1, 2)[chosen],
            b_query[chosen],
            a_output.swapaxes(1, 2)[chosen],
            b_output[chosen],
            a_router.swapaxes(1, 2)[chosen],
            jnp.pad(odd, ((0, 0), (0, part - odd.shape[1]))),
            w_router.T,
            gain_attn[None],
            gain_ffn[None],
            jnp.pad(padding.astype(BF16)[None], ((0, 5), (0, part - count))),
        ],
        axis=0,
    )
    if groups == 2:
        small_far = from_others(small)
        joined = jnp.where(
            member == 0,
            jnp.concatenate([small, small_far], axis=1),
            jnp.concatenate([small_far, small], axis=1),
        )
    else:
        joined = in_order(small[None], from_others(small[None])).swapaxes(0, 1).reshape(-1, width)
    qkv_in = joined[: 3 * RANK]
    query_out = joined[3 * RANK : 4 * RANK]
    output_in = joined[4 * RANK : 5 * RANK]
    output_out = joined[5 * RANK : 6 * RANK]
    router_in = joined[6 * RANK : 7 * RANK]
    odd = joined[7 * RANK : 8 * RANK].reshape(RANK, groups, part)
    keyval_out = [odd[:, :, n * kv_part : (n + 1) * kv_part].reshape(RANK, kv_width) for n in range(2)]
    router_out = odd[:, :, 2 * kv_part : 2 * kv_part + experts_dev].reshape(RANK, experts)
    router_full = joined[8 * RANK : 8 * RANK + experts]
    last = 8 * RANK + experts
    attn_gain = joined[last]
    ffn_gain = joined[last + 1]
    pad_all = joined[last + 2].reshape(groups, part)[:, :count].reshape(-1)
    attn_gain = attn_gain.astype(F32)
    ffn_gain = ffn_gain.astype(F32)
    query_far, _, query_piece = fetch_wide(w_query)
    keyval_far = fetch_halves(w_keyval, (query_piece,))
    query_full = in_order(w_query, query_far)
    if groups == 2:
        (got, _), (other, _) = keyval_far
        ahead = lax.axis_index("rep") % 2 == 0
        keyval_full = in_order(
            w_keyval, jnp.where(ahead, jnp.concatenate([got, other], 0), jnp.concatenate([other, got], 0))
        )
    else:
        keyval_full = in_order(w_keyval, keyval_far[0][0])
    note = (jnp.arange(width, dtype=jnp.int32) == chosen).astype(BF16)
    output_far, notes, _ = fetch_wide(w_output, note)
    output_full = in_order(w_output, output_far)
    ids_all = jnp.sum(
        notes[:, :adapters].astype(jnp.int32) * jnp.arange(adapters, dtype=jnp.int32), axis=1
    )
    routes_far = from_others(routes)
    maps = (a_gateup.swapaxes(2, 3), b_gateup, a_down.swapaxes(2, 3), b_down)
    calls = 2 if experts_dev % (4 * FLUSH) == 0 and groups == 2 else 1
    each = experts_dev // calls
    some = -(-each // 2)

    def fold(call, late, held, after):
        at = some if late else 0
        count = each - some if late else some
        return fold_adapters(
            adapter_ids, w_gateup, w_down, *maps, call * each + at, count, held, at, each, after
        )

    first_fold = fold(0, False, (), ())

    tokens_f = tokens.astype(F32)
    normed = rms_norm(tokens_f, attn_gain).astype(BF16)
    low_rank = product_back(normed, qkv_in).astype(BF16)
    own_columns = columns(normed, member * part, part)
    if groups == 2:
        keyvals = product(own_columns, w_keyval)
        for piece, start in keyval_far:
            keyvals = keyvals + product(columns(normed, start, piece.shape[0]), piece)
    else:
        keyvals = product(normed, keyval_full)
    keyvals = jnp.concatenate(
        [
            keyvals[:, :kv_width] + product(low_rank[:, RANK : 2 * RANK], keyval_out[0]),
            keyvals[:, kv_width:] + product(low_rank[:, 2 * RANK :], keyval_out[1]),
        ],
        axis=1,
    ).astype(BF16)
    folded = [fold(0, True, first_fold, (keyvals,))]
    keyvals_far = from_others(keyvals)
    upstream_far = from_others(delayed(cotangent, (keyvals_far,)))
    if groups == 2:
        query_rows = product(own_columns, w_query) + product(columns(normed, (1 - member) * part, part), query_far)
    else:
        query_rows = product(normed, query_full)
    query_rows = (query_rows + product(low_rank[:, :RANK], query_out)).astype(BF16)
    pad_whole = jnp.roll(pad_all, -first)
    listing, steps, own_bias, live = visits(parents[0], pad_whole[:count], pad_whole[count:], first)
    attended, logs = run_attention(listing, steps, query_rows, keyvals, keyvals_far, own_bias, live)
    out_rank = product_back(attended, output_in).astype(BF16)
    middle = tokens_f + product(attended, output_full) + product(out_rank, output_out)
    normed_ffn = rms_norm(middle, ffn_gain).astype(BF16)
    if calls == 2:
        folded.append(fold(1, True, fold(1, False, (), (normed_ffn,)), ()))
    router_rank = product_back(normed_ffn, router_in).astype(BF16)
    logits = product_back(normed_ffn, router_full) + product(router_rank, router_out)

    labels = jnp.arange(experts, dtype=jnp.int32)
    named = jnp.any(routes[:, :, None] == labels, axis=1)
    best = jnp.max(jnp.where(named, logits, -jnp.inf), axis=1, keepdims=True)
    powers = jnp.where(named, jnp.exp(jnp.where(named, logits, best) - best), 0.0)
    gates = powers / jnp.sum(powers, axis=1, keepdims=True)

    mine = member * experts_dev + jnp.arange(experts_dev, dtype=jnp.int32)
    routes_all = jnp.concatenate([routes, routes_far], axis=0).reshape(groups, count, TOPK)
    hits = jnp.any(routes_all[:, :, :, None] == mine, axis=2)
    before = (jnp.arange(count)[:, None] > jnp.arange(count)[None, :]).astype(BF16)
    ranks = jnp.einsum("ts,gse->get", before, hits.astype(BF16), preferred_element_type=F32)
    places = jnp.where(hits.transpose(0, 2, 1), ranks.astype(jnp.int32), -1).transpose(1, 0, 2)

    most = jnp.max(places, axis=(1, 2)) + 1
    rows_far = from_others(normed_ffn)
    gates_t = gates.T
    if groups == 2:
        gates_near = lax.dynamic_slice_in_dim(gates_t, member * experts_dev, experts_dev, 0)
        gates_far = from_others(lax.dynamic_slice_in_dim(gates_t, (1 - member) * experts_dev, experts_dev, 0))
        gates_mine = jnp.stack([gates_near, gates_far], axis=1)
    else:
        gates_mine = lax.all_gather(gates_t, "grp", axis=0)
        gates_mine = lax.dynamic_slice_in_dim(gates_mine, member * experts_dev, experts_dev, 1)
        gates_mine = jnp.roll(gates_mine, -member, axis=0).transpose(1, 0, 2)
    sums = ()
    gate_terms = []
    spread = []
    for n in range(calls):
        *sums, terms, grads = run_experts(
            adapter_ids,
            most,
            normed_ffn,
            rows_far,
            cotangent,
            upstream_far,
            places,
            gates_mine,
            *folded[n],
            *maps,
            tuple(sums),
            cap,
            n * each,
            each,
        )
        gate_terms.append(terms)
        if n:
            sums[3], swapped = lax.optimization_barrier((sums[3], swapped))
            spread.append(lax.all_gather(totals(ids_all, swapped, adapters), "rep", axis=0))
        swapped = lax.all_to_all(
            grads.reshape(reps, -1, UNIT), "rep", split_axis=0, concat_axis=0, tiled=True
        )
    result_near, result_far, d_near, d_far = sums
    part_gates = jnp.concatenate(gate_terms, axis=0)
    if groups == 2:
        d_gates = in_order(part_gates[:, 0], from_others(part_gates[:, 1]))
    else:
        d_gates = jnp.roll(part_gates, member, axis=1)
        d_gates = lax.all_to_all(d_gates, "grp", split_axis=1, concat_axis=0, tiled=True)
    d_gates = d_gates.reshape(experts, count).T
    d_sum = to_owners(d_near, d_far)
    upstream = cotangent.astype(F32)
    d_logits = (gates * (d_gates - jnp.sum(gates * d_gates, axis=1, keepdims=True))).astype(BF16)

    d_router_rank = product_back(d_logits, router_out).astype(BF16)
    d_normed_ffn = d_sum + product(d_logits, router_full) + product(d_router_rank, router_in)
    grad_router_out = product_outer(router_rank, d_logits)
    grad_router_in = product_outer(d_router_rank, normed_ffn)
    d_middle = upstream + rms_back(middle, ffn_gain, d_normed_ffn)
    d_attn = d_middle.astype(BF16)
    d_out_rank = product_back(d_attn, output_out).astype(BF16)
    attended_gradient = (product_back(d_attn, output_full) + product(d_out_rank, output_in)).astype(BF16)
    grad_output_out = product_outer(out_rank, d_attn)
    grad_output_in = product_outer(d_out_rank, attended)
    parts = []
    pairs = KEY_VALUE_HEADS // 4
    for n in range(2):
        d_q, *d_kv = run_attention_back(
            listing,
            steps,
            query_rows,
            keyvals,
            keyvals_far,
            own_bias,
            live,
            attended,
            attended_gradient,
            logs,
            n * pairs,
            pairs,
        )
        d_kv = to_owners(jnp.concatenate(d_kv[:2], axis=1), jnp.concatenate(d_kv[2:], axis=1)).astype(BF16)
        parts.append((d_q, d_kv[:, : kv_width // 2], d_kv[:, kv_width // 2 :]))
    mixture = owners_terms(result_near, delayed(result_far, (parts[1][1],)))
    d_queries, d_keys, d_values = [jnp.concatenate(pair, axis=1) for pair in zip(*parts)]
    d_keyvals = jnp.concatenate([d_keys, d_values], axis=1)
    d_rank_qkv = jnp.concatenate(
        [
            product_back(d_queries, query_out),
            product_back(d_keys, keyval_out[0]),
            product_back(d_values, keyval_out[1]),
        ],
        axis=-1,
    ).astype(BF16)
    d_normed = (
        product_back(d_queries, query_full)
        + product_back(d_keyvals, keyval_full)
        + product(d_rank_qkv, qkv_in)
    )
    grad_input = (d_middle + rms_back(tokens_f, attn_gain, d_normed)).astype(BF16)
    grad_qkv_in = product_outer(d_rank_qkv, normed)
    grad_query_out = product_outer(low_rank[:, :RANK], d_queries)
    grad_keyval_out = jnp.stack(
        [
            product_outer(low_rank[:, RANK : 2 * RANK], d_keys),
            product_outer(low_rank[:, 2 * RANK :], d_values),
        ],
        axis=0,
    )

    last = totals(ids_all, swapped, adapters, after=(parts[0][0],))
    spread.append(lax.all_gather(last, "rep", axis=0))
    expert_grads = ()
    for n in range(calls):
        expert_grads = unpack_grads(spread[n], experts_dev, n * each, tuple(expert_grads), width)
    grad_a_gateup, grad_b_gateup, grad_a_down, grad_b_down = expert_grads

    tall = jnp.concatenate(
        [grad_qkv_in, grad_query_out, grad_output_in, grad_output_out, grad_router_in], axis=0
    ).astype(BF16)
    high = tall.shape[0]
    tall = tall.reshape(high, groups, part).swapaxes(0, 1)
    wide = [
        grad_keyval_out[0].reshape(RANK, groups, kv_part),
        grad_keyval_out[1].reshape(RANK, groups, kv_part),
        grad_router_out.reshape(RANK, groups, experts_dev),
        jnp.zeros((RANK, groups, part - 2 * kv_part - experts_dev), F32),
    ]
    wide = jnp.concatenate(wide, axis=2).astype(BF16).swapaxes(0, 1)
    dense = jnp.concatenate([tall, wide], axis=1).reshape(groups, reps, -1, part).swapaxes(0, 1)
    dense = dense.reshape(reps * groups, -1, part)
    result = add_up(middle, *mixture, after=(dense,))
    dense = lax.all_to_all(dense, ("rep", "grp"), split_axis=0, concat_axis=0, tiled=True)
    owner_hot = (jnp.arange(adapters, dtype=jnp.int32)[:, None] == jnp.repeat(ids_all, groups)[None, :])
    dense = jnp.sum(jnp.where(owner_hot[:, :, None, None], dense.astype(F32)[None], 0.0), axis=1).astype(BF16)
    dense = jnp.broadcast_to(dense[None], (reps,) + dense.shape)
    dense = lax.all_to_all(dense, "rep", split_axis=0, concat_axis=0, tiled=True).swapaxes(0, 1).reshape(adapters, -1, part).astype(F32)
    wide = dense[:, high:]
    owned = [
        dense[:, : 3 * RANK],
        dense[:, 3 * RANK : 4 * RANK],
        jnp.stack([wide[:, :, :kv_part], wide[:, :, kv_part : 2 * kv_part]], axis=1),
        dense[:, 4 * RANK : 5 * RANK],
        dense[:, 5 * RANK : 6 * RANK],
        dense[:, 6 * RANK : 7 * RANK],
        wide[:, :, 2 * kv_part : 2 * kv_part + experts_dev],
    ]
    return (
        result,
        grad_input,
        owned[0].swapaxes(1, 2),
        owned[1],
        owned[2],
        owned[3].swapaxes(1, 2),
        owned[4],
        owned[5].swapaxes(1, 2),
        owned[6],
        grad_a_gateup.swapaxes(2, 3),
        grad_b_gateup,
        grad_a_down.swapaxes(2, 3),
        grad_b_down,
    )


def solution(mesh):
    in_specs = (
        P(("rep", "grp"), None),
        P(("rep", "grp"), None),
        P(("rep", "grp"), None),
        P(("rep", "grp")),
        P("rep", None),
        P("rep"),
        P("grp", None),
        P("grp", None),
        P("grp", None),
        P("grp", None),
        P("grp"),
        P("grp"),
        P("grp", None, None),
        P("grp", None, None),
        P(None, "grp", None),
        P(None, None, "grp"),
        P(None, None, None, "grp"),
        P(None, "grp", None),
        P(None, None, "grp"),
        P(None, "grp", None),
        P(None, None, "grp"),
        P(None, "grp", None, None),
        P(None, "grp", None, None, None),
        P(None, "grp", None, None),
        P(None, "grp", None, None),
    )
    out_specs = (
        P(("rep", "grp"), None),
        P(("rep", "grp"), None),
        P(None, "grp", None),
        P(None, None, "grp"),
        P(None, None, None, "grp"),
        P(None, "grp", None),
        P(None, None, "grp"),
        P(None, "grp", None),
        P(None, None, "grp"),
        P(None, "grp", None, None),
        P(None, "grp", None, None, None),
        P(None, "grp", None, None),
        P(None, "grp", None, None),
    )
    return jax.shard_map(local, mesh=mesh, in_specs=in_specs, out_specs=out_specs, check_vma=False)
```

```python
import functools

import jax
import jax.numpy as jnp
from jax import lax
from jax.experimental import pallas as pl
from jax.experimental.pallas import tpu as pltpu
from jax.sharding import PartitionSpec as P

QUERY_HEADS = 24
KEY_VALUE_HEADS = 8
HEAD_SIZE = 64
FF = 512
TOPK = 8
RANK = 16
SEG = 128
FLUSH = 5
UNIT = 768

EPSILON = 1e-05
BF16 = jnp.bfloat16
F32 = jnp.float32


def product(left, right):
    return jnp.dot(left, right, preferred_element_type=F32)


def product_back(left, right):
    return lax.dot_general(left, right, (((1,), (1,)), ((), ())), preferred_element_type=F32)


def product_outer(left, right):
    return lax.dot_general(left, right, (((0,), (0,)), ((), ())), preferred_element_type=F32)


def rms_norm(value_rows, gain):
    return (
        value_rows
        * lax.rsqrt(jnp.mean(value_rows * value_rows, axis=-1, keepdims=True) + EPSILON)
        * gain
    )


def rms_back(value_rows, gain, upstream):
    factor = lax.rsqrt(jnp.mean(value_rows * value_rows, axis=-1, keepdims=True) + EPSILON)
    scaled = value_rows * factor
    incoming = upstream * gain
    return factor * (incoming - scaled * jnp.mean(incoming * scaled, axis=-1, keepdims=True))


def ancestry(parent_row):
    total = parent_row.shape[0]
    labels = jnp.arange(total, dtype=jnp.int32)
    own = labels[:, None] == labels[None, :]
    reached = jnp.logical_or(own, parent_row[:, None] == labels[None, :])
    steps = 1
    while steps < total:
        reached = jnp.any(jnp.logical_and(reached[:, :, None], reached[None, :, :]), axis=1)
        steps *= 2
    return reached.astype(jnp.int32)


def tile_parts(ref_k, seg_a, seg_b):
    return jnp.concatenate(
        [
            ref_k[pl.ds(pl.multiple_of(seg_a * SEG, SEG), SEG), :],
            ref_k[pl.ds(pl.multiple_of(seg_b * SEG, SEG), SEG), :],
        ],
        axis=0,
    )


def fill_doubled(held, near_ref, far_ref, ones=False):
    near = near_ref.shape[0]
    for ref, at in ((near_ref, 0), (far_ref, near)):
        rows = ref[...].astype(F32)
        low = lax.broadcasted_iota(jnp.int32, rows.shape, 1) < HEAD_SIZE
        turned = pltpu.roll(rows, HEAD_SIZE, axis=1)
        there = pl.ds(at, rows.shape[0])
        held[0, there, :] = jnp.where(low, rows, 1.0 if ones else turned).astype(BF16)
        held[1, there, :] = jnp.where(low, turned, 1.0 if ones else rows).astype(BF16)


PLACES = (((0, 0), (0, 1), (1, 0)), ((1, 1), (2, 0), (2, 1)))


def stacked_heads(ref, at, which, scale=None):
    low = lax.broadcasted_iota(jnp.int32, (SEG, 2 * HEAD_SIZE), 1) < HEAD_SIZE
    out = []
    for column, half in PLACES[which]:
        piece = ref[at, column * 2 * HEAD_SIZE : (column + 1) * 2 * HEAD_SIZE].astype(F32)
        if scale is not None:
            piece = piece * scale
        out.append(jnp.where(low if half == 0 else jnp.logical_not(low), piece, 0.0))
    return jnp.concatenate(out, axis=0)


def unstack(first, second):
    low = lax.broadcasted_iota(jnp.int32, (SEG, 2 * HEAD_SIZE), 1) < HEAD_SIZE
    return [
        jnp.where(low, first[0:SEG], first[SEG : 2 * SEG]),
        jnp.where(low, first[2 * SEG :], second[0:SEG]),
        jnp.where(low, second[SEG : 2 * SEG], second[2 * SEG :]),
    ]


def first_bias(own_ref, live_ref, i, seg_b):
    other = jnp.broadcast_to(live_ref[seg_b], (SEG, SEG))
    tile = jnp.concatenate([own_ref[i], other], axis=1)
    return jnp.concatenate([tile] * 3, axis=0)


def next_bias(live_ref, seg_a, seg_b):
    return jnp.concatenate([live_ref[seg_a], live_ref[seg_b]], axis=1)


def attend_kernel(
    list_ref,
    steps_ref,
    q_ref,
    k_ref,
    v_ref,
    k_far,
    v_far,
    own_ref,
    live_ref,
    o_ref,
    l_ref,
    kf,
    vf,
    *,
    here,
    segs,
    scale,
):
    fill_doubled(kf, k_ref, k_far)
    fill_doubled(vf, v_ref, v_far, ones=True)
    lanes = lax.broadcasted_iota(jnp.int32, (SEG, 2 * HEAD_SIZE), 1)
    low = lanes < HEAD_SIZE
    slots = 2 * segs
    for i in range(here):
        at = pl.ds(i * SEG, SEG)
        queries = [stacked_heads(q_ref, at, which, scale).astype(BF16) for which in range(2)]

        def pair_of(t):
            return (
                lax.rem(list_ref[i * slots + 2 * t], segs),
                lax.rem(list_ref[i * slots + 2 * t + 1], segs),
            )

        seg_a, seg_b = pair_of(0)
        bias = first_bias(own_ref, live_ref, i, list_ref[i * slots + 1])
        state = []
        for which in range(2):
            s = product_back(queries[which], tile_parts(kf.at[which], seg_a, seg_b)) + bias
            top = jnp.max(s, axis=1, keepdims=True)
            p = jnp.exp(s - top).astype(BF16)
            state.append((top, product(p, tile_parts(vf.at[which], seg_a, seg_b))))

        def body(t, state):
            bias = next_bias(live_ref, list_ref[i * slots + 2 * t], list_ref[i * slots + 2 * t + 1])
            seg_a, seg_b = pair_of(t)
            out = []
            for which in range(2):
                top, acc = state[which]
                s = product_back(queries[which], tile_parts(kf.at[which], seg_a, seg_b)) + bias
                higher = jnp.maximum(top, jnp.max(s, axis=1, keepdims=True))
                p = jnp.exp(s - higher).astype(BF16)
                acc = acc * jnp.exp(top - higher) + product(p, tile_parts(vf.at[which], seg_a, seg_b))
                out.append((higher, acc))
            return tuple(out)

        state = lax.fori_loop(1, steps_ref[i], body, tuple(state))
        turned = [pltpu.roll(acc, HEAD_SIZE, axis=1) for _, acc in state]
        logs = jnp.zeros((SEG, 2 * HEAD_SIZE), F32)
        heads = []
        for which in range(2):
            for n, (_, half) in enumerate(PLACES[which]):
                rows = slice(n * SEG, (n + 1) * SEG)
                plain, other = state[which][1][rows], turned[which][rows]
                heads.append(plain / other if half == 0 else other / plain)
                total = jnp.where(low, other, plain)
                logs = jnp.where(lanes == which * 3 + n, state[which][0][rows] + jnp.log(total), logs)
        l_ref[0, at, :] = logs
        for column in range(3):
            o_ref[at, column * 2 * HEAD_SIZE : (column + 1) * 2 * HEAD_SIZE] = jnp.where(
                low, heads[2 * column], heads[2 * column + 1]
            ).astype(BF16)


def attend_back_kernel(
    list_ref,
    steps_ref,
    q_ref,
    k_ref,
    v_ref,
    k_far,
    v_far,
    own_ref,
    live_ref,
    o_ref,
    do_ref,
    l_ref,
    *refs,
    here,
    segs,
    scale,
    after,
):
    dq_ref, dk_ref, dv_ref, dk_far, dv_far, kf, vf, dkf, dvf = refs[after:]
    fill_doubled(kf, k_ref, k_far)
    fill_doubled(vf, v_ref, v_far)
    dkf[...] = jnp.zeros_like(dkf)
    dvf[...] = jnp.zeros_like(dvf)
    slots = 2 * segs
    for i in range(here):
        at = pl.ds(i * SEG, SEG)
        fixed = []
        for which in range(2):
            d_o = stacked_heads(do_ref, at, which)
            fixed.append(
                (
                    stacked_heads(q_ref, at, which, scale).astype(BF16),
                    d_o.astype(BF16),
                    jnp.sum(d_o * stacked_heads(o_ref, at, which), axis=1, keepdims=True),
                    jnp.concatenate(
                        [l_ref[0, at, which * 3 + n : which * 3 + n + 1] for n in range(3)], axis=0
                    ),
                )
            )

        def step(t, bias):
            seg_a = lax.rem(list_ref[i * slots + 2 * t], segs)
            seg_b = lax.rem(list_ref[i * slots + 2 * t + 1], segs)
            out = []
            for which, (q, d_o, delta, log_total) in enumerate(fixed):
                k = tile_parts(kf.at[which], seg_a, seg_b)
                v = tile_parts(vf.at[which], seg_a, seg_b)
                p = jnp.exp(product_back(q, k) + bias - log_total)
                d_p = product_back(d_o, v)
                d_s = (p * (d_p - delta)).astype(BF16)
                d_v = product_outer(p.astype(BF16), d_o)
                d_k = product_outer(d_s, q)
                for n, seg in enumerate((seg_a, seg_b)):
                    rows = pl.ds(pl.multiple_of(seg * SEG, SEG), SEG)
                    dkf[which, rows, :] += d_k[n * SEG : (n + 1) * SEG]
                    dvf[which, rows, :] += d_v[n * SEG : (n + 1) * SEG]
                out.append(product(d_s, k))
            return tuple(out)

        d_q = step(0, first_bias(own_ref, live_ref, i, list_ref[i * slots + 1]))

        def body(t, carry):
            bias = next_bias(live_ref, list_ref[i * slots + 2 * t], list_ref[i * slots + 2 * t + 1])
            return tuple(a + b for a, b in zip(carry, step(t, bias)))

        d_q = lax.fori_loop(1, steps_ref[i], body, d_q)
        for column, piece in enumerate(unstack(*d_q)):
            dq_ref[at, column * 2 * HEAD_SIZE : (column + 1) * 2 * HEAD_SIZE] = (piece * scale).astype(BF16)
    near = dk_ref.shape[0]
    for out, far_out, held in ((dk_ref, dk_far, dkf), (dv_ref, dv_far, dvf)):
        first = held[0] + pltpu.roll(held[0], HEAD_SIZE, axis=1)
        second = held[1] + pltpu.roll(held[1], HEAD_SIZE, axis=1)
        low = lax.broadcasted_iota(jnp.int32, first.shape, 1) < HEAD_SIZE
        total = jnp.where(low, first, second).astype(BF16)
        out[...] = total[:near]
        far_out[...] = total[near:]


def visits(parent_row, pad_near, pad_far, first):
    count = pad_near.shape[0]
    tree_length = count + pad_far.shape[0]
    segs = tree_length // SEG
    here = count // SEG
    own = jnp.arange(here, dtype=jnp.int32)
    labels = jnp.arange(segs, dtype=jnp.int32)
    table = lax.dynamic_slice_in_dim(ancestry(parent_row), first // SEG, here, 0)
    turn = (labels[:, None] == (labels[None, :] + segs - first // SEG) % segs).astype(F32)
    table = product_back(table.astype(F32), turn).astype(jnp.int32)
    table = jnp.where(labels[None, :] == own[:, None], 0, table)
    order = jnp.sum(jnp.where(labels[None, :] <= labels[:, None], table[:, None, :], 0), axis=2)
    spots = jnp.arange(1, 2 * segs, dtype=jnp.int32)
    found = jnp.logical_and(table[:, None, :] > 0, order[:, None, :] == spots[None, :, None])
    listing = jnp.where(jnp.any(found, axis=2), jnp.sum(found * labels, axis=2), segs)
    listing = jnp.concatenate([own[:, None], listing], axis=1).astype(jnp.int32)
    steps = (2 + order[:, -1]) // 2
    live = jnp.where(jnp.concatenate([pad_near, pad_far]) > 0, 0.0, -1e30).astype(F32).reshape(segs, SEG)
    places = jnp.arange(SEG)
    causal = places[None, :] <= places[:, None]
    same = places[None, :] == places[:, None]
    own_bias = jnp.where(same[None], 0.0, jnp.where(causal[None], live[:here, None, :], -1e30))
    live = jnp.concatenate([live, jnp.full((1, SEG), -1e30, F32)], axis=0)[:, None, :]
    return listing.reshape(-1), steps.astype(jnp.int32), own_bias, live


def attention_specs(count, far, here, segs, skip=0):
    narrow = 2 * HEAD_SIZE
    shift = KEY_VALUE_HEADS // 2 + skip
    return [
        pl.BlockSpec((count, 3 * narrow), lambda h, a, b: (0, h + skip)),
        pl.BlockSpec((count, narrow), lambda h, a, b: (0, h + skip)),
        pl.BlockSpec((count, narrow), lambda h, a, b: (0, h + shift)),
        pl.BlockSpec((far, narrow), lambda h, a, b: (0, h + skip)),
        pl.BlockSpec((far, narrow), lambda h, a, b: (0, h + shift)),
        pl.BlockSpec((here, SEG, SEG), lambda h, a, b: (0, 0, 0)),
        pl.BlockSpec((segs + 1, 1, SEG), lambda h, a, b: (0, 0, 0)),
    ]


def run_attention(listing, steps, queries, near, far, own_bias, live):
    count, width = queries.shape
    tree_length = count + far.shape[0]
    here, segs = count // SEG, tree_length // SEG
    pairs = KEY_VALUE_HEADS // 2
    narrow = 2 * HEAD_SIZE
    return pl.pallas_call(
        functools.partial(attend_kernel, here=here, segs=segs, scale=HEAD_SIZE ** (-0.5)),
        grid_spec=pltpu.PrefetchScalarGridSpec(
            num_scalar_prefetch=2,
            grid=(pairs,),
            in_specs=attention_specs(count, far.shape[0], here, segs),
            out_specs=[
                pl.BlockSpec((count, 3 * narrow), lambda h, a, b: (0, h)),
                pl.BlockSpec((1, count, narrow), lambda h, a, b: (h, 0, 0)),
            ],
            scratch_shapes=[pltpu.VMEM((2, tree_length, narrow), BF16)] * 2,
        ),
        out_shape=[
            jax.ShapeDtypeStruct((count, width), BF16),
            jax.ShapeDtypeStruct((pairs, count, narrow), F32),
        ],
        compiler_params=pltpu.CompilerParams(
            vmem_limit_bytes=60 * 1024 * 1024, dimension_semantics=("arbitrary",)
        ),
        cost_estimate=pl.CostEstimate(flops=40_000_000_000, bytes_accessed=8_000_000, transcendentals=10_000_000),
        name="attention",
    )(listing, steps, queries, near, near, far, far, own_bias, live)


def run_attention_back(
    listing, steps, queries, near, far, own_bias, live, attended, gradient, logs, skip, pairs, after=()
):
    count = queries.shape[0]
    tree_length = count + far.shape[0]
    here, segs = count // SEG, tree_length // SEG
    narrow = 2 * HEAD_SIZE
    rows = pl.BlockSpec((count, 3 * narrow), lambda h, a, b: (0, h + skip))
    outs = [pl.BlockSpec((count, narrow), lambda h, a, b: (0, h))] * 2
    outs += [pl.BlockSpec((far.shape[0], narrow), lambda h, a, b: (0, h))] * 2
    return pl.pallas_call(
        functools.partial(
            attend_back_kernel, here=here, segs=segs, scale=HEAD_SIZE ** (-0.5), after=len(after)
        ),
        grid_spec=pltpu.PrefetchScalarGridSpec(
            num_scalar_prefetch=2,
            grid=(pairs,),
            in_specs=attention_specs(count, far.shape[0], here, segs, skip)
            + [rows, rows, pl.BlockSpec((1, count, narrow), lambda h, a, b: (h + skip, 0, 0))]
            + [pl.BlockSpec(memory_space=pl.ANY)] * len(after),
            out_specs=[pl.BlockSpec((count, 3 * narrow), lambda h, a, b: (0, h))] + outs,
            scratch_shapes=[pltpu.VMEM((2, tree_length, narrow), BF16)] * 2
            + [pltpu.VMEM((2, tree_length, narrow), F32)] * 2,
        ),
        out_shape=[jax.ShapeDtypeStruct((count, 3 * pairs * narrow), BF16)]
        + [jax.ShapeDtypeStruct((count, pairs * narrow), BF16)] * 2
        + [jax.ShapeDtypeStruct((far.shape[0], pairs * narrow), BF16)] * 2,
        compiler_params=pltpu.CompilerParams(
            vmem_limit_bytes=60 * 1024 * 1024, dimension_semantics=("arbitrary",)
        ),
        cost_estimate=pl.CostEstimate(
            flops=17_000_000_000 * pairs, bytes_accessed=3_000_000 * pairs, transcendentals=0
        ),
        name="attention_back",
    )(listing, steps, queries, near, near, far, far, own_bias, live, attended, gradient, logs, *after)


def expert_kernel(
    chosen_ref,
    x_ref,
    x_far,
    g_ref,
    g_far,
    pos_ref,
    gate_ref,
    w1_ref,
    w2_ref,
    a1_ref,
    b1_ref,
    a2_ref,
    b2_ref,
    *refs,
    blocks,
    rows_block,
    cap,
    flush,
    carried,
):
    held = refs[:4] if carried else ()
    (
        r_out,
        r_far,
        d_out,
        d_far,
        dg_out,
        grad_out,
        hot_s,
        o_s,
        dx_s,
        accr,
        accd,
        x_s,
        g_s,
        gate_s,
        b1_s,
        dgu_s,
    ) = refs[len(held) :]
    e = pl.program_id(0)
    slot = lax.rem(e, flush)
    width = x_ref.shape[-1]
    halves = width // UNIT

    @pl.when(e == 0)
    def _():
        b1_s[...] = jnp.zeros_like(b1_s)
        if carried:
            for n, acc in enumerate((accr, accd)):
                acc[0:rows_block, :] = held[2 * n][...].astype(F32)
                acc[rows_block:, :] = held[2 * n + 1][...].astype(F32)
        else:
            accr[...] = jnp.zeros_like(accr)
            accd[...] = jnp.zeros_like(accd)

    at = pl.multiple_of(slot * cap, 16)
    for b in range(blocks):
        rows_ref, g_rows_ref = (x_ref, g_ref) if b == 0 else (x_far, g_far)
        here = pl.ds(max(b - 1, 0) * rows_block, rows_block)
        there = pl.ds(b * cap, cap)
        places = lax.broadcasted_iota(jnp.int32, (cap, rows_block), 0)
        hit = places == pos_ref[0, b : b + 1, :]
        hot = hit.astype(F32).astype(BF16)
        hot_s[b, pl.ds(at, cap), :] = hot
        x_s[there, :] = product(hot, rows_ref[here, :]).astype(BF16)
        g_s[there, :] = product(hot, g_rows_ref[here, :]).astype(BF16)
        gate_s[there, :] = jnp.sum(
            jnp.where(hit, gate_ref[0, b : b + 1, :], 0.0), axis=1, keepdims=True
        )
    b1_s[0:RANK, 0:FF] = b1_ref[0, 0, 0]
    b1_s[RANK : 2 * RANK, FF : 2 * FF] = b1_ref[0, 0, 1]

    x = x_s[...]
    gate_col = gate_s[...]
    rank_in = product_back(a1_ref[0, 0], x).astype(BF16)
    pre = product(x, w1_ref[0])
    gate_pre = pre[:, :FF]
    up_pre = pre[:, FF:]
    sig = 1.0 / (1.0 + jnp.exp(-gate_pre))
    act = gate_pre * sig
    hidden = (act * up_pre).astype(BF16)
    rank_down = product_back(a2_ref[0, 0], hidden).astype(BF16)
    out = product(hidden, w2_ref[0]).astype(BF16).astype(F32)
    g = g_s[...].astype(F32)
    d_gate_col = jnp.sum(g * out, axis=1, keepdims=True)
    out = (gate_col * out).astype(BF16)
    d_exp = (gate_col * g).astype(BF16)
    d_rank_down = product_back(b2_ref[0, 0], d_exp).astype(BF16)
    d_hidden = product_back(d_exp, w2_ref[0])
    dgu_s[:, :FF] = (d_hidden * up_pre * sig * (1.0 + gate_pre * (1.0 - sig))).astype(BF16)
    dgu_s[:, FF:] = (d_hidden * act).astype(BF16)
    dgu = dgu_s[...]
    d_rank_in = product_back(b1_s[...], dgu).astype(BF16)
    dx = product_back(dgu, w1_ref[0]).astype(BF16)
    for b in range(blocks):
        o_s[b, pl.ds(at, cap), :] = out[b * cap : (b + 1) * cap]
        dx_s[b, pl.ds(at, cap), :] = dx[b * cap : (b + 1) * cap]
        places = lax.broadcasted_iota(jnp.int32, (cap, rows_block), 0)
        hit = places == pos_ref[0, b : b + 1, :]
        dg_out[0, b : b + 1, :] = jnp.sum(
            jnp.where(hit, d_gate_col[b * cap : (b + 1) * cap], 0.0), axis=0, keepdims=True
        )

    grad_a1 = product(d_rank_in, x)
    grad_b1 = product(rank_in, dgu)
    grad_a2 = product(d_rank_down, hidden)
    grad_b2 = product(rank_down, d_exp)
    last = jnp.concatenate([grad_b1[:RANK, :FF], grad_b1[RANK:, FF:], grad_a2], axis=1)
    for n, piece in enumerate((grad_a1[:RANK], grad_a1[RANK:], grad_b2, last)):
        for half in range(halves):
            rows = slice((n * halves + half) * RANK, (n * halves + half + 1) * RANK)
            grad_out[0, rows, :] = piece[:, half * UNIT : (half + 1) * UNIT].astype(BF16)

    @pl.when(slot == flush - 1)
    def _():
        for b in range(blocks):
            here = pl.ds(b * rows_block, rows_block)
            accr[here, :] += product_outer(hot_s[b], o_s[b])
            accd[here, :] += product_outer(hot_s[b], dx_s[b])

    @pl.when(e == pl.num_programs(0) - 1)
    def _():
        r_out[...] = accr[0:rows_block, :].astype(BF16)
        r_far[...] = accr[rows_block:, :].astype(BF16)
        d_out[...] = accd[0:rows_block, :].astype(BF16)
        d_far[...] = accd[rows_block:, :].astype(BF16)


def run_experts(chosen, x, x_far, g, g_far, pos, gate, w1, w2, a1, b1, a2, b2, held, cap, first, count):
    _, blocks, rows_block = pos.shape
    width = x.shape[1]
    tokens = blocks * rows_block
    rows = blocks * cap
    flush = FLUSH if count % FLUSH == 0 else 1
    record = 4 * RANK * width // UNIT
    lead = lambda e, c: (e, 0, 0)
    shifted = lambda e, c: (e + first, 0, 0)
    near = pl.BlockSpec((rows_block, width), lambda e, c: (0, 0), pipeline_mode=pl.Buffered(1))
    away = pl.BlockSpec((tokens - rows_block, width), lambda e, c: (0, 0), pipeline_mode=pl.Buffered(1))
    near_shape = jax.ShapeDtypeStruct((rows_block, width), BF16)
    away_shape = jax.ShapeDtypeStruct((tokens - rows_block, width), BF16)
    return pl.pallas_call(
        functools.partial(
            expert_kernel,
            blocks=blocks,
            rows_block=rows_block,
            cap=cap,
            flush=flush,
            carried=bool(held),
        ),
        grid_spec=pltpu.PrefetchScalarGridSpec(
            num_scalar_prefetch=1,
            grid=(count,),
            in_specs=[
                near,
                away,
                near,
                away,
                pl.BlockSpec((1, blocks, rows_block), shifted),
                pl.BlockSpec((1, blocks, rows_block), shifted),
                pl.BlockSpec((1, width, 2 * FF), lead),
                pl.BlockSpec((1, FF, width), lead),
                pl.BlockSpec((1, 1, 2 * RANK, width), lambda e, c: (c[0], e + first, 0, 0)),
                pl.BlockSpec((1, 1, 2, RANK, FF), lambda e, c: (c[0], e + first, 0, 0, 0)),
                pl.BlockSpec((1, 1, RANK, FF), lambda e, c: (c[0], e + first, 0, 0)),
                pl.BlockSpec((1, 1, RANK, width), lambda e, c: (c[0], e + first, 0, 0)),
            ]
            + ([near, away, near, away] if held else []),
            out_specs=[
                near,
                away,
                near,
                away,
                pl.BlockSpec((1, blocks, rows_block), lead),
                pl.BlockSpec((1, record, UNIT), lead),
            ],
            scratch_shapes=[
                pltpu.VMEM((blocks, flush * cap, rows_block), BF16),
                pltpu.VMEM((blocks, flush * cap, width), BF16),
                pltpu.VMEM((blocks, flush * cap, width), BF16),
                pltpu.VMEM((tokens, width), F32),
                pltpu.VMEM((tokens, width), F32),
                pltpu.VMEM((rows, width), BF16),
                pltpu.VMEM((rows, width), BF16),
                pltpu.VMEM((rows, 1), F32),
                pltpu.VMEM((2 * RANK, 2 * FF), BF16),
                pltpu.VMEM((rows, 2 * FF), BF16),
            ],
        ),
        out_shape=[
            near_shape,
            away_shape,
            near_shape,
            away_shape,
            jax.ShapeDtypeStruct((count, blocks, rows_block), F32),
            jax.ShapeDtypeStruct((count, record, UNIT), BF16),
        ],
        compiler_params=pltpu.CompilerParams(
            vmem_limit_bytes=63 * 1024 * 1024, dimension_semantics=("arbitrary",)
        ),
        cost_estimate=pl.CostEstimate(
            flops=8_000_000_000 * count,
            bytes_accessed=5_000_000 * count,
            transcendentals=rows * FF * count,
        ),
        name="experts",
    )(chosen, x, x_far, g, g_far, pos, gate, w1, w2, a1, b1, a2, b2, *held)


def fold_kernel(chosen_ref, w1_ref, w2_ref, a1_ref, b1_ref, a2_ref, b2_ref, *refs):
    o1_ref, o2_ref = refs[-2:]
    for n in range(2):
        at = slice(n * FF, (n + 1) * FF)
        a1 = a1_ref[0, 0, n * RANK : (n + 1) * RANK, :]
        o1_ref[0, :, at] = (w1_ref[0, :, at].astype(F32) + product_outer(a1, b1_ref[0, 0, n])).astype(BF16)
    o2_ref[0] = (w2_ref[0].astype(F32) + product_outer(a2_ref[0, 0], b2_ref[0, 0])).astype(BF16)


def fold_adapters(chosen, w1, w2, a1, b1, a2, b2, first, count, held=(), skip=0, size=None, after=()):
    size = size or count
    placed = lambda e, c: (e + skip, 0, 0)
    _, width, _ = w1.shape
    shifted = lambda e, c: (e + first, 0, 0)
    return pl.pallas_call(
        fold_kernel,
        grid_spec=pltpu.PrefetchScalarGridSpec(
            num_scalar_prefetch=1,
            grid=(count,),
            in_specs=[
                pl.BlockSpec((1, width, 2 * FF), shifted),
                pl.BlockSpec((1, FF, width), shifted),
                pl.BlockSpec((1, 1, 2 * RANK, width), lambda e, c: (c[0], e + first, 0, 0)),
                pl.BlockSpec((1, 1, 2, RANK, FF), lambda e, c: (c[0], e + first, 0, 0, 0)),
                pl.BlockSpec((1, 1, RANK, FF), lambda e, c: (c[0], e + first, 0, 0)),
                pl.BlockSpec((1, 1, RANK, width), lambda e, c: (c[0], e + first, 0, 0)),
            ]
            + [pl.BlockSpec(memory_space=pl.ANY)] * (len(held) + len(after)),
            out_specs=[pl.BlockSpec((1, width, 2 * FF), placed), pl.BlockSpec((1, FF, width), placed)],
        ),
        out_shape=[
            jax.ShapeDtypeStruct((size, width, 2 * FF), BF16),
            jax.ShapeDtypeStruct((size, FF, width), BF16),
        ],
        input_output_aliases={7 + n: n for n in range(len(held))},
        compiler_params=pltpu.CompilerParams(
            vmem_limit_bytes=60 * 1024 * 1024, dimension_semantics=("arbitrary",)
        ),
        cost_estimate=pl.CostEstimate(
            flops=3_000_000_000 * count, bytes_accessed=12_000_000 * count, transcendentals=0
        ),
        name="fold",
    )(chosen, w1, w2, a1, b1, a2, b2, *held, *after)


def total_kernel(ids_ref, rows_ref, *refs):
    out_ref, held = refs[-2:]
    held[...] = jnp.zeros_like(held)
    for n in range(rows_ref.shape[0]):
        held[ids_ref[n]] += rows_ref[n].astype(F32)
    out_ref[...] = held[...].astype(BF16)


def totals(ids, rows, adapters, after=()):
    shape = (adapters,) + rows.shape[1:]
    if rows.shape[1] % 16:
        hot = (jnp.arange(adapters, dtype=jnp.int32)[:, None] == ids[None, :]).astype(F32)
        return jnp.sum(hot[:, :, None, None] * rows.astype(F32)[None], axis=1).astype(BF16)
    return pl.pallas_call(
        total_kernel,
        grid_spec=pltpu.PrefetchScalarGridSpec(
            num_scalar_prefetch=1,
            grid=(1,),
            in_specs=[pl.BlockSpec(rows.shape, lambda i, c: (0, 0, 0))]
            + [pl.BlockSpec(memory_space=pl.ANY)] * len(after),
            out_specs=pl.BlockSpec(shape, lambda i, c: (0, 0, 0)),
            scratch_shapes=[pltpu.VMEM(shape, F32)],
        ),
        out_shape=jax.ShapeDtypeStruct(shape, BF16),
        compiler_params=pltpu.CompilerParams(vmem_limit_bytes=60 * 1024 * 1024),
        cost_estimate=pl.CostEstimate(flops=0, bytes_accessed=5_000_000, transcendentals=0),
        name="totals",
    )(ids, rows, *after)


def add_kernel(first_ref, second_ref, third_ref, *refs):
    total = first_ref[...] + second_ref[...].astype(F32) + third_ref[...].astype(F32)
    refs[-1][...] = total.astype(BF16)


def add_up(first, second, third, after=()):
    block, count = row_blocks(first)
    return pl.pallas_call(
        add_kernel,
        grid=(count,),
        in_specs=[block] * 3 + [pl.BlockSpec(memory_space=pl.ANY)] * len(after),
        out_specs=block,
        out_shape=jax.ShapeDtypeStruct(first.shape, BF16),
        compiler_params=pltpu.CompilerParams(vmem_limit_bytes=16 * 1024 * 1024),
        name="add_up",
    )(first, second, third, *after)


def unpack_kernel(rows_ref, *refs, share):
    a1_ref, b1_ref, a2_ref, b2_ref = refs[-4:]
    halves = a1_ref.shape[-1] // UNIT
    record = 4 * RANK * halves
    for e in range(rows_ref.shape[0] * share // record):
        unit = []
        for n in range(4 * halves):
            at = e * record + n * RANK
            unit.append(rows_ref[at // share, 0, at % share : at % share + RANK, :].astype(F32))
        for half in range(halves):
            at = slice(half * UNIT, (half + 1) * UNIT)
            a1_ref[0, e, 0:RANK, at] = unit[half]
            a1_ref[0, e, RANK:, at] = unit[halves + half]
            b2_ref[0, e, :, at] = unit[2 * halves + half]
        last = jnp.concatenate(unit[3 * halves :], axis=1)
        b1_ref[0, e, 0] = last[:, :FF]
        b1_ref[0, e, 1] = last[:, FF : 2 * FF]
        a2_ref[0, e] = last[:, 2 * FF :]


def unpack_grads(gathered, experts, first, held, width):
    ranks, adapters, share, _ = gathered.shape
    halves = width // UNIT
    record = 4 * RANK * halves
    if share % 16:
        flat = gathered.swapaxes(0, 1).reshape(adapters, experts, 4, halves, RANK, UNIT)
        flat = flat.swapaxes(3, 4).reshape(adapters, experts, 4 * RANK, width).astype(F32)
        last = flat[:, :, 3 * RANK :]
        return (
            flat[:, :, : 2 * RANK],
            jnp.stack([last[..., :FF], last[..., FF : 2 * FF]], axis=2),
            last[..., 2 * FF :],
            flat[:, :, 2 * RANK : 3 * RANK],
        )
    together = 1
    while together * share % record:
        together += 1
    each = together * share // record
    skip = first // each
    return pl.pallas_call(
        functools.partial(unpack_kernel, share=share),
        grid=(adapters, ranks // together),
        in_specs=[pl.BlockSpec((together, 1, share, UNIT), lambda a, i: (i, a, 0, 0))]
        + [pl.BlockSpec(memory_space=pl.ANY)] * len(held),
        out_specs=[
            pl.BlockSpec((1, each, 2 * RANK, width), lambda a, i: (a, i + skip, 0, 0)),
            pl.BlockSpec((1, each, 2, RANK, FF), lambda a, i: (a, i + skip, 0, 0, 0)),
            pl.BlockSpec((1, each, RANK, FF), lambda a, i: (a, i + skip, 0, 0)),
            pl.BlockSpec((1, each, RANK, width), lambda a, i: (a, i + skip, 0, 0)),
        ],
        out_shape=[
            jax.ShapeDtypeStruct((adapters, experts, 2 * RANK, width), F32),
            jax.ShapeDtypeStruct((adapters, experts, 2, RANK, FF), F32),
            jax.ShapeDtypeStruct((adapters, experts, RANK, FF), F32),
            jax.ShapeDtypeStruct((adapters, experts, RANK, width), F32),
        ],
        input_output_aliases={1 + n: n for n in range(len(held))},
        compiler_params=pltpu.CompilerParams(
            vmem_limit_bytes=40 * 1024 * 1024, dimension_semantics=("arbitrary", "arbitrary")
        ),
        cost_estimate=pl.CostEstimate(flops=0, bytes_accessed=30_000_000, transcendentals=0),
        name="unpack",
    )(gathered, *held)


def swap_pairs(size):
    return [(i, i ^ 1) for i in range(size)]


def from_others(piece):
    groups = lax.axis_size("grp")
    if groups == 2:
        return lax.ppermute(piece, "grp", swap_pairs(2))
    rows = piece.shape[0]
    every = lax.all_gather(piece, "grp", axis=0, tiled=True)
    return jnp.roll(every, -lax.axis_index("grp") * rows, axis=0)[rows:]


def owners_terms(near, far):
    if lax.axis_size("grp") == 2:
        return near, lax.ppermute(far, "grp", swap_pairs(2))
    return to_owners(near, far), jnp.zeros_like(near)


def to_owners(near, far):
    groups = lax.axis_size("grp")
    if groups == 2:
        return near.astype(F32) + lax.ppermute(far, "grp", swap_pairs(2)).astype(F32)
    every = jnp.roll(jnp.concatenate([near, far], axis=0), lax.axis_index("grp") * near.shape[0], axis=0)
    return lax.psum_scatter(every, "grp", scatter_dimension=0, tiled=True).astype(F32)


def in_order(near, far):
    if lax.axis_size("grp") != 2:
        return jnp.roll(jnp.concatenate([near, far], axis=0), lax.axis_index("grp") * near.shape[0], axis=0)
    ahead = lax.axis_index("grp") == 0
    return jnp.where(ahead, jnp.concatenate([near, far], axis=0), jnp.concatenate([far, near], axis=0))


def fetch_halves(half, after):
    groups = lax.axis_size("grp")
    member = lax.axis_index("grp")
    if groups != 2:
        return [(from_others(half), None)]
    rows = half.shape[0] // 2
    core = lax.axis_index("rep") % 2
    mine = delayed(lax.dynamic_slice_in_dim(half, core * rows, rows, 0), after)
    got = lax.ppermute(mine, "grp", swap_pairs(2))
    other = lax.ppermute(got, "rep", swap_pairs(lax.axis_size("rep")))
    away = (1 - member) * 2 * rows
    return [(got, away + core * rows), (other, away + (1 - core) * rows)]


def fetch_wide(half, note=None):
    reps = lax.axis_size("rep")
    if lax.axis_size("grp") != 2 or half.shape[0] % (reps * 16):
        notes = None if note is None else lax.all_gather(note, "rep", axis=0)
        far = from_others(half)
        return far, notes, half
    rows = half.shape[0] // reps
    mine = lax.dynamic_slice_in_dim(half, lax.axis_index("rep") * rows, rows, 0)
    got = lax.ppermute(mine, "grp", swap_pairs(2))
    if note is None:
        return lax.all_gather(got, "rep", axis=0, tiled=True), None, mine
    noted = jnp.concatenate([got, jnp.broadcast_to(note[None], (8, note.shape[0]))], axis=0)
    every = lax.all_gather(noted, "rep", axis=0)
    return every[:, :rows].reshape(half.shape), every[:, rows], mine


def columns(rows, start, count):
    return lax.dynamic_slice_in_dim(rows, start, count, 1)


def delayed_kernel(rows_ref, *refs):
    refs[-1][...] = rows_ref[...]


def row_blocks(rows):
    count = 4 if rows.shape[0] % 64 == 0 else 1
    shape = (rows.shape[0] // count,) + rows.shape[1:]
    return pl.BlockSpec(shape, lambda i: (i,) + (0,) * (rows.ndim - 1)), count


def delayed(rows, after):
    block, count = row_blocks(rows)
    return pl.pallas_call(
        delayed_kernel,
        grid=(count,),
        in_specs=[block] + [pl.BlockSpec(memory_space=pl.ANY)] * len(after),
        out_specs=block,
        out_shape=jax.ShapeDtypeStruct(rows.shape, rows.dtype),
        compiler_params=pltpu.CompilerParams(vmem_limit_bytes=16 * 1024 * 1024),
        name="delayed",
    )(rows, *after)


def local(
    tokens,
    cotangent,
    routes,
    padding,
    parents,
    adapter_ids,
    w_query,
    w_keyval,
    w_output,
    w_router,
    gain_attn,
    gain_ffn,
    w_gateup,
    w_down,
    a_qkv,
    b_query,
    b_keyval,
    a_output,
    b_output,
    a_router,
    b_router,
    a_gateup,
    b_gateup,
    a_down,
    b_down,
):
    groups = lax.axis_size("grp")
    reps = lax.axis_size("rep")
    member = lax.axis_index("grp")
    count = tokens.shape[0]
    width = tokens.shape[1]
    part = width // groups
    tree_length = count * groups
    experts_dev = w_gateup.shape[0]
    experts = experts_dev * groups
    capacity = count * TOPK * 7 // (experts * 5)
    cap = -(-capacity // 16) * 16
    kv_width = KEY_VALUE_HEADS * HEAD_SIZE
    chosen = adapter_ids[0]
    first = member * count
    adapters = a_qkv.shape[0]

    kv_part = kv_width // groups
    odd = jnp.concatenate([b_keyval[chosen, 0], b_keyval[chosen, 1], b_router[chosen]], axis=1)
    small = jnp.concatenate(
        [
            a_qkv.swapaxes(1, 2)[chosen],
            b_query[chosen],
            a_output.swapaxes(1, 2)[chosen],
            b_output[chosen],
            a_router.swapaxes(1, 2)[chosen],
            jnp.pad(odd, ((0, 0), (0, part - odd.shape[1]))),
            w_router.T,
            gain_attn[None],
            gain_ffn[None],
            jnp.pad(padding.astype(BF16)[None], ((0, 5), (0, part - count))),
        ],
        axis=0,
    )
    if groups == 2:
        small_far = from_others(small)
        joined = jnp.where(
            member == 0,
            jnp.concatenate([small, small_far], axis=1),
            jnp.concatenate([small_far, small], axis=1),
        )
    else:
        joined = in_order(small[None], from_others(small[None])).swapaxes(0, 1).reshape(-1, width)
    qkv_in = joined[: 3 * RANK]
    query_out = joined[3 * RANK : 4 * RANK]
    output_in = joined[4 * RANK : 5 * RANK]
    output_out = joined[5 * RANK : 6 * RANK]
    router_in = joined[6 * RANK : 7 * RANK]
    odd = joined[7 * RANK : 8 * RANK].reshape(RANK, groups, part)
    keyval_out = [odd[:, :, n * kv_part : (n + 1) * kv_part].reshape(RANK, kv_width) for n in range(2)]
    router_out = odd[:, :, 2 * kv_part : 2 * kv_part + experts_dev].reshape(RANK, experts)
    router_full = joined[8 * RANK : 8 * RANK + experts]
    last = 8 * RANK + experts
    attn_gain = joined[last]
    ffn_gain = joined[last + 1]
    pad_all = joined[last + 2].reshape(groups, part)[:, :count].reshape(-1)
    attn_gain = attn_gain.astype(F32)
    ffn_gain = ffn_gain.astype(F32)
    query_far, _, query_piece = fetch_wide(w_query)
    keyval_far = fetch_halves(w_keyval, (query_piece,))
    query_full = in_order(w_query, query_far)
    if groups == 2:
        (got, _), (other, _) = keyval_far
        ahead = lax.axis_index("rep") % 2 == 0
        keyval_full = in_order(
            w_keyval, jnp.where(ahead, jnp.concatenate([got, other], 0), jnp.concatenate([other, got], 0))
        )
    else:
        keyval_full = in_order(w_keyval, keyval_far[0][0])
    note = (jnp.arange(width, dtype=jnp.int32) == chosen).astype(BF16)
    output_far, notes, _ = fetch_wide(w_output, note)
    output_full = in_order(w_output, output_far)
    ids_all = jnp.sum(
        notes[:, :adapters].astype(jnp.int32) * jnp.arange(adapters, dtype=jnp.int32), axis=1
    )
    routes_far = from_others(routes)
    maps = (a_gateup.swapaxes(2, 3), b_gateup, a_down.swapaxes(2, 3), b_down)
    calls = 2 if experts_dev % (4 * FLUSH) == 0 and groups == 2 else 1
    each = experts_dev // calls
    some = -(-each // 2)

    def fold(call, late, held, after):
        at = some if late else 0
        count = each - some if late else some
        return fold_adapters(
            adapter_ids, w_gateup, w_down, *maps, call * each + at, count, held, at, each, after
        )

    first_fold = fold(0, False, (), ())

    tokens_f = tokens.astype(F32)
    normed = rms_norm(tokens_f, attn_gain).astype(BF16)
    low_rank = product_back(normed, qkv_in).astype(BF16)
    own_columns = columns(normed, member * part, part)
    if groups == 2:
        keyvals = product(own_columns, w_keyval)
        for piece, start in keyval_far:
            keyvals = keyvals + product(columns(normed, start, piece.shape[0]), piece)
    else:
        keyvals = product(normed, keyval_full)
    keyvals = jnp.concatenate(
        [
            keyvals[:, :kv_width] + product(low_rank[:, RANK : 2 * RANK], keyval_out[0]),
            keyvals[:, kv_width:] + product(low_rank[:, 2 * RANK :], keyval_out[1]),
        ],
        axis=1,
    ).astype(BF16)
    folded = [fold(0, True, first_fold, (keyvals,))]
    keyvals_far = from_others(keyvals)
    upstream_far = from_others(delayed(cotangent, (keyvals_far,)))
    if groups == 2:
        query_rows = product(own_columns, w_query) + product(columns(normed, (1 - member) * part, part), query_far)
    else:
        query_rows = product(normed, query_full)
    query_rows = (query_rows + product(low_rank[:, :RANK], query_out)).astype(BF16)
    pad_whole = jnp.roll(pad_all, -first)
    listing, steps, own_bias, live = visits(parents[0], pad_whole[:count], pad_whole[count:], first)
    attended, logs = run_attention(listing, steps, query_rows, keyvals, keyvals_far, own_bias, live)
    out_rank = product_back(attended, output_in).astype(BF16)
    middle = tokens_f + product(attended, output_full) + product(out_rank, output_out)
    normed_ffn = rms_norm(middle, ffn_gain).astype(BF16)
    if calls == 2:
        folded.append(fold(1, True, fold(1, False, (), (normed_ffn,)), ()))
    router_rank = product_back(normed_ffn, router_in).astype(BF16)
    logits = product_back(normed_ffn, router_full) + product(router_rank, router_out)

    labels = jnp.arange(experts, dtype=jnp.int32)
    named = jnp.any(routes[:, :, None] == labels, axis=1)
    best = jnp.max(jnp.where(named, logits, -jnp.inf), axis=1, keepdims=True)
    powers = jnp.where(named, jnp.exp(jnp.where(named, logits, best) - best), 0.0)
    gates = powers / jnp.sum(powers, axis=1, keepdims=True)

    mine = member * experts_dev + jnp.arange(experts_dev, dtype=jnp.int32)
    routes_all = jnp.concatenate([routes, routes_far], axis=0).reshape(groups, count, TOPK)
    hits = jnp.any(routes_all[:, :, :, None] == mine, axis=2)
    before = (jnp.arange(count)[:, None] > jnp.arange(count)[None, :]).astype(BF16)
    ranks = jnp.einsum("ts,gse->get", before, hits.astype(BF16), preferred_element_type=F32)
    places = jnp.where(hits.transpose(0, 2, 1), ranks.astype(jnp.int32), -1).transpose(1, 0, 2)

    rows_far = from_others(normed_ffn)
    gates_t = gates.T
    if groups == 2:
        gates_near = lax.dynamic_slice_in_dim(gates_t, member * experts_dev, experts_dev, 0)
        gates_far = from_others(lax.dynamic_slice_in_dim(gates_t, (1 - member) * experts_dev, experts_dev, 0))
        gates_mine = jnp.stack([gates_near, gates_far], axis=1)
    else:
        gates_mine = lax.all_gather(gates_t, "grp", axis=0)
        gates_mine = lax.dynamic_slice_in_dim(gates_mine, member * experts_dev, experts_dev, 1)
        gates_mine = jnp.roll(gates_mine, -member, axis=0).transpose(1, 0, 2)
    sums = ()
    gate_terms = []
    spread = []
    for n in range(calls):
        *sums, terms, grads = run_experts(
            adapter_ids,
            normed_ffn,
            rows_far,
            cotangent,
            upstream_far,
            places,
            gates_mine,
            *folded[n],
            *maps,
            tuple(sums),
            cap,
            n * each,
            each,
        )
        gate_terms.append(terms)
        if n:
            sums[3], swapped = lax.optimization_barrier((sums[3], swapped))
            spread.append(lax.all_gather(totals(ids_all, swapped, adapters), "rep", axis=0))
        swapped = lax.all_to_all(
            grads.reshape(reps, -1, UNIT), "rep", split_axis=0, concat_axis=0, tiled=True
        )
    result_near, result_far, d_near, d_far = sums
    part_gates = jnp.concatenate(gate_terms, axis=0)
    if groups == 2:
        d_gates = in_order(part_gates[:, 0], from_others(part_gates[:, 1]))
    else:
        d_gates = jnp.roll(part_gates, member, axis=1)
        d_gates = lax.all_to_all(d_gates, "grp", split_axis=1, concat_axis=0, tiled=True)
    d_gates = d_gates.reshape(experts, count).T
    d_sum = to_owners(d_near, d_far)
    upstream = cotangent.astype(F32)
    d_logits = (gates * (d_gates - jnp.sum(gates * d_gates, axis=1, keepdims=True))).astype(BF16)

    d_router_rank = product_back(d_logits, router_out).astype(BF16)
    d_normed_ffn = d_sum + product(d_logits, router_full) + product(d_router_rank, router_in)
    grad_router_out = product_outer(router_rank, d_logits)
    grad_router_in = product_outer(d_router_rank, normed_ffn)
    d_middle = upstream + rms_back(middle, ffn_gain, d_normed_ffn)
    d_attn = d_middle.astype(BF16)
    d_out_rank = product_back(d_attn, output_out).astype(BF16)
    attended_gradient = (product_back(d_attn, output_full) + product(d_out_rank, output_in)).astype(BF16)
    grad_output_out = product_outer(out_rank, d_attn)
    grad_output_in = product_outer(d_out_rank, attended)
    parts = []
    pairs = KEY_VALUE_HEADS // 4
    for n in range(2):
        d_q, *d_kv = run_attention_back(
            listing,
            steps,
            query_rows,
            keyvals,
            keyvals_far,
            own_bias,
            live,
            attended,
            attended_gradient,
            logs,
            n * pairs,
            pairs,
        )
        d_kv = to_owners(jnp.concatenate(d_kv[:2], axis=1), jnp.concatenate(d_kv[2:], axis=1)).astype(BF16)
        parts.append((d_q, d_kv[:, : kv_width // 2], d_kv[:, kv_width // 2 :]))
    mixture = owners_terms(result_near, delayed(result_far, (parts[1][1],)))
    d_queries, d_keys, d_values = [jnp.concatenate(pair, axis=1) for pair in zip(*parts)]
    d_keyvals = jnp.concatenate([d_keys, d_values], axis=1)
    d_rank_qkv = jnp.concatenate(
        [
            product_back(d_queries, query_out),
            product_back(d_keys, keyval_out[0]),
            product_back(d_values, keyval_out[1]),
        ],
        axis=-1,
    ).astype(BF16)
    d_normed = (
        product_back(d_queries, query_full)
        + product_back(d_keyvals, keyval_full)
        + product(d_rank_qkv, qkv_in)
    )
    grad_input = (d_middle + rms_back(tokens_f, attn_gain, d_normed)).astype(BF16)
    grad_qkv_in = product_outer(d_rank_qkv, normed)
    grad_query_out = product_outer(low_rank[:, :RANK], d_queries)
    grad_keyval_out = jnp.stack(
        [
            product_outer(low_rank[:, RANK : 2 * RANK], d_keys),
            product_outer(low_rank[:, 2 * RANK :], d_values),
        ],
        axis=0,
    )

    last = totals(ids_all, swapped, adapters, after=(parts[0][0],))
    spread.append(lax.all_gather(last, "rep", axis=0))
    expert_grads = ()
    for n in range(calls):
        expert_grads = unpack_grads(spread[n], experts_dev, n * each, tuple(expert_grads), width)
    grad_a_gateup, grad_b_gateup, grad_a_down, grad_b_down = expert_grads

    tall = jnp.concatenate(
        [grad_qkv_in, grad_query_out, grad_output_in, grad_output_out, grad_router_in], axis=0
    ).astype(BF16)
    high = tall.shape[0]
    tall = tall.reshape(high, groups, part).swapaxes(0, 1)
    wide = [
        grad_keyval_out[0].reshape(RANK, groups, kv_part),
        grad_keyval_out[1].reshape(RANK, groups, kv_part),
        grad_router_out.reshape(RANK, groups, experts_dev),
        jnp.zeros((RANK, groups, part - 2 * kv_part - experts_dev), F32),
    ]
    wide = jnp.concatenate(wide, axis=2).astype(BF16).swapaxes(0, 1)
    dense = jnp.concatenate([tall, wide], axis=1).reshape(groups, reps, -1, part).swapaxes(0, 1)
    dense = dense.reshape(reps * groups, -1, part)
    result = add_up(middle, *mixture, after=(dense,))
    dense = lax.all_to_all(dense, ("rep", "grp"), split_axis=0, concat_axis=0, tiled=True)
    owner_hot = (jnp.arange(adapters, dtype=jnp.int32)[:, None] == jnp.repeat(ids_all, groups)[None, :])
    dense = jnp.sum(jnp.where(owner_hot[:, :, None, None], dense.astype(F32)[None], 0.0), axis=1).astype(BF16)
    dense = jnp.broadcast_to(dense[None], (reps,) + dense.shape)
    dense = lax.all_to_all(dense, "rep", split_axis=0, concat_axis=0, tiled=True).swapaxes(0, 1).reshape(adapters, -1, part).astype(F32)
    wide = dense[:, high:]
    owned = [
        dense[:, : 3 * RANK],
        dense[:, 3 * RANK : 4 * RANK],
        jnp.stack([wide[:, :, :kv_part], wide[:, :, kv_part : 2 * kv_part]], axis=1),
        dense[:, 4 * RANK : 5 * RANK],
        dense[:, 5 * RANK : 6 * RANK],
        dense[:, 6 * RANK : 7 * RANK],
        wide[:, :, 2 * kv_part : 2 * kv_part + experts_dev],
    ]
    return (
        result,
        grad_input,
        owned[0].swapaxes(1, 2),
        owned[1],
        owned[2],
        owned[3].swapaxes(1, 2),
        owned[4],
        owned[5].swapaxes(1, 2),
        owned[6],
        grad_a_gateup.swapaxes(2, 3),
        grad_b_gateup,
        grad_a_down.swapaxes(2, 3),
        grad_b_down,
    )


def solution(mesh):
    in_specs = (
        P(("rep", "grp"), None),
        P(("rep", "grp"), None),
        P(("rep", "grp"), None),
        P(("rep", "grp")),
        P("rep", None),
        P("rep"),
        P("grp", None),
        P("grp", None),
        P("grp", None),
        P("grp", None),
        P("grp"),
        P("grp"),
        P("grp", None, None),
        P("grp", None, None),
        P(None, "grp", None),
        P(None, None, "grp"),
        P(None, None, None, "grp"),
        P(None, "grp", None),
        P(None, None, "grp"),
        P(None, "grp", None),
        P(None, None, "grp"),
        P(None, "grp", None, None),
        P(None, "grp", None, None, None),
        P(None, "grp", None, None),
        P(None, "grp", None, None),
    )
    out_specs = (
        P(("rep", "grp"), None),
        P(("rep", "grp"), None),
        P(None, "grp", None),
        P(None, None, "grp"),
        P(None, None, None, "grp"),
        P(None, "grp", None),
        P(None, None, "grp"),
        P(None, "grp", None),
        P(None, None, "grp"),
        P(None, "grp", None, None),
        P(None, "grp", None, None, None),
        P(None, "grp", None, None),
        P(None, "grp", None, None),
    )
    return jax.shard_map(local, mesh=mesh, in_specs=in_specs, out_specs=out_specs, check_vma=False)
```
